32 devices in a mesh: batch: 8 (over z, x), blk: 4 (over y, core).
Axes of the slice: x: 2, y: 2, z: 4, core: 2. Of those that a mesh axis runs over, the one named last changes fastest.
Arguments:
- tokens: bfloat16 [8, 1024, 512], P('batch', 'blk'), may hold values from -6 to 6
- memory: bfloat16 [8, 1024, 512], P('batch', 'blk'), may hold values from -6 to 6
- lengths: int32 [8], P('batch'), may hold values from 769 to 1024, as said below
- targets: int32 [8, 1024], P('batch'), may hold values from 0 to 31999
- expert_ids: int32 [2, 8, 1024, 1], P(None, 'batch', 'blk'), may hold values from 0 to 3; in each aligned block of 256 rows (0 to 255, 256 to 511, ..., all dimensions but the last counted through in order) at most 96 rows name the same one
- gain_self: float32 [512], replicated, may hold values from 0.5 to 1.5
- gain_cross: float32 [512], replicated, may hold values from 0.5 to 1.5
- gain_ffn: float32 [512], replicated, may hold values from 0.5 to 1.5
- gain_out: float32 [512], replicated, may hold values from 0.5 to 1.5
- wq: bfloat16 [512, 512], replicated, may hold values from -0.25 to 0.25
- wk: bfloat16 [512, 512], replicated, may hold values from -0.25 to 0.25
- wv: bfloat16 [512, 512], replicated, may hold values from -0.25 to 0.25
- wo: bfloat16 [512, 512], replicated, may hold values from -0.75 to 0.75
- cq: bfloat16 [512, 512], replicated, may hold values from -0.25 to 0.25
- ck: bfloat16 [512, 512], replicated, may hold values from -0.25 to 0.25
- cv: bfloat16 [512, 512], replicated, may hold values from -0.25 to 0.25
- co: bfloat16 [512, 512], replicated, may hold values from -0.75 to 0.75
- w_in: bfloat16 [4, 512, 2048], P('blk'), may hold values from -0.25 to 0.25
- w_out: bfloat16 [4, 2048, 512], P('blk'), may hold values from -0.125 to 0.125
- embed: bfloat16 [32000, 512], P('blk'), may hold values from -0.5 to 0.5
Outputs:
- token_loss: float32 [8, 1024], P('batch', 'blk')
- grad_tokens: float32 [8, 1024, 512], P('batch', 'blk')
- grad_memory: float32 [8, 1024, 512], P('batch', 'blk')
- grad_gain_self: float32 [512], replicated
- grad_gain_cross: float32 [512], replicated
- grad_gain_ffn: float32 [512], replicated
- grad_gain_out: float32 [512], replicated
- grad_wq: float32 [512, 512], P('batch', 'blk')
- grad_wk: float32 [512, 512], P('batch', 'blk')
- grad_wv: float32 [512, 512], P('batch', 'blk')
- grad_wo: float32 [512, 512], P('batch', 'blk')
- grad_cq: float32 [512, 512], P('batch', 'blk')
- grad_ck: float32 [512, 512], P('batch', 'blk')
- grad_cv: float32 [512, 512], P('batch', 'blk')
- grad_co: float32 [512, 512], P('batch', 'blk')
- grad_w_in: float32 [4, 512, 2048], P('blk', 'batch')
- grad_w_out: float32 [4, 2048, 512], P('blk', 'batch')
- grad_embed: float32 [32000, 512], P('blk', 'batch')
The draws below stay inside these ranges and needn't reach their ends.
Inputs may be any that keep to these rules, and one draw needn't show every extreme that they name: `lengths`: every sequence has live positions on the last device of its group (769 or more); some sequence is full. `expert_ids`: among the 256 tokens of one device in one pass, at most 96 name the same expert.
All inputs are finite; a program needn't handle non-finite values.
Results may differ from the reference program's by a relative error of at most 0.019.
Values may be sent and summed in bfloat16 or wider, within the bound.
No kernel may reach another device: no remote copies, remote signals or barrier semaphores. Data moves between devices by JAX's collectives and lax.ppermute only.
A program may use at most 384 MiB of HBM per device.

```python
import math
import jax
import jax.numpy as jnp
import numpy as np
from jax import lax

D = 512
HEADS = 8
HD = 64
FF = 2048
VOCAB = 32000
TOK_DEV = 256
EXPERTS = 4
SEQ = 1024
MEM = 1024
NSEQ = 8
CAP = 96


def draw_lengths(key, part):
    key_one, key_two = jax.random.split(key)
    drawn = jax.random.randint(key_one, (NSEQ,), SEQ - TOK_DEV + 1, SEQ + 1)
    pick_full = jax.random.randint(key_two, (), 0, NSEQ)
    return jnp.where(jnp.arange(NSEQ) == pick_full, SEQ, drawn).astype(jnp.int32)


def set_ends(values, own_key, low, top_value):
    extent = values.shape
    place = [jax.random.randint(jax.random.fold_in(own_key, axis), (), 0, extent[axis]) for axis in range(len(extent))]
    values = values.at[tuple(place)].set(low)
    longest = extent.index(max(extent))
    place[longest] = (place[longest] + 1) % extent[longest]
    return values.at[tuple(place)].set(top_value)


def shard_levels(own_key, extent, shards, least, high):
    def one(axis_at, parts):
        draws = jax.random.uniform(jax.random.fold_in(jax.random.fold_in(own_key, 6), axis_at), (parts,), jnp.float32, least / len(shards), high / len(shards))
        return jnp.repeat(jnp.exp(draws), extent[axis_at] // parts).reshape((-1,) + (1,) * (len(extent) - axis_at - 1))

    level = one(*shards[0])
    for cut in shards[1:]:
        level = level * one(*cut)
    return level


def rank_bounds(amount, lean):
    weights = [(1 << 20) // math.isqrt(standing ** lean) + 1 for standing in range(1, amount + 1)]
    deviation = 1 + sum(weights) // (1 << 30)
    return np.cumsum(np.array([max(1, weight // deviation) for weight in weights]))


def ranked(rng, shape, count, skew):
    table = rank_bounds(count, skew)
    pick = jax.random.randint(jax.random.fold_in(rng, 1), shape, 0, int(table[count - 1]))
    rank = jnp.searchsorted(jnp.asarray(table, jnp.int32), pick, side="right")
    return jax.random.permutation(jax.random.fold_in(rng, 2), count)[rank].astype(jnp.int32)


def routed_block(key, own, number, rows, number_of, top, reach, slope):
    order = jax.random.permutation(key, number_of)
    packed, common = load_shares(number_of, rows * top, reach, slope, True), load_shares(number_of, rows * top, reach, slope, False)
    places = jnp.arange(number_of)

    def named(sizes, offset_by):
        used = int((sizes > 0).sum())
        fixed = max(1, used // 4)
        moved = fixed + (places - fixed + offset_by * (used - fixed)) % max(1, number_of - fixed)
        return jnp.zeros((number_of,), jnp.int32).at[order[jnp.where(places < fixed, places, moved)]].set(jnp.asarray(sizes, jnp.int32))

    sizes = jnp.where(number % 4 == 0, named(packed, number // 4), named(common, number - number // 4 - 1))
    mixed = jax.random.permutation(jax.random.fold_in(own, 3), number_of)
    giver, taker = mixed[0:number_of // 2 * 2:2], mixed[1:number_of // 2 * 2:2]
    slack = jnp.minimum(sizes[giver] - 1, reach - sizes[taker]) // 2
    slack = jnp.where((giver == order[0]) | (taker == order[0]) | (sizes[taker] == 0), 0, jnp.maximum(slack, 0))
    moved = jax.random.randint(jax.random.fold_in(own, 4), (number_of // 2,), 0, 1 << 20) % (slack + 1)
    sizes = sizes.at[giver].add(-moved).at[taker].add(moved)
    members = jnp.searchsorted(jnp.cumsum(sizes), jnp.arange(rows * top), side="right").astype(jnp.int32)
    table = members.reshape(top, rows).T
    table = table[jax.random.permutation(jax.random.fold_in(own, 1), rows)]
    offset_by = jax.random.randint(jax.random.fold_in(own, 2), (rows, 1), 0, top)
    return jnp.take_along_axis(table, (jnp.arange(top)[None, :] + offset_by) % top, axis=1)


def load_shares(number_of, total, reach, slope, full):
    portions = [(1 << 20) // math.isqrt(grade ** slope) + 1 for grade in range(1, number_of + 1)]
    largest = reach if full else min(reach, max(-(-total // number_of), total * portions[0] // sum(portions)))
    least = 1 if total - largest >= number_of - 1 else 0
    counts, rest = [largest] + [least] * (number_of - 1), total - largest - least * (number_of - 1)
    while rest > 0:
        movable = [i for i in range(1, number_of) if counts[i] < largest] or [i for i in range(1, number_of) if counts[i] < reach]
        pool, left = sum([portions[i] for i in movable]), rest
        for i in movable:
            more = min(reach - counts[i], max(1, left * portions[i] // pool), rest)
            counts[i] = counts[i] + more
            rest = rest - more
    return np.array(counts)


def scatter_about(key, extent, deviation, bound, shards=(), kind=jnp.bfloat16):
    loudness = shard_levels(key, extent, shards, -0.22, 0.18) if shards else 1.0
    values = jax.random.normal(key, extent, jnp.float32) * deviation * loudness
    return jnp.minimum(jnp.maximum(values, -bound), bound).astype(kind)


def setup_inputs(seed: int = 0) -> dict:
    arg_keys = jax.random.split(jax.random.key(seed), 21)
    tokens = scatter_about(arg_keys[0], (NSEQ, SEQ, D), 1.0, 6.0, ((0, 8), (1, 4)))
    memory = scatter_about(arg_keys[1], (NSEQ, MEM, D), 1.0, 6.0, ((0, 8), (1, 4)))
    lengths = draw_lengths(jax.random.fold_in(arg_keys[20], 71), 0)
    targets = set_ends(ranked(arg_keys[3], (NSEQ, SEQ), VOCAB, 2), jax.random.fold_in(arg_keys[3], 3), 0, VOCAB - 1).astype(jnp.int32)
    expert_ids_keys = jax.random.split(jax.random.fold_in(arg_keys[4], 1), 2 * NSEQ * SEQ // TOK_DEV)
    expert_ids_turns = jax.random.permutation(jax.random.fold_in(arg_keys[4], 3), 2 * NSEQ * SEQ // TOK_DEV)
    expert_ids = jax.vmap(lambda own, number: routed_block(jax.random.fold_in(arg_keys[4], 2), own, number, TOK_DEV, EXPERTS, 1, CAP, 1))(expert_ids_keys, expert_ids_turns).reshape((2, NSEQ, SEQ, 1))
    gain_self = jnp.clip(1.0 + 0.1 * jax.random.normal(arg_keys[5], (D,), jnp.float32), 0.5, 1.5)
    gain_cross = jnp.clip(1.0 + 0.1 * jax.random.normal(arg_keys[6], (D,), jnp.float32), 0.5, 1.5)
    gain_ffn = jnp.clip(1.0 + 0.1 * jax.random.normal(arg_keys[7], (D,), jnp.float32), 0.5, 1.5)
    gain_out = jnp.clip(1.0 + 0.1 * jax.random.normal(arg_keys[8], (D,), jnp.float32), 0.5, 1.5)
    wq = scatter_about(arg_keys[9], (D, D), D ** -0.5, 0.25)
    wk = scatter_about(arg_keys[10], (D, D), D ** -0.5, 0.25)
    wv = scatter_about(arg_keys[11], (D, D), D ** -0.5, 0.25)
    wo = scatter_about(arg_keys[12], (D, D), HD ** -0.5, 0.75)
    cq = scatter_about(arg_keys[13], (D, D), D ** -0.5, 0.25)
    ck = scatter_about(arg_keys[14], (D, D), D ** -0.5, 0.25)
    cv = scatter_about(arg_keys[15], (D, D), D ** -0.5, 0.25)
    co = scatter_about(arg_keys[16], (D, D), HD ** -0.5, 0.75)
    w_in = scatter_about(arg_keys[17], (EXPERTS, D, FF), D ** -0.5, 0.25, ((0, 4),))
    w_out = scatter_about(arg_keys[18], (EXPERTS, FF, D), FF ** -0.5, 0.125, ((0, 4),))
    embed = scatter_about(arg_keys[19], (VOCAB, D), (D // 4) ** -0.5, 0.5, ((0, 4),))
    return dict(tokens=tokens, memory=memory, lengths=lengths, targets=targets, expert_ids=expert_ids, gain_self=gain_self, gain_cross=gain_cross, gain_ffn=gain_ffn, gain_out=gain_out, wq=wq, wk=wk, wv=wv, wo=wo, cq=cq, ck=ck, cv=cv, co=co, w_in=w_in, w_out=w_out, embed=embed)


EPS_NORM = 1e-05
SMOOTH = 0.1
HIGH = lax.Precision.HIGHEST

@jax.custom_vjp
def low(v):
    return lax.optimization_barrier(v.astype(jnp.bfloat16)).astype(jnp.float32)

@jax.custom_vjp
def low_back(v):
    return v

def low_keep(v):
    return (low(v), None)

def low_pass(kept, grad):
    return (grad,)

def back_keep(v):
    return (v, None)

def back_low(kept, grad):
    return (low(grad),)
low.defvjp(low_keep, low_pass)
low_back.defvjp(back_keep, back_low)

def layer_norm(values, gain):
    center = values - lax.optimization_barrier(jnp.mean(values, axis=-1, keepdims=True))
    spread = lax.optimization_barrier(jnp.mean(center * center, axis=-1, keepdims=True))
    return center * lax.rsqrt(spread + EPS_NORM) * gain

def matmul(left, right):
    return jnp.dot(left, right, precision=HIGH)

def attention(queries, keys, values, causal):
    total_rows = queries.shape[0]
    block = min(512, total_rows)
    head_keys = keys.reshape(keys.shape[0], HEADS, HD)
    head_values = values.reshape(values.shape[0], HEADS, HD)
    key_pos = jnp.arange(keys.shape[0]).astype(jnp.int32)

    def one_block(start):
        query_block = lax.dynamic_slice_in_dim(queries, start, block, 0).reshape(block, HEADS, HD)
        scores = jnp.einsum('qhd,khd->hqk', query_block, head_keys, precision=HIGH) * HD ** (-0.5)
        scores = low_back(scores)
        if causal:
            query_pos = start + jnp.arange(block).astype(jnp.int32)
            scores = jnp.where(key_pos[None, None, :] <= query_pos[None, :, None], scores, -1e+30)
        row_max = lax.optimization_barrier(jnp.max(scores, axis=-1, keepdims=True))
        weights = jnp.exp(scores - row_max)
        probs = low(weights / lax.optimization_barrier(jnp.sum(weights, axis=-1, keepdims=True)))
        output = jnp.einsum('hqk,khd->qhd', probs, head_values, precision=HIGH)
        return output.reshape(block, HEADS * HD)
    starts = (jnp.arange(total_rows // block) * block).astype(jnp.int32)
    return lax.map(jax.checkpoint(one_block), starts).reshape(total_rows, HEADS * HD)

def expert_pass(normed, picks, w_in, w_out):
    count = normed.shape[0]
    blocks = count // TOK_DEV
    flat = picks.reshape(count).astype(jnp.int32)
    onehot = (flat[:, None] == jnp.arange(EXPERTS).astype(jnp.int32)[None, :]).astype(jnp.int32)
    onehot = onehot.reshape(blocks, TOK_DEV, EXPERTS)
    before = jnp.cumsum(onehot, axis=1) - onehot
    slot = lax.optimization_barrier(jnp.sum(onehot * before, axis=-1)).reshape(count)
    block_of = (jnp.arange(count) // TOK_DEV).astype(jnp.int32)
    position = ((flat * blocks + block_of) * CAP + slot).astype(jnp.int32)
    buffer = jnp.zeros((EXPERTS * blocks * CAP, normed.shape[1]), jnp.float32).at[position].set(normed)
    buffer = buffer.reshape(EXPERTS, blocks * CAP, normed.shape[1])
    up_values = low_back(jnp.einsum('erd,edf->erf', buffer, w_in, precision=HIGH))
    activity = low(jax.nn.gelu(up_values))
    result = low(jnp.einsum('erf,efd->erd', activity, w_out, precision=HIGH))
    return low_back(result.reshape(-1, normed.shape[1])[position])

def loss_rows(z_pair, labels, live, embed):
    logit_pair = low_back(jnp.einsum('prd,vd->prv', z_pair, embed, precision=HIGH))
    row_max = lax.optimization_barrier(jnp.max(logit_pair, axis=-1, keepdims=True))
    log_total = row_max + jnp.log(lax.optimization_barrier(jnp.sum(jnp.exp(logit_pair - row_max), axis=-1, keepdims=True)))
    probs = jnp.exp(logit_pair - log_total)
    index = jnp.broadcast_to(labels[None, :, None], (2, labels.shape[0], 1))
    picked = jnp.take_along_axis(logit_pair, index, axis=2)[..., 0]
    cross = log_total[..., 0] - (1.0 - SMOOTH) * picked - SMOOTH * lax.optimization_barrier(jnp.mean(logit_pair, axis=-1))
    symmetric = lax.optimization_barrier(jnp.sum((probs[0] - probs[1]) * (logit_pair[0] - logit_pair[1]), axis=-1))
    return live * (cross[0] + cross[1] + symmetric)

def forward(tokens, memory, gain_self, gain_cross, gain_ffn, gain_out, wq, wk, wv, wo, cq, ck, cv, co, w_in, w_out, embed, lengths, targets, expert_ids):

    def sequence(operands):
        seq_states, seq_memory = operands
        h_one = low(layer_norm(seq_states, gain_self))
        queries = low_back(low(matmul(h_one, wq)))
        keys = low(matmul(h_one, wk))
        values = low(matmul(h_one, wv))
        attn_out = low_back(low(attention(queries, keys, values, True)))
        middle = seq_states + low_back(matmul(attn_out, wo))
        h_two = low(layer_norm(middle, gain_cross))
        cross_q = low_back(low(matmul(h_two, cq)))
        mem_keys = low(matmul(seq_memory, ck))
        mem_values = low(matmul(seq_memory, cv))
        cross_out = low_back(low(attention(cross_q, mem_keys, mem_values, False)))
        return middle + low_back(matmul(cross_out, co))
    after_cross = lax.map(sequence, (tokens, memory)).reshape(NSEQ * SEQ, D)
    h_three = low(layer_norm(after_cross, gain_ffn))
    expert_out = jnp.stack([expert_pass(h_three, expert_ids[0], w_in, w_out), expert_pass(h_three, expert_ids[1], w_in, w_out)])
    outputs = after_cross[None] + expert_out
    z_pair = low(layer_norm(outputs, gain_out))
    count = NSEQ * SEQ
    block = min(512, count)
    steps_count = count // block
    live = (jnp.arange(SEQ).astype(jnp.int32)[None, :] < lengths[:, None]).astype(jnp.float32).reshape(steps_count, block)
    labels = targets.reshape(steps_count, block)
    z_blocks = z_pair.reshape(2, steps_count, block, D).transpose(1, 0, 2, 3)

    def one_block(operands):
        return loss_rows(operands[0], operands[1], operands[2], embed)
    losses = lax.map(jax.checkpoint(one_block), (z_blocks, labels, live))
    return losses.reshape(NSEQ, SEQ)

def reference(tokens, memory, lengths, targets, expert_ids, gain_self, gain_cross, gain_ffn, gain_out, wq, wk, wv, wo, cq, ck, cv, co, w_in, w_out, embed):
    floats = (tokens, memory, gain_self, gain_cross, gain_ffn, gain_out, wq, wk, wv, wo, cq, ck, cv, co, w_in, w_out, embed)
    floats = tuple((item.astype(jnp.float32) for item in floats))

    def objective(*operands):
        return forward(*operands, lengths, targets, expert_ids)
    losses, pullback = jax.vjp(objective, *floats)
    grads = pullback(jnp.ones_like(losses))
    return (losses, grads[0], grads[1], grads[2], grads[3], grads[4], grads[5], grads[6], grads[7], grads[8], grads[9], grads[10], grads[11], grads[12], grads[13], grads[14], grads[15], grads[16])
```

```python
import functools

import jax
import jax.numpy as jnp
from jax import lax
from jax.experimental import pallas as pl
from jax.experimental.pallas import tpu as pltpu
from jax.sharding import PartitionSpec as P

HEADS = 8
HD = 64


EPS_NORM = 1e-05
SMOOTH = 0.1
LOG2E = 1.4426950408889634
NN = (((1,), (0,)), ((), ()))
NT = (((1,), (1,)), ((), ()))


def dot(left, right, dims):
    return lax.dot_general(left, right, dims, preferred_element_type=jnp.float32)


def swap(value, axis, mask):
    size = lax.axis_size(axis)
    return lax.ppermute(value, axis, [(i, i ^ mask) for i in range(size)])


def gather_blocks(own, axis):
    size = lax.axis_size(axis)
    blocks = {0: own}
    bit = 2
    while bit < size:
        for k in range(0, bit, 2):
            blocks[bit | k] = swap(blocks[k], axis, bit)
        bit *= 2
    for k in range(0, size, 2):
        blocks[k | 1] = swap(blocks[k], axis, 1)
    return [blocks[j] for j in range(size)]


def scatter_blocks(parts, axis):
    parts = list(parts)
    size = len(parts)
    bit = 1
    while bit < size:
        odd = [j for j in range(0, size, bit) if j & bit]
        even = [j ^ bit for j in odd]
        moved = swap(jnp.stack([parts[j] for j in odd]), axis, bit)
        for k, j in enumerate(even):
            parts[j] = add_low(parts[j], moved[k])
        bit *= 2
    return parts[0]


def add_low(left, right):
    return (left.astype(jnp.float32) + right.astype(jnp.float32)).astype(left.dtype)


def ring_order(size):
    return list(range(0, 1)) + list(range(1, size, 2)) + list(range(size - 2, 0, -2))


def relative_index(axis):
    size = lax.axis_size(axis)
    high = size // 2
    order = jnp.asarray(ring_order(high), jnp.int32)
    place = [ring_order(high).index(i) for i in range(high)]
    me = lax.axis_index(axis)
    mine = jnp.asarray(place, jnp.int32)[me // 2]
    steps = jnp.mod(mine - 1 - jnp.arange(high, dtype=jnp.int32), high)
    lows = me % 2
    return jnp.stack([order[steps] * 2 + (lows ^ low) for low in range(2)]).reshape(size)


def ring_scatter(parts, axis, pair_first):
    high = parts.shape[1]
    order = ring_order(high)
    links = [
        (order[k] * 2 + low, order[(k + 1) % high] * 2 + low) for k in range(high) for low in range(2)
    ]

    def ring(value):
        total = value[0]
        for step in range(high - 1):
            total = add_low(lax.ppermute(total, axis, links), value[step + 1])
        return total

    if pair_first:
        return ring(add_low(parts[0], swap(parts[1], axis, 1)))
    total = ring(parts.transpose((1, 0) + tuple(range(2, parts.ndim))))
    return add_low(total[0], swap(total[1], axis, 1))


def pick_parts(value, index):
    count = value.shape[0]
    parts = [lax.dynamic_index_in_dim(value, index[k], 0, keepdims=False) for k in range(count)]
    return jnp.stack(parts).reshape((2, count // 2) + value.shape[1:])


def stats_kernel(cols, steps, embed_ref, z_ref, out_ref, max_ref, sum_ref, mix_ref):
    step = pl.program_id(0)
    half = z_ref.shape[0] // 2

    @pl.when(step == 0)
    def _():
        max_ref[...] = jnp.full_like(max_ref, -jnp.inf)
        sum_ref[...] = jnp.zeros_like(sum_ref)
        mix_ref[...] = jnp.zeros_like(mix_ref)

    embed = embed_ref[...]
    for col in range(half // cols):
        places = [slice(p * half + col * cols, p * half + (col + 1) * cols) for p in range(2)]
        logits = [dot(embed, z_ref[place, :], NT).reshape(-1, 8, cols) for place in places]
        apart = logits[0] - logits[1]
        for place, logit in zip(places, logits):
            old = max_ref[:, place]
            new = jnp.maximum(old, jnp.max(logit, axis=0))
            max_ref[:, place] = new
            scale = jnp.exp2((old - new) * LOG2E)
            weights = jnp.exp2((logit - new[None]) * LOG2E)
            sum_ref[:, place] = sum_ref[:, place] * scale + jnp.sum(weights, axis=0)
            mix_ref[:, place] = mix_ref[:, place] * scale + jnp.sum(weights * apart, axis=0)

    @pl.when(step == steps - 1)
    def _():
        top = jnp.max(max_ref[...], axis=0, keepdims=True)
        scale = jnp.exp2((max_ref[...] - top) * LOG2E)
        out_ref[0:1, :] = top
        out_ref[1:2, :] = jnp.sum(sum_ref[...] * scale, axis=0, keepdims=True)
        out_ref[2:3, :] = jnp.sum(mix_ref[...] * scale, axis=0, keepdims=True)


def row_tile(rows, limit):
    return max(size for size in range(16, limit + 1, 16) if rows % size == 0)


def vocab_stats(embed, z_rows):
    vocab, width = embed.shape
    rows = z_rows.shape[0]
    tile = row_tile(vocab, 800)
    cols = min(256, rows // 2)
    steps = vocab // tile
    return pl.pallas_call(
        functools.partial(stats_kernel, cols, steps),
        grid=(steps,),
        in_specs=[
            pl.BlockSpec((tile, width), lambda i: (i, 0)),
            pl.BlockSpec((rows, width), lambda i: (0, 0)),
        ],
        out_specs=pl.BlockSpec((3, rows), lambda i: (0, 0)),
        out_shape=jax.ShapeDtypeStruct((3, rows), jnp.float32),
        scratch_shapes=[pltpu.VMEM((8, rows), jnp.float32)] * 3,
        compiler_params=pltpu.CompilerParams(vmem_limit_bytes=48 << 20),
        cost_estimate=pl.CostEstimate(
            flops=2 * vocab * rows * width,
            bytes_accessed=2 * (vocab + rows) * width,
            transcendentals=vocab * rows,
        ),
    )(embed, z_rows)


def loss_back_kernel(cols, steps, has_total, has_carry, last, *refs):
    base_ref, embed_ref, embed_t_ref, z_ref, z_t_ref, row_ref, label_ref = refs[:7]
    refs = list(refs[7:])
    total_ref = refs.pop(0) if has_total else None
    carry_ref = refs.pop(0) if has_carry else None
    grad_embed_ref, grad_z_ref, loss_ref, grad_ref, sum_ref = refs
    step = pl.program_id(0)
    half = z_ref.shape[0] // 2
    tile = embed_ref.shape[0]

    @pl.when(step == 0)
    def _():
        sum_ref[...] = carry_ref[...] if has_carry else jnp.zeros_like(sum_ref)
        loss_ref[...] = jnp.zeros_like(loss_ref)

    embed = embed_ref[...]
    ids = lax.broadcasted_iota(jnp.int32, (tile // 8, 8, cols), 0) * 8
    ids = ids + lax.broadcasted_iota(jnp.int32, (tile // 8, 8, cols), 1)
    base = base_ref[0] + step * tile
    for col in range(half // cols):
        one = slice(col * cols, (col + 1) * cols)
        two = slice(half + col * cols, half + (col + 1) * cols)
        logit_one = dot(embed, z_ref[one, :], NT).reshape(-1, 8, cols)
        logit_two = dot(embed, z_ref[two, :], NT).reshape(-1, 8, cols)
        row = [row_ref[k : k + 1, one].reshape(1, 1, cols) for k in range(6)]
        prob_one = jnp.exp2(logit_one * LOG2E - row[0])
        prob_two = jnp.exp2(logit_two * LOG2E - row[1])
        apart = logit_one - logit_two
        hits = ids == (label_ref[0:1, one] - base).reshape(1, 1, cols)
        smooth = jnp.where(hits, row[4], row[5])
        grad_one = prob_one * (apart + row[2]) - (prob_two + smooth)
        grad_two = prob_two * (row[3] - apart) - (prob_one + smooth)
        loss_ref[:, one] += jnp.sum(smooth * (logit_one + logit_two), axis=0)
        grad_ref[:, one] = grad_one.reshape(tile, cols).astype(jnp.bfloat16)
        grad_ref[:, two] = grad_two.reshape(tile, cols).astype(jnp.bfloat16)
    grads = grad_ref[...]
    grad_embed = dot(z_t_ref[...], grads, NT)
    if has_total:
        grad_embed = grad_embed + total_ref[...]
    grad_embed_ref[...] = grad_embed.astype(grad_embed_ref.dtype)
    sum_ref[...] += dot(embed_t_ref[...], grads, NN)

    @pl.when(step == steps - 1)
    def _():
        if last:
            grad_z_ref[...] = sum_ref[...].T.astype(grad_z_ref.dtype)
        else:
            grad_z_ref[...] = sum_ref[...]


def loss_back(base, embed, embed_t, z_rows, z_t, row_values, labels, span, total, carry, last):
    width = embed.shape[1]
    rows = z_rows.shape[0]
    tile = TILE
    low, high = span
    steps, first = (high - low) // tile, low // tile
    cols = min(256, rows // 2)
    operands = [base + low, embed, embed_t, z_rows, z_t, row_values, labels]
    whole = lambda i: (0, 0)
    specs = [
        pl.BlockSpec(memory_space=pltpu.SMEM),
        pl.BlockSpec((tile, width), lambda i: (i + first, 0)),
        pl.BlockSpec((width, tile), lambda i: (0, i + first)),
        pl.BlockSpec((rows, width), whole),
        pl.BlockSpec((width, rows), whole),
        pl.BlockSpec((6, rows // 2), whole),
        pl.BlockSpec((1, rows // 2), whole),
    ]
    if total is not None:
        operands.append(total)
        specs.append(pl.BlockSpec((width, tile), lambda i: (0, i + first)))
    if carry is not None:
        operands.append(carry)
        specs.append(pl.BlockSpec((width, rows), whole))
    emit = jnp.bfloat16 if last is not None else jnp.float32
    grad_z = (
        jax.ShapeDtypeStruct((rows, width), jnp.bfloat16)
        if last is not False
        else jax.ShapeDtypeStruct((width, rows), jnp.float32)
    )
    return pl.pallas_call(
        functools.partial(
            loss_back_kernel, cols, steps, total is not None, carry is not None, last is not False
        ),
        grid=(steps,),
        in_specs=specs,
        out_specs=[
            pl.BlockSpec((width, tile), lambda i: (0, i)),
            pl.BlockSpec(grad_z.shape, whole),
            pl.BlockSpec((8, rows // 2), whole),
        ],
        out_shape=[
            jax.ShapeDtypeStruct((width, high - low), emit),
            grad_z,
            jax.ShapeDtypeStruct((8, rows // 2), jnp.float32),
        ],
        scratch_shapes=[
            pltpu.VMEM((tile, rows), jnp.bfloat16),
            pltpu.VMEM((width, rows), jnp.float32),
        ],
        compiler_params=pltpu.CompilerParams(vmem_limit_bytes=56 << 20),
        cost_estimate=pl.CostEstimate(
            flops=6 * (high - low) * rows * width,
            bytes_accessed=8 * (high - low) * width,
            transcendentals=(high - low) * rows,
        ),
    )(*operands)


TILE = 1024


def join_stats(first, second):
    top = jnp.maximum(first[0], second[0])
    scale_one, scale_two = jnp.exp(first[0] - top), jnp.exp(second[0] - top)
    return jnp.stack(
        [top, first[1] * scale_one + second[1] * scale_two, first[2] * scale_one + second[2] * scale_two]
    )


def norm_rows(values, gain):
    center = values - jnp.mean(values, axis=-1, keepdims=True)
    spread = jnp.mean(center * center, axis=-1, keepdims=True)
    return center * lax.rsqrt(spread + EPS_NORM) * gain


def norm_back(values, gain, upstream):
    _, pullback = jax.vjp(norm_rows, values, gain)
    return pullback(upstream)


def project(inputs, weight):
    return jnp.dot(inputs, weight, preferred_element_type=jnp.float32).astype(jnp.bfloat16)


def wide_product(form, left, right):
    return jnp.einsum(
        form, left.astype(jnp.float32), right.astype(jnp.float32), precision=lax.Precision.HIGHEST
    )


def split_heads(matrix):
    return matrix.reshape(matrix.shape[0], HEADS, HD).transpose(1, 0, 2)


def join_heads(stacked):
    return stacked.transpose(1, 0, 2).reshape(stacked.shape[1], HEADS * HD)


def head_scores(query_head, key_head, query_pos, causal):
    scores = jnp.einsum(
        "qd,kd->qk", query_head, key_head, preferred_element_type=jnp.float32
    ) * HD ** (-0.5)
    if causal:
        key_pos = jnp.arange(key_head.shape[0], dtype=jnp.int32)
        scores = jnp.where(key_pos[None, :] <= query_pos[:, None], scores, -1e30)
    return scores


def attend_heads(queries, keys, values, query_pos, causal):

    def one_head(operands):
        query_head, key_head, value_head = operands
        scores = head_scores(query_head, key_head, query_pos, causal)
        row_max = jnp.max(scores, axis=-1, keepdims=True)
        weights = jnp.exp(scores - row_max)
        row_total = jnp.sum(weights, axis=-1, keepdims=True)
        probs = (weights / row_total).astype(jnp.bfloat16)
        output = jnp.dot(probs, value_head, preferred_element_type=jnp.float32).astype(jnp.bfloat16)
        return (output, (row_max + jnp.log(row_total))[:, 0])

    outputs, log_totals = lax.map(
        one_head, (split_heads(queries), split_heads(keys), split_heads(values))
    )
    return (join_heads(outputs), log_totals)


def attend_back(queries, keys, values, log_totals, upstream, query_pos, causal):

    def one_head(operands):
        query_head, key_head, value_head, log_total, up_head = operands
        scores = head_scores(query_head, key_head, query_pos, causal)
        probs = jnp.exp(scores - log_total[:, None])
        grad_probs = jnp.einsum(
            "qd,kd->qk", up_head, value_head, preferred_element_type=jnp.float32
        )
        grad_value = jnp.einsum(
            "qk,qd->kd", probs.astype(jnp.bfloat16), up_head, preferred_element_type=jnp.float32
        )
        inner = jnp.sum(probs * grad_probs, axis=-1, keepdims=True)
        grad_scores = (probs * (grad_probs - inner)).astype(jnp.bfloat16)
        grad_query = jnp.dot(grad_scores, key_head, preferred_element_type=jnp.float32) * HD ** (
            -0.5
        )
        grad_key = jnp.einsum(
            "qk,qd->kd", grad_scores, query_head, preferred_element_type=jnp.float32
        ) * HD ** (-0.5)
        return (grad_query, grad_key, grad_value)

    operands = (
        split_heads(queries),
        split_heads(keys),
        split_heads(values),
        log_totals,
        split_heads(upstream),
    )
    grad_queries, grad_keys, grad_values = lax.map(one_head, operands)
    return (join_heads(grad_queries), join_heads(grad_keys), join_heads(grad_values))


def to_experts(grouped, experts_dev, group_size, count, model_width):
    return (
        grouped.reshape(2, group_size, experts_dev, count, model_width)
        .transpose(2, 0, 1, 3, 4)
        .reshape(experts_dev, 2 * group_size * count, model_width)
    )


def from_experts(stacked, experts_dev, group_size, count, model_width):
    return (
        stacked.reshape(experts_dev, 2, group_size, count, model_width)
        .transpose(1, 2, 0, 3, 4)
        .reshape(2, group_size * experts_dev, count, model_width)
    )


def per_device(
    tokens,
    memory,
    lengths,
    targets,
    expert_ids,
    gain_self,
    gain_cross,
    gain_ffn,
    gain_out,
    wq,
    wk,
    wv,
    wo,
    cq,
    ck,
    cv,
    co,
    w_in,
    w_out,
    embed,
):
    group_index = lax.axis_index("blk")
    group_size = lax.axis_size("blk")
    batch_size = lax.axis_size("batch")
    own_rows = tokens.shape[1]
    model_width = tokens.shape[2]
    own_states = tokens[0].astype(jnp.float32)
    own_memory = memory[0]
    query_pos = group_index * own_rows + jnp.arange(own_rows, dtype=jnp.int32)
    h_one = norm_rows(own_states, gain_self).astype(jnp.bfloat16)
    queries = project(h_one, wq)
    keys_own = project(h_one, wk)
    values_own = project(h_one, wv)
    memkey_own = project(own_memory, ck)
    memval_own = project(own_memory, cv)
    all_keys, all_values, mem_keys, mem_values = (
        lax.all_gather(keys_own, "blk", axis=0, tiled=True),
        lax.all_gather(values_own, "blk", axis=0, tiled=True),
        lax.all_gather(memkey_own, "blk", axis=0, tiled=True),
        lax.all_gather(memval_own, "blk", axis=0, tiled=True),
    )
    attn_out, self_lse = attend_heads(queries, all_keys, all_values, query_pos, True)
    middle = own_states + jnp.dot(attn_out, wo, preferred_element_type=jnp.float32)
    h_two = norm_rows(middle, gain_cross).astype(jnp.bfloat16)
    cross_q = project(h_two, cq)
    cross_out, cross_lse = attend_heads(cross_q, mem_keys, mem_values, query_pos, False)
    after_cross = middle + jnp.dot(cross_out, co, preferred_element_type=jnp.float32)
    h_three = norm_rows(after_cross, gain_ffn).astype(jnp.bfloat16)
    experts_dev = w_in.shape[0]
    experts_all = experts_dev * group_size
    capacity = 3 * own_rows // (2 * experts_all)
    picks = expert_ids[:, 0, :, 0]
    onehot = (picks[:, :, None] == jnp.arange(experts_all, dtype=jnp.int32)[None, None, :]).astype(
        jnp.int32
    )
    before = jnp.cumsum(onehot, axis=1) - onehot
    slot = jnp.sum(onehot * before, axis=-1)
    target_slot = picks * capacity + slot
    routing = (
        target_slot[:, None, :]
        == jnp.arange(experts_all * capacity, dtype=jnp.int32)[None, :, None]
    ).astype(jnp.bfloat16)
    send_rows = jnp.einsum(
        "psr,rd->psd", routing, h_three, preferred_element_type=jnp.float32
    ).astype(jnp.bfloat16)
    send_rows = send_rows.reshape(2, experts_all, capacity, model_width)
    arrived = lax.all_to_all(send_rows, "blk", split_axis=1, concat_axis=1, tiled=True)
    count = arrived.shape[2]
    grouped = to_experts(arrived, experts_dev, group_size, count, model_width)
    up_values = jnp.einsum("erd,edf->erf", grouped, w_in, preferred_element_type=jnp.float32)
    activity = jax.nn.gelu(up_values).astype(jnp.bfloat16)
    result = jnp.einsum("erf,efd->erd", activity, w_out, preferred_element_type=jnp.float32).astype(
        jnp.bfloat16
    )
    result = from_experts(result, experts_dev, group_size, count, model_width)
    returned = lax.all_to_all(result, "blk", split_axis=1, concat_axis=1, tiled=True)
    returned, arrived = (returned, arrived)
    expert_out = jnp.einsum(
        "psr,psd->prd",
        routing,
        returned.reshape(2, experts_all * capacity, model_width),
        preferred_element_type=jnp.float32,
    )
    outputs = after_cross[None] + expert_out
    z_pair = norm_rows(outputs, gain_out).astype(jnp.bfloat16)
    z_blocks = gather_blocks(z_pair, "blk")
    vocab_part = embed.shape[0]
    vocab_total = vocab_part * group_size
    padded = -(-vocab_part // TILE) * TILE
    embed_pad = jnp.pad(embed, ((0, padded - vocab_part), (0, 0)))
    embed_t = embed_pad.T
    count = max(2, group_size * own_rows // 1024)
    per_group = group_size // count
    groups = [list(range(k * per_group, (k + 1) * per_group)) for k in range(count)]
    group_z = [
        jnp.stack([z_blocks[j] for j in group], axis=1).reshape(-1, model_width) for group in groups
    ]
    stats = jnp.stack([vocab_stats(embed, rows) for rows in group_z])
    stats = stats.reshape(count, 3, 2, per_group, own_rows).transpose(1, 0, 3, 2, 4)
    stats = stats.reshape(3, group_size, 2, own_rows)
    bit = 1
    while bit < group_size:
        moved = swap(stats, "blk", bit)
        moved = moved.reshape(3, group_size // (2 * bit), 2, bit, 2, own_rows)[:, :, ::-1]
        stats = join_stats(stats, moved.reshape(stats.shape))
        bit *= 2
    log_total = stats[0] + jnp.log(stats[1])
    expect = stats[2] / stats[1]
    positions = jnp.stack(
        [
            (group_index ^ j) * own_rows + jnp.arange(own_rows, dtype=jnp.int32)
            for j in range(group_size)
        ]
    )
    live = positions < lengths[0]
    labels = jnp.stack(
        [
            lax.dynamic_slice_in_dim(targets[0], (group_index ^ j) * own_rows, own_rows)
            for j in range(group_size)
        ]
    )
    labels = jnp.where(live, labels, -1)
    live = live.astype(jnp.float32)
    row_values = jnp.stack(
        [
            jnp.where(live > 0, log_total[:, 0] * LOG2E, 1e30),
            jnp.where(live > 0, log_total[:, 1] * LOG2E, 1e30),
            2.0 - expect[:, 0],
            2.0 + expect[:, 1],
            live * (1.0 - SMOOTH + SMOOTH / vocab_total),
            live * (SMOOTH / vocab_total),
        ]
    )
    relative = relative_index("batch")
    vocab_base = (group_index * vocab_part).astype(jnp.int32).reshape(1)
    total = None
    grad_z_parts, smooth_parts, embed_chunks = {}, {}, []
    for at in range(count - 1, -1, -1):
        group = groups[at]
        z_t = group_z[at].T
        z_t = pick_parts(z_t.reshape(batch_size, -1, z_t.shape[1]), relative).reshape(z_t.shape)
        at_rows = [group[0], group[-1] + 1]
        part_rows = row_values[:, at_rows[0] : at_rows[1]].reshape(6, -1)
        part_labels = labels[at_rows[0] : at_rows[1]].reshape(1, -1)
        if at > 0:
            total, grad_z, smooth = loss_back(
                vocab_base, embed_pad, embed_t, group_z[at], z_t, part_rows, part_labels,
                (0, padded), total, None, None,
            )
        else:
            grad_z, smooth = None, 0.0
            chunk = max(padded // 4, TILE)
            for low in range(0, padded, chunk):
                grad_embed, grad_z, more = loss_back(
                    vocab_base, embed_pad, embed_t, group_z[at], z_t, part_rows, part_labels,
                    (low, low + chunk), total, grad_z, low + chunk == padded,
                )
                smooth = smooth + more
                grad_embed = grad_embed.reshape(2, batch_size // 2, model_width // batch_size, chunk)
                embed_chunks.append(ring_scatter(grad_embed, "batch", low > 0))
        grad_z = grad_z.reshape(2, per_group, own_rows, model_width)
        smooth = jnp.sum(smooth, axis=0).reshape(per_group, own_rows)
        for k, j in enumerate(group):
            grad_z_parts[j] = grad_z[:, k]
            smooth_parts[j] = smooth[k]
    grad_z_own = scatter_blocks(
        [grad_z_parts[j] for j in range(group_size)], "blk"
    ).astype(jnp.float32)
    smooth_own = scatter_blocks([smooth_parts[j] for j in range(group_size)], "blk")
    own_loss = live[0] * (log_total[0, 0] + log_total[0, 1] + expect[0, 0] - expect[0, 1]) - smooth_own
    embed_sum = jnp.concatenate(embed_chunks, axis=-1)[:, :vocab_part].astype(jnp.float32).T
    grad_outputs, grad_gain_out = norm_back(outputs, gain_out, grad_z_own)
    send_grads = jnp.einsum(
        "psr,prd->psd",
        routing,
        grad_outputs.astype(jnp.bfloat16),
        preferred_element_type=jnp.float32,
    ).astype(jnp.bfloat16)
    send_grads = send_grads.reshape(2, experts_all, capacity, model_width)
    arrived_grads = lax.all_to_all(send_grads, "blk", split_axis=1, concat_axis=1, tiled=True)
    grouped = to_experts(arrived, experts_dev, group_size, capacity, model_width)
    grouped_grads = to_experts(arrived_grads, experts_dev, group_size, capacity, model_width)
    up_values = jnp.einsum("erd,edf->erf", grouped, w_in, preferred_element_type=jnp.float32)
    activity = jax.nn.gelu(up_values).astype(jnp.bfloat16)
    grad_activity = jnp.einsum(
        "erd,efd->erf", grouped_grads, w_out, preferred_element_type=jnp.float32
    )
    _, gelu_pull = jax.vjp(jax.nn.gelu, up_values)
    grad_up = gelu_pull(grad_activity)[0].astype(jnp.bfloat16)
    w_out_local = jnp.einsum(
        "erf,erd->efd", activity, grouped_grads, preferred_element_type=jnp.float32
    )
    w_in_local = jnp.einsum("erd,erf->edf", grouped, grad_up, preferred_element_type=jnp.float32)
    grad_rows = jnp.einsum("erf,edf->erd", grad_up, w_in, preferred_element_type=jnp.float32)
    grad_rows = from_experts(grad_rows, experts_dev, group_size, capacity, model_width)
    back_grads = lax.all_to_all(
        grad_rows.astype(jnp.bfloat16), "blk", split_axis=1, concat_axis=1, tiled=True
    ).astype(grad_rows.dtype)
    grad_h_three = jnp.einsum(
        "psr,psd->rd",
        routing.astype(jnp.float32),
        back_grads.reshape(2, experts_all * capacity, model_width),
    )
    norm_part, grad_gain_ffn = norm_back(after_cross, gain_ffn, grad_h_three)
    grad_after = grad_outputs[0] + grad_outputs[1] + norm_part
    branch_two = grad_after.astype(jnp.bfloat16)
    grad_co = jnp.einsum("rd,re->de", cross_out, branch_two, preferred_element_type=jnp.float32)
    grad_cross_out = jnp.einsum(
        "re,de->rd", branch_two, co, preferred_element_type=jnp.float32
    ).astype(jnp.bfloat16)
    grad_cross_q, memkey_part, memval_part = attend_back(
        cross_q, mem_keys, mem_values, cross_lse, grad_cross_out, query_pos, False
    )
    cross_q_low = grad_cross_q.astype(jnp.bfloat16)
    grad_cq = jnp.einsum("rd,re->de", h_two, cross_q_low, preferred_element_type=jnp.float32)
    grad_h_two = jnp.einsum("re,de->rd", cross_q_low, cq, preferred_element_type=jnp.float32)
    norm_part, grad_gain_cross = norm_back(middle, gain_cross, grad_h_two)
    grad_middle = grad_after + norm_part
    branch_one = grad_middle.astype(jnp.bfloat16)
    grad_wo = jnp.einsum("rd,re->de", attn_out, branch_one, preferred_element_type=jnp.float32)
    grad_attn_out = jnp.einsum(
        "re,de->rd", branch_one, wo, preferred_element_type=jnp.float32
    ).astype(jnp.bfloat16)
    grad_queries, key_part, value_part = attend_back(
        queries, all_keys, all_values, self_lse, grad_attn_out, query_pos, True
    )
    queries_low = grad_queries.astype(jnp.bfloat16)
    grad_wq = jnp.einsum("rd,re->de", h_one, queries_low, preferred_element_type=jnp.float32)
    grad_h_one = jnp.einsum("re,de->rd", queries_low, wq, preferred_element_type=jnp.float32)
    grad_keys, grad_values, grad_memkeys, grad_memvals = (
        lax.psum_scatter(
            key_part.astype(jnp.bfloat16), "blk", scatter_dimension=0, tiled=True
        ).astype(jnp.float32),
        lax.psum_scatter(
            value_part.astype(jnp.bfloat16), "blk", scatter_dimension=0, tiled=True
        ).astype(jnp.float32),
        lax.psum_scatter(
            memkey_part.astype(jnp.bfloat16), "blk", scatter_dimension=0, tiled=True
        ).astype(jnp.float32),
        lax.psum_scatter(
            memval_part.astype(jnp.bfloat16), "blk", scatter_dimension=0, tiled=True
        ).astype(jnp.float32),
    )
    own_key_term = wide_product("re,de->rd", grad_keys, wk) + wide_product(
        "re,de->rd", grad_values, wv
    )
    grad_wk = wide_product("rd,re->de", h_one, grad_keys)
    grad_wv = wide_product("rd,re->de", h_one, grad_values)
    grad_ck = wide_product("rd,re->de", own_memory, grad_memkeys)
    grad_cv = wide_product("rd,re->de", own_memory, grad_memvals)
    grad_memory = wide_product("re,de->rd", grad_memkeys, ck) + wide_product(
        "re,de->rd", grad_memvals, cv
    )
    grad_h_one = grad_h_one + own_key_term
    norm_part, grad_gain_self = norm_back(own_states, gain_self, grad_h_one)
    grad_tokens = grad_middle + norm_part
    row_part = model_width // batch_size
    col_part = model_width // group_size

    def sum_weights(weights):
        stacked = jnp.stack([weight.astype(jnp.bfloat16) for weight in weights])
        parts = [
            lax.dynamic_slice_in_dim(stacked, (group_index ^ j) * col_part, col_part, axis=2)
            for j in range(group_size)
        ]
        summed = scatter_blocks(parts, "blk")
        summed = summed.reshape(len(weights), batch_size, row_part, col_part).transpose(1, 0, 2, 3)
        return ring_scatter(pick_parts(summed, relative), "batch", True).astype(jnp.float32)

    cross_sums = sum_weights([grad_cq, grad_ck, grad_cv, grad_co])
    self_sums = sum_weights([grad_wq, grad_wk, grad_wv, grad_wo])
    summed_weights = [self_sums[k] for k in range(4)] + [cross_sums[k] for k in range(4)]
    summed_gains = jnp.stack([grad_gain_self, grad_gain_cross, grad_gain_ffn, grad_gain_out])
    for axis in ("blk", "batch"):
        bit = 1
        while bit < lax.axis_size(axis):
            summed_gains = summed_gains + swap(summed_gains, axis, bit)
            bit *= 2
    w_in_parts = w_in_local[0].astype(jnp.bfloat16).reshape(batch_size, row_part, -1)
    w_in_sum = ring_scatter(pick_parts(w_in_parts, relative), "batch", True).astype(jnp.float32)[None]
    w_out_parts = w_out_local[0].astype(jnp.bfloat16).reshape(batch_size, -1, model_width)
    w_out_sum = ring_scatter(pick_parts(w_out_parts, relative), "batch", True).astype(jnp.float32)[None]
    return (
        own_loss[None],
        grad_tokens[None],
        grad_memory[None],
        summed_gains[0],
        summed_gains[1],
        summed_gains[2],
        summed_gains[3],
        summed_weights[0],
        summed_weights[1],
        summed_weights[2],
        summed_weights[3],
        summed_weights[4],
        summed_weights[5],
        summed_weights[6],
        summed_weights[7],
        w_in_sum,
        w_out_sum,
        embed_sum,
    )


def solution(mesh):
    return jax.shard_map(
        per_device,
        mesh=mesh,
        in_specs=(
            P("batch", "blk", None),
            P("batch", "blk", None),
            P("batch"),
            P("batch", None),
            P(None, "batch", "blk", None),
            P(),
            P(),
            P(),
            P(),
            P(),
            P(),
            P(),
            P(),
            P(),
            P(),
            P(),
            P(),
            P("blk", None, None),
            P("blk", None, None),
            P("blk", None),
        ),
        out_specs=(
            P("batch", "blk"),
            P("batch", "blk", None),
            P("batch", "blk", None),
            P(),
            P(),
            P(),
            P(),
            P("batch", "blk"),
            P("batch", "blk"),
            P("batch", "blk"),
            P("batch", "blk"),
            P("batch", "blk"),
            P("batch", "blk"),
            P("batch", "blk"),
            P("batch", "blk"),
            P("blk", "batch", None),
            P("blk", "batch", None),
            P("blk", "batch"),
        ),
        check_vma=False,
    )
```

```python
import functools

import jax
import jax.numpy as jnp
from jax import lax
from jax.experimental import pallas as pl
from jax.experimental.pallas import tpu as pltpu
from jax.sharding import PartitionSpec as P

HEADS = 8
HD = 64


EPS_NORM = 1e-05
SMOOTH = 0.1
LOG2E = 1.4426950408889634
NN = (((1,), (0,)), ((), ()))
NT = (((1,), (1,)), ((), ()))


def dot(left, right, dims):
    return lax.dot_general(left, right, dims, preferred_element_type=jnp.float32)


def swap(value, axis, mask):
    size = lax.axis_size(axis)
    return lax.ppermute(value, axis, [(i, i ^ mask) for i in range(size)])


def gather_blocks(own, axis):
    size = lax.axis_size(axis)
    blocks = {0: own}
    bit = 2
    while bit < size:
        for k in range(0, bit, 2):
            blocks[bit | k] = swap(blocks[k], axis, bit)
        bit *= 2
    for k in range(0, size, 2):
        blocks[k | 1] = swap(blocks[k], axis, 1)
    return [blocks[j] for j in range(size)]


def scatter_blocks(parts, axis):
    parts = list(parts)
    size = len(parts)
    bit = 1
    while bit < size:
        odd = [j for j in range(0, size, bit) if j & bit]
        even = [j ^ bit for j in odd]
        moved = swap(jnp.stack([parts[j] for j in odd]), axis, bit)
        for k, j in enumerate(even):
            parts[j] = add_low(parts[j], moved[k])
        bit *= 2
    return parts[0]


def add_low(left, right):
    return (left.astype(jnp.float32) + right.astype(jnp.float32)).astype(left.dtype)


def ring_order(size):
    return list(range(0, 1)) + list(range(1, size, 2)) + list(range(size - 2, 0, -2))


def relative_index(axis):
    size = lax.axis_size(axis)
    high = size // 2
    order = jnp.asarray(ring_order(high), jnp.int32)
    place = [ring_order(high).index(i) for i in range(high)]
    me = lax.axis_index(axis)
    mine = jnp.asarray(place, jnp.int32)[me // 2]
    steps = jnp.mod(mine - 1 - jnp.arange(high, dtype=jnp.int32), high)
    lows = me % 2
    return jnp.stack([order[steps] * 2 + (lows ^ low) for low in range(2)]).reshape(size)


def ring_scatter(parts, axis, pair_first):
    high = parts.shape[1]
    order = ring_order(high)
    links = [
        (order[k] * 2 + low, order[(k + 1) % high] * 2 + low) for k in range(high) for low in range(2)
    ]

    def ring(value):
        total = value[0]
        for step in range(high - 1):
            total = add_low(lax.ppermute(total, axis, links), value[step + 1])
        return total

    if pair_first:
        return ring(add_low(parts[0], swap(parts[1], axis, 1)))
    total = ring(parts.transpose((1, 0) + tuple(range(2, parts.ndim))))
    return add_low(total[0], swap(total[1], axis, 1))


def pick_parts(value, index):
    count = value.shape[0]
    parts = [lax.dynamic_index_in_dim(value, index[k], 0, keepdims=False) for k in range(count)]
    return jnp.stack(parts).reshape((2, count // 2) + value.shape[1:])


def stats_kernel(cols, steps, embed_ref, z_ref, out_ref, max_ref, sum_ref, mix_ref):
    step = pl.program_id(0)
    half = z_ref.shape[0] // 2

    @pl.when(step == 0)
    def _():
        max_ref[...] = jnp.full_like(max_ref, -jnp.inf)
        sum_ref[...] = jnp.zeros_like(sum_ref)
        mix_ref[...] = jnp.zeros_like(mix_ref)

    embed = embed_ref[...]
    for col in range(half // cols):
        places = [slice(p * half + col * cols, p * half + (col + 1) * cols) for p in range(2)]
        logits = [dot(embed, z_ref[place, :], NT).reshape(-1, 8, cols) for place in places]
        apart = logits[0] - logits[1]
        for place, logit in zip(places, logits):
            old = max_ref[:, place]
            new = jnp.maximum(old, jnp.max(logit, axis=0))
            max_ref[:, place] = new
            scale = jnp.exp2((old - new) * LOG2E)
            weights = jnp.exp2((logit - new[None]) * LOG2E)
            sum_ref[:, place] = sum_ref[:, place] * scale + jnp.sum(weights, axis=0)
            mix_ref[:, place] = mix_ref[:, place] * scale + jnp.sum(weights * apart, axis=0)

    @pl.when(step == steps - 1)
    def _():
        top = jnp.max(max_ref[...], axis=0, keepdims=True)
        scale = jnp.exp2((max_ref[...] - top) * LOG2E)
        out_ref[0:1, :] = top
        out_ref[1:2, :] = jnp.sum(sum_ref[...] * scale, axis=0, keepdims=True)
        out_ref[2:3, :] = jnp.sum(mix_ref[...] * scale, axis=0, keepdims=True)


def row_tile(rows, limit):
    return max(size for size in range(16, limit + 1, 16) if rows % size == 0)


def vocab_stats(embed, z_rows):
    vocab, width = embed.shape
    rows = z_rows.shape[0]
    tile = row_tile(vocab, 800)
    cols = min(256, rows // 2)
    steps = vocab // tile
    return pl.pallas_call(
        functools.partial(stats_kernel, cols, steps),
        grid=(steps,),
        in_specs=[
            pl.BlockSpec((tile, width), lambda i: (i, 0)),
            pl.BlockSpec((rows, width), lambda i: (0, 0)),
        ],
        out_specs=pl.BlockSpec((3, rows), lambda i: (0, 0)),
        out_shape=jax.ShapeDtypeStruct((3, rows), jnp.float32),
        scratch_shapes=[pltpu.VMEM((8, rows), jnp.float32)] * 3,
        compiler_params=pltpu.CompilerParams(vmem_limit_bytes=48 << 20),
        cost_estimate=pl.CostEstimate(
            flops=2 * vocab * rows * width,
            bytes_accessed=2 * (vocab + rows) * width,
            transcendentals=vocab * rows,
        ),
    )(embed, z_rows)


def padded_kernel(count, embed_ref, pad_ref, turned_ref):
    start = pl.program_id(0) * embed_ref.shape[0]
    rows = lax.broadcasted_iota(jnp.int32, embed_ref.shape, 0) + start
    values = jnp.where(rows < count, embed_ref[...], jnp.zeros_like(embed_ref[...]))
    pad_ref[...] = values
    turned_ref[...] = values.T


def padded_embed(embed, padded):
    count, width = embed.shape
    return pl.pallas_call(
        functools.partial(padded_kernel, count),
        grid=(padded // TILE,),
        in_specs=[pl.BlockSpec((TILE, width), lambda i: (i, 0))],
        out_specs=[
            pl.BlockSpec((TILE, width), lambda i: (i, 0)),
            pl.BlockSpec((width, TILE), lambda i: (0, i)),
        ],
        out_shape=[
            jax.ShapeDtypeStruct((padded, width), embed.dtype),
            jax.ShapeDtypeStruct((width, padded), embed.dtype),
        ],
        compiler_params=pltpu.CompilerParams(vmem_limit_bytes=24 << 20),
        cost_estimate=pl.CostEstimate(
            flops=0, bytes_accessed=6 * padded * width, transcendentals=0
        ),
    )(embed)


def loss_back_kernel(cols, steps, has_total, has_carry, last, *refs):
    base_ref, embed_ref, embed_t_ref, z_ref, z_t_ref, row_ref, label_ref = refs[:7]
    refs = list(refs[7:])
    total_ref = refs.pop(0) if has_total else None
    carry_ref = refs.pop(0) if has_carry else None
    grad_embed_ref, grad_z_ref, loss_ref, grad_ref, sum_ref = refs
    step = pl.program_id(0)
    half = z_ref.shape[0] // 2
    tile = embed_ref.shape[0]

    @pl.when(step == 0)
    def _():
        sum_ref[...] = carry_ref[...] if has_carry else jnp.zeros_like(sum_ref)
        loss_ref[...] = jnp.zeros_like(loss_ref)

    embed = embed_ref[...]
    ids = lax.broadcasted_iota(jnp.int32, (tile // 8, 8, cols), 0) * 8
    ids = ids + lax.broadcasted_iota(jnp.int32, (tile // 8, 8, cols), 1)
    base = base_ref[0] + step * tile
    for col in range(half // cols):
        one = slice(col * cols, (col + 1) * cols)
        two = slice(half + col * cols, half + (col + 1) * cols)
        logit_one = dot(embed, z_ref[one, :], NT).reshape(-1, 8, cols)
        logit_two = dot(embed, z_ref[two, :], NT).reshape(-1, 8, cols)
        row = [row_ref[k : k + 1, one].reshape(1, 1, cols) for k in range(6)]
        prob_one = jnp.exp2(logit_one * LOG2E - row[0])
        prob_two = jnp.exp2(logit_two * LOG2E - row[1])
        apart = logit_one - logit_two
        hits = ids == (label_ref[0:1, one] - base).reshape(1, 1, cols)
        smooth = jnp.where(hits, row[4], row[5])
        grad_one = prob_one * (apart + row[2]) - (prob_two + smooth)
        grad_two = prob_two * (row[3] - apart) - (prob_one + smooth)
        loss_ref[:, one] += jnp.sum(smooth * (logit_one + logit_two), axis=0)
        grad_ref[:, one] = grad_one.reshape(tile, cols).astype(jnp.bfloat16)
        grad_ref[:, two] = grad_two.reshape(tile, cols).astype(jnp.bfloat16)
    grads = grad_ref[...]
    grad_embed = dot(z_t_ref[...], grads, NT)
    if has_total:
        grad_embed = grad_embed + total_ref[...]
    grad_embed_ref[...] = grad_embed.astype(grad_embed_ref.dtype)
    sum_ref[...] += dot(embed_t_ref[...], grads, NN)

    @pl.when(step == steps - 1)
    def _():
        if last:
            grad_z_ref[...] = sum_ref[...].T.astype(grad_z_ref.dtype)
        else:
            grad_z_ref[...] = sum_ref[...]


def loss_back(base, embed, embed_t, z_rows, z_t, row_values, labels, span, total, carry, last):
    width = embed.shape[1]
    rows = z_rows.shape[0]
    tile = TILE
    low, high = span
    steps, first = (high - low) // tile, low // tile
    cols = min(256, rows // 2)
    operands = [base + low, embed, embed_t, z_rows, z_t, row_values, labels]
    whole = lambda i: (0, 0)
    specs = [
        pl.BlockSpec(memory_space=pltpu.SMEM),
        pl.BlockSpec((tile, width), lambda i: (i + first, 0)),
        pl.BlockSpec((width, tile), lambda i: (0, i + first)),
        pl.BlockSpec((rows, width), whole),
        pl.BlockSpec((width, rows), whole),
        pl.BlockSpec((6, rows // 2), whole),
        pl.BlockSpec((1, rows // 2), whole),
    ]
    if total is not None:
        operands.append(total)
        specs.append(pl.BlockSpec((width, tile), lambda i: (0, i + first)))
    if carry is not None:
        operands.append(carry)
        specs.append(pl.BlockSpec((width, rows), whole))
    emit = jnp.bfloat16 if last is not None else jnp.float32
    grad_z = (
        jax.ShapeDtypeStruct((rows, width), jnp.bfloat16)
        if last is not False
        else jax.ShapeDtypeStruct((width, rows), jnp.float32)
    )
    return pl.pallas_call(
        functools.partial(
            loss_back_kernel, cols, steps, total is not None, carry is not None, last is not False
        ),
        grid=(steps,),
        in_specs=specs,
        out_specs=[
            pl.BlockSpec((width, tile), lambda i: (0, i)),
            pl.BlockSpec(grad_z.shape, whole),
            pl.BlockSpec((8, rows // 2), whole),
        ],
        out_shape=[
            jax.ShapeDtypeStruct((width, high - low), emit),
            grad_z,
            jax.ShapeDtypeStruct((8, rows // 2), jnp.float32),
        ],
        scratch_shapes=[
            pltpu.VMEM((tile, rows), jnp.bfloat16),
            pltpu.VMEM((width, rows), jnp.float32),
        ],
        compiler_params=pltpu.CompilerParams(vmem_limit_bytes=56 << 20),
        cost_estimate=pl.CostEstimate(
            flops=6 * (high - low) * rows * width,
            bytes_accessed=8 * (high - low) * width,
            transcendentals=(high - low) * rows,
        ),
    )(*operands)


TILE = 1024


def join_stats(first, second):
    top = jnp.maximum(first[0], second[0])
    scale_one, scale_two = jnp.exp(first[0] - top), jnp.exp(second[0] - top)
    return jnp.stack(
        [top, first[1] * scale_one + second[1] * scale_two, first[2] * scale_one + second[2] * scale_two]
    )


def norm_rows(values, gain):
    center = values - jnp.mean(values, axis=-1, keepdims=True)
    spread = jnp.mean(center * center, axis=-1, keepdims=True)
    return center * lax.rsqrt(spread + EPS_NORM) * gain


def norm_back(values, gain, upstream):
    _, pullback = jax.vjp(norm_rows, values, gain)
    return pullback(upstream)


SCALE = HD ** (-0.5)


def head_lanes(pair, head):
    lanes = lax.broadcasted_iota(jnp.int32, pair.shape, 1)
    return jnp.where((lanes >= HD) == (head % 2 == 1), pair, jnp.zeros_like(pair))


def block_bias(me, rows, blocks, causal):
    if not causal:
        return [None] * blocks
    keys = lax.broadcasted_iota(jnp.int32, (rows, rows), 0)
    queries = lax.broadcasted_iota(jnp.int32, (rows, rows), 1)
    biases = [jnp.where(keys <= queries, 0.0, -1e30)]
    for block in range(1, blocks):
        biases.append(jnp.where((me ^ block) < me, 0.0, -1e30))
    return biases


def head_weights(keys, query, biases, rows):
    scores = []
    for block, bias in enumerate(biases):
        part = dot(keys[block * rows : (block + 1) * rows], query, NT)
        scores.append(part if bias is None else part + bias)
    return scores


def attend_kernel(causal, me_ref, source_ref, memory_ref, residual_ref, gain_ref,
                  wq_ref, wk_ref, wv_ref, wo_ref,
                  query_ref, key_ref, value_ref, out_ref, log_ref, sum_ref, next_ref,
                  value_t_ref, out_t_ref):
    rows = source_ref.shape[0]
    blocks = memory_ref.shape[0] // rows
    query_ref[...] = dot(source_ref[...], wq_ref[...], NN).astype(jnp.bfloat16)
    key_ref[...] = dot(memory_ref[...], wk_ref[...], NN).astype(jnp.bfloat16)
    values = dot(memory_ref[...], wv_ref[...], NN).astype(jnp.bfloat16)
    value_ref[...] = values
    value_t_ref[...] = values.T
    biases = block_bias(me_ref[0], rows, blocks, causal)
    factor = SCALE * LOG2E
    for head in range(HEADS):
        lanes = slice(head // 2 * 128, head // 2 * 128 + 128)
        query = head_lanes(query_ref[:, lanes], head)
        scores = head_weights(key_ref[:, lanes], query, biases, rows)
        top = functools.reduce(
            jnp.maximum, [jnp.max(part.reshape(-1, 8, rows), axis=0) for part in scores]
        )
        top = jnp.max(top, axis=0, keepdims=True) * factor
        weights = [jnp.exp2(part * factor - top) for part in scores]
        total = sum(jnp.sum(part.reshape(-1, 8, rows), axis=0) for part in weights)
        total = jnp.sum(total, axis=0, keepdims=True)
        log_ref[head : head + 1, :] = top + jnp.log2(total)
        weights = jnp.concatenate([part.astype(jnp.bfloat16) for part in weights], axis=0)
        place = slice(head * HD, (head + 1) * HD)
        out_t_ref[place, :] = dot(value_t_ref[place, :], weights, NN) / total
    out = out_t_ref[...].T.astype(jnp.bfloat16)
    out_ref[...] = out
    states = residual_ref[...] + dot(out, wo_ref[...], NN)
    sum_ref[...] = states
    center = states - jnp.mean(states, axis=-1, keepdims=True)
    spread = jnp.mean(center * center, axis=-1, keepdims=True)
    next_ref[...] = (center * lax.rsqrt(spread + EPS_NORM) * gain_ref[...]).astype(jnp.bfloat16)


def attend(me, source, memory, residual, gain, wq, wk, wv, wo, causal):
    rows, width = source.shape
    count = memory.shape[0]
    low = lambda *shape: jax.ShapeDtypeStruct(shape, jnp.bfloat16)
    wide = lambda *shape: jax.ShapeDtypeStruct(shape, jnp.float32)
    vmem = pl.BlockSpec(memory_space=pltpu.VMEM)
    return pl.pallas_call(
        functools.partial(attend_kernel, causal),
        in_specs=[pl.BlockSpec(memory_space=pltpu.SMEM)] + [vmem] * 8,
        out_specs=[vmem] * 7,
        out_shape=[
            low(rows, width), low(count, width), low(count, width), low(rows, width),
            wide(HEADS, rows), wide(rows, width), low(rows, width),
        ],
        scratch_shapes=[pltpu.VMEM((width, count), jnp.bfloat16), pltpu.VMEM((width, rows), jnp.float32)],
        compiler_params=pltpu.CompilerParams(vmem_limit_bytes=48 << 20),
        cost_estimate=pl.CostEstimate(
            flops=4 * rows * count * width + 4 * count * width * width + 4 * rows * width * width,
            bytes_accessed=8 * count * width + 8 * width * width,
            transcendentals=HEADS * rows * count,
        ),
    )(me, source, memory, residual, gain[None], wq, wk, wv, wo)


def attend_back_kernel(causal, me_ref, branch_ref, wo_ref, query_ref, key_ref, value_ref, log_ref,
                       grad_query_ref, grad_key_ref, grad_value_ref,
                       key_t_ref, up_ref, query_t_ref):
    rows = query_ref.shape[0]
    blocks = key_ref.shape[0] // rows
    up_ref[...] = dot(branch_ref[...], wo_ref[...], NT).astype(jnp.bfloat16)
    key_t_ref[...] = key_ref[...].T
    biases = block_bias(me_ref[0], rows, blocks, causal)
    factor = SCALE * LOG2E
    for pair in range(HEADS // 2):
        lanes = slice(pair * 128, pair * 128 + 128)
        grad_keys, grad_values = 0.0, 0.0
        for head in (2 * pair, 2 * pair + 1):
            query = head_lanes(query_ref[:, lanes], head)
            upstream = head_lanes(up_ref[:, lanes], head)
            log_total = log_ref[head : head + 1, :]
            scores = head_weights(key_ref[:, lanes], query, biases, rows)
            probs = jnp.concatenate([jnp.exp2(part * factor - log_total) for part in scores], axis=0)
            grad_probs = dot(value_ref[:, lanes], upstream, NT)
            inner = jnp.sum((probs * grad_probs).reshape(-1, 8, rows), axis=0)
            inner = jnp.sum(inner, axis=0, keepdims=True)
            grad_scores = (probs * (grad_probs - inner)).astype(jnp.bfloat16)
            grad_values = grad_values + dot(probs.astype(jnp.bfloat16), upstream, NN)
            grad_keys = grad_keys + dot(grad_scores, query, NN)
            place = slice(head * HD, (head + 1) * HD)
            query_t_ref[place, :] = dot(key_t_ref[place, :], grad_scores, NN) * SCALE
        grad_value_ref[:, lanes] = grad_values.astype(jnp.bfloat16)
        grad_key_ref[:, lanes] = (grad_keys * SCALE).astype(jnp.bfloat16)
    grad_query_ref[...] = query_t_ref[...].T.astype(jnp.bfloat16)


def attend_back(me, branch, wo, queries, keys, values, log_totals, causal):
    rows, width = queries.shape
    count = keys.shape[0]
    low = lambda *shape: jax.ShapeDtypeStruct(shape, jnp.bfloat16)
    vmem = pl.BlockSpec(memory_space=pltpu.VMEM)
    return pl.pallas_call(
        functools.partial(attend_back_kernel, causal),
        in_specs=[pl.BlockSpec(memory_space=pltpu.SMEM)] + [vmem] * 6,
        out_specs=[vmem] * 3,
        out_shape=[low(rows, width), low(count, width), low(count, width)],
        scratch_shapes=[
            pltpu.VMEM((width, count), jnp.bfloat16),
            pltpu.VMEM((rows, width), jnp.bfloat16),
            pltpu.VMEM((width, rows), jnp.float32),
        ],
        compiler_params=pltpu.CompilerParams(vmem_limit_bytes=48 << 20),
        cost_estimate=pl.CostEstimate(
            flops=10 * rows * count * width + 2 * rows * width * width,
            bytes_accessed=8 * count * width + 2 * width * width,
            transcendentals=HEADS * rows * count,
        ),
    )(me, branch, wo, queries, keys, values, log_totals)


def weight_grad(left, right):
    return jnp.einsum("rd,re->de", left, right, preferred_element_type=jnp.float32)


def to_experts(grouped, experts_dev, group_size, count, model_width):
    return (
        grouped.reshape(2, group_size, experts_dev, count, model_width)
        .transpose(2, 0, 1, 3, 4)
        .reshape(experts_dev, 2 * group_size * count, model_width)
    )


def from_experts(stacked, experts_dev, group_size, count, model_width):
    return (
        stacked.reshape(experts_dev, 2, group_size, count, model_width)
        .transpose(1, 2, 0, 3, 4)
        .reshape(2, group_size * experts_dev, count, model_width)
    )


def per_device(
    tokens,
    memory,
    lengths,
    targets,
    expert_ids,
    gain_self,
    gain_cross,
    gain_ffn,
    gain_out,
    wq,
    wk,
    wv,
    wo,
    cq,
    ck,
    cv,
    co,
    w_in,
    w_out,
    embed,
):
    group_index = lax.axis_index("blk")
    group_size = lax.axis_size("blk")
    batch_size = lax.axis_size("batch")
    own_rows = tokens.shape[1]
    model_width = tokens.shape[2]
    own_states = tokens[0].astype(jnp.float32)
    own_memory = memory[0]
    me = group_index.astype(jnp.int32).reshape(1)
    h_one = norm_rows(own_states, gain_self).astype(jnp.bfloat16)
    h_all = jnp.concatenate(gather_blocks(h_one, "blk"))
    memory_all = jnp.concatenate(gather_blocks(own_memory, "blk"))
    queries, all_keys, all_values, attn_out, self_log, middle, h_two = attend(
        me, h_one, h_all, own_states, gain_cross, wq, wk, wv, wo, True
    )
    cross_q, mem_keys, mem_values, cross_out, cross_log, after_cross, h_three = attend(
        me, h_two, memory_all, middle, gain_ffn, cq, ck, cv, co, False
    )
    experts_dev = w_in.shape[0]
    experts_all = experts_dev * group_size
    capacity = 3 * own_rows // (2 * experts_all)
    picks = expert_ids[:, 0, :, 0]
    onehot = (picks[:, :, None] == jnp.arange(experts_all, dtype=jnp.int32)[None, None, :]).astype(
        jnp.int32
    )
    before = jnp.cumsum(onehot, axis=1) - onehot
    slot = jnp.sum(onehot * before, axis=-1)
    target_slot = picks * capacity + slot
    routing = (
        target_slot[:, None, :]
        == jnp.arange(experts_all * capacity, dtype=jnp.int32)[None, :, None]
    ).astype(jnp.bfloat16)
    send_rows = jnp.einsum(
        "psr,rd->psd", routing, h_three, preferred_element_type=jnp.float32
    ).astype(jnp.bfloat16)
    send_rows = send_rows.reshape(2, experts_all, capacity, model_width)
    arrived = lax.all_to_all(send_rows, "blk", split_axis=1, concat_axis=1, tiled=True)
    count = arrived.shape[2]
    grouped = to_experts(arrived, experts_dev, group_size, count, model_width)
    up_values = jnp.einsum("erd,edf->erf", grouped, w_in, preferred_element_type=jnp.float32)
    activity = jax.nn.gelu(up_values).astype(jnp.bfloat16)
    result = jnp.einsum("erf,efd->erd", activity, w_out, preferred_element_type=jnp.float32).astype(
        jnp.bfloat16
    )
    result = from_experts(result, experts_dev, group_size, count, model_width)
    returned = lax.all_to_all(result, "blk", split_axis=1, concat_axis=1, tiled=True)
    returned, arrived = (returned, arrived)
    expert_out = jnp.einsum(
        "psr,psd->prd",
        routing,
        returned.reshape(2, experts_all * capacity, model_width),
        preferred_element_type=jnp.float32,
    )
    outputs = after_cross[None] + expert_out
    z_pair = norm_rows(outputs, gain_out).astype(jnp.bfloat16)
    z_blocks = gather_blocks(z_pair, "blk")
    vocab_part = embed.shape[0]
    vocab_total = vocab_part * group_size
    padded = -(-vocab_part // TILE) * TILE
    embed_pad, embed_t = padded_embed(embed, padded)
    count = max(2, group_size * own_rows // 1024)
    per_group = group_size // count
    groups = [list(range(k * per_group, (k + 1) * per_group)) for k in range(count)]
    group_z = [
        jnp.stack([z_blocks[j] for j in group], axis=1).reshape(-1, model_width) for group in groups
    ]
    stats = jnp.stack([vocab_stats(embed, rows) for rows in group_z])
    stats = stats.reshape(count, 3, 2, per_group, own_rows).transpose(1, 0, 3, 2, 4)
    stats = stats.reshape(3, group_size, 2, own_rows)
    bit = 1
    while bit < group_size:
        moved = swap(stats, "blk", bit)
        moved = moved.reshape(3, group_size // (2 * bit), 2, bit, 2, own_rows)[:, :, ::-1]
        stats = join_stats(stats, moved.reshape(stats.shape))
        bit *= 2
    log_total = stats[0] + jnp.log(stats[1])
    expect = stats[2] / stats[1]
    positions = jnp.stack(
        [
            (group_index ^ j) * own_rows + jnp.arange(own_rows, dtype=jnp.int32)
            for j in range(group_size)
        ]
    )
    live = positions < lengths[0]
    labels = jnp.stack(
        [
            lax.dynamic_slice_in_dim(targets[0], (group_index ^ j) * own_rows, own_rows)
            for j in range(group_size)
        ]
    )
    labels = jnp.where(live, labels, -1)
    live = live.astype(jnp.float32)
    row_values = jnp.stack(
        [
            jnp.where(live > 0, log_total[:, 0] * LOG2E, 1e30),
            jnp.where(live > 0, log_total[:, 1] * LOG2E, 1e30),
            2.0 - expect[:, 0],
            2.0 + expect[:, 1],
            live * (1.0 - SMOOTH + SMOOTH / vocab_total),
            live * (SMOOTH / vocab_total),
        ]
    )
    relative = relative_index("batch")
    vocab_base = (group_index * vocab_part).astype(jnp.int32).reshape(1)
    total = None
    grad_z_parts, smooth_parts, embed_chunks = {}, {}, []
    for at in range(count - 1, -1, -1):
        group = groups[at]
        z_t = group_z[at].T
        z_t = pick_parts(z_t.reshape(batch_size, -1, z_t.shape[1]), relative).reshape(z_t.shape)
        at_rows = [group[0], group[-1] + 1]
        part_rows = row_values[:, at_rows[0] : at_rows[1]].reshape(6, -1)
        part_labels = labels[at_rows[0] : at_rows[1]].reshape(1, -1)
        if at > 0:
            total, grad_z, smooth = loss_back(
                vocab_base, embed_pad, embed_t, group_z[at], z_t, part_rows, part_labels,
                (0, padded), total, None, None,
            )
        else:
            grad_z, smooth = None, 0.0
            chunk = max(padded // 4, TILE)
            for low in range(0, padded, chunk):
                grad_embed, grad_z, more = loss_back(
                    vocab_base, embed_pad, embed_t, group_z[at], z_t, part_rows, part_labels,
                    (low, low + chunk), total, grad_z, low + chunk == padded,
                )
                smooth = smooth + more
                grad_embed = grad_embed.reshape(2, batch_size // 2, model_width // batch_size, chunk)
                embed_chunks.append(ring_scatter(grad_embed, "batch", low > 0))
        grad_z = grad_z.reshape(2, per_group, own_rows, model_width)
        smooth = jnp.sum(smooth, axis=0).reshape(per_group, own_rows)
        for k, j in enumerate(group):
            grad_z_parts[j] = grad_z[:, k]
            smooth_parts[j] = smooth[k]
    grad_z_own = scatter_blocks(
        [grad_z_parts[j] for j in range(group_size)], "blk"
    ).astype(jnp.float32)
    smooth_own = scatter_blocks([smooth_parts[j] for j in range(group_size)], "blk")
    own_loss = live[0] * (log_total[0, 0] + log_total[0, 1] + expect[0, 0] - expect[0, 1]) - smooth_own
    embed_sum = jnp.concatenate(embed_chunks, axis=-1)[:, :vocab_part].astype(jnp.float32).T
    grad_outputs, grad_gain_out = norm_back(outputs, gain_out, grad_z_own)
    send_grads = jnp.einsum(
        "psr,prd->psd",
        routing,
        grad_outputs.astype(jnp.bfloat16),
        preferred_element_type=jnp.float32,
    ).astype(jnp.bfloat16)
    send_grads = send_grads.reshape(2, experts_all, capacity, model_width)
    arrived_grads = lax.all_to_all(send_grads, "blk", split_axis=1, concat_axis=1, tiled=True)
    grouped = to_experts(arrived, experts_dev, group_size, capacity, model_width)
    grouped_grads = to_experts(arrived_grads, experts_dev, group_size, capacity, model_width)
    up_values = jnp.einsum("erd,edf->erf", grouped, w_in, preferred_element_type=jnp.float32)
    activity = jax.nn.gelu(up_values).astype(jnp.bfloat16)
    grad_activity = jnp.einsum(
        "erd,efd->erf", grouped_grads, w_out, preferred_element_type=jnp.float32
    )
    _, gelu_pull = jax.vjp(jax.nn.gelu, up_values)
    grad_up = gelu_pull(grad_activity)[0].astype(jnp.bfloat16)
    w_out_local = jnp.einsum(
        "erf,erd->efd", activity, grouped_grads, preferred_element_type=jnp.float32
    )
    w_in_local = jnp.einsum("erd,erf->edf", grouped, grad_up, preferred_element_type=jnp.float32)
    grad_rows = jnp.einsum("erf,edf->erd", grad_up, w_in, preferred_element_type=jnp.float32)
    grad_rows = from_experts(grad_rows, experts_dev, group_size, capacity, model_width)
    back_grads = lax.all_to_all(
        grad_rows.astype(jnp.bfloat16), "blk", split_axis=1, concat_axis=1, tiled=True
    ).astype(grad_rows.dtype)
    grad_h_three = jnp.einsum(
        "psr,psd->rd",
        routing.astype(jnp.float32),
        back_grads.reshape(2, experts_all * capacity, model_width),
    )
    norm_part, grad_gain_ffn = norm_back(after_cross, gain_ffn, grad_h_three)
    grad_after = grad_outputs[0] + grad_outputs[1] + norm_part
    branch_two = grad_after.astype(jnp.bfloat16)
    grad_co = weight_grad(cross_out, branch_two)
    cross_q_low, memkey_part, memval_part = attend_back(
        me, branch_two, co, cross_q, mem_keys, mem_values, cross_log, False
    )
    grad_cq = weight_grad(h_two, cross_q_low)
    grad_ck = weight_grad(memory_all, memkey_part)
    grad_cv = weight_grad(memory_all, memval_part)
    memory_part = (dot(memkey_part, ck, NT) + dot(memval_part, cv, NT)).astype(jnp.bfloat16)
    grad_h_two = dot(cross_q_low, cq, NT)
    norm_part, grad_gain_cross = norm_back(middle, gain_cross, grad_h_two)
    grad_middle = grad_after + norm_part
    branch_one = grad_middle.astype(jnp.bfloat16)
    grad_wo = weight_grad(attn_out, branch_one)
    queries_low, key_part, value_part = attend_back(
        me, branch_one, wo, queries, all_keys, all_values, self_log, True
    )
    grad_wq = weight_grad(h_one, queries_low)
    grad_wk = weight_grad(h_all, key_part)
    grad_wv = weight_grad(h_all, value_part)
    state_part = (dot(key_part, wk, NT) + dot(value_part, wv, NT)).astype(jnp.bfloat16)
    own_part = scatter_blocks(list(state_part.reshape(group_size, own_rows, model_width)), "blk")
    grad_h_one = dot(queries_low, wq, NT) + own_part.astype(jnp.float32)
    grad_memory = scatter_blocks(
        list(memory_part.reshape(group_size, own_rows, model_width)), "blk"
    ).astype(jnp.float32)
    norm_part, grad_gain_self = norm_back(own_states, gain_self, grad_h_one)
    grad_tokens = grad_middle + norm_part
    row_part = model_width // batch_size
    col_part = model_width // group_size

    def sum_weights(weights):
        stacked = jnp.stack([weight.astype(jnp.bfloat16) for weight in weights])
        parts = [
            lax.dynamic_slice_in_dim(stacked, (group_index ^ j) * col_part, col_part, axis=2)
            for j in range(group_size)
        ]
        summed = scatter_blocks(parts, "blk")
        summed = summed.reshape(len(weights), batch_size, row_part, col_part).transpose(1, 0, 2, 3)
        return ring_scatter(pick_parts(summed, relative), "batch", True).astype(jnp.float32)

    cross_sums = sum_weights([grad_cq, grad_ck, grad_cv, grad_co])
    self_sums = sum_weights([grad_wq, grad_wk, grad_wv, grad_wo])
    summed_weights = [self_sums[k] for k in range(4)] + [cross_sums[k] for k in range(4)]
    summed_gains = jnp.stack([grad_gain_self, grad_gain_cross, grad_gain_ffn, grad_gain_out])
    for axis in ("blk", "batch"):
        bit = 1
        while bit < lax.axis_size(axis):
            summed_gains = summed_gains + swap(summed_gains, axis, bit)
            bit *= 2
    w_in_parts = w_in_local[0].astype(jnp.bfloat16).reshape(batch_size, row_part, -1)
    w_in_sum = ring_scatter(pick_parts(w_in_parts, relative), "batch", True).astype(jnp.float32)[None]
    w_out_parts = w_out_local[0].astype(jnp.bfloat16).reshape(batch_size, -1, model_width)
    w_out_sum = ring_scatter(pick_parts(w_out_parts, relative), "batch", True).astype(jnp.float32)[None]
    return (
        own_loss[None],
        grad_tokens[None],
        grad_memory[None],
        summed_gains[0],
        summed_gains[1],
        summed_gains[2],
        summed_gains[3],
        summed_weights[0],
        summed_weights[1],
        summed_weights[2],
        summed_weights[3],
        summed_weights[4],
        summed_weights[5],
        summed_weights[6],
        summed_weights[7],
        w_in_sum,
        w_out_sum,
        embed_sum,
    )


def solution(mesh):
    return jax.shard_map(
        per_device,
        mesh=mesh,
        in_specs=(
            P("batch", "blk", None),
            P("batch", "blk", None),
            P("batch"),
            P("batch", None),
            P(None, "batch", "blk", None),
            P(),
            P(),
            P(),
            P(),
            P(),
            P(),
            P(),
            P(),
            P(),
            P(),
            P(),
            P(),
            P("blk", None, None),
            P("blk", None, None),
            P("blk", None),
        ),
        out_specs=(
            P("batch", "blk"),
            P("batch", "blk", None),
            P("batch", "blk", None),
            P(),
            P(),
            P(),
            P(),
            P("batch", "blk"),
            P("batch", "blk"),
            P("batch", "blk"),
            P("batch", "blk"),
            P("batch", "blk"),
            P("batch", "blk"),
            P("batch", "blk"),
            P("batch", "blk"),
            P("blk", "batch", None),
            P("blk", "batch", None),
            P("blk", "batch"),
        ),
        check_vma=False,
    )
```

```python
import functools

import jax
import jax.numpy as jnp
from jax import lax
from jax.experimental import pallas as pl
from jax.experimental.pallas import tpu as pltpu
from jax.sharding import PartitionSpec as P

HEADS = 8
HD = 64


EPS_NORM = 1e-05
SMOOTH = 0.1
LOG2E = 1.4426950408889634
VMEM_LIMIT = 60 << 20
SMALL = pl.CostEstimate(flops=1000, bytes_accessed=1000, transcendentals=0)
NN = (((1,), (0,)), ((), ()))
NT = (((1,), (1,)), ((), ()))


def dot(left, right, dims):
    return lax.dot_general(left, right, dims, preferred_element_type=jnp.float32)


def swap(value, axis, mask):
    size = lax.axis_size(axis)
    return lax.ppermute(value, axis, [(i, i ^ mask) for i in range(size)])


def gather_blocks(own, axis, *gates):
    size = lax.axis_size(axis)
    blocks = {0: own}
    bit = 2
    while bit < size:
        for k in range(0, bit, 2):
            blocks[bit | k] = swap(blocks[k], axis, bit)
        bit *= 2
    for k in range(0, size, 2):
        if k:
            blocks[k] = after(blocks[k], *gates)
        blocks[k | 1] = swap(blocks[k], axis, 1)
    return [blocks[j] for j in range(size)]


def exchange_blocks(own, axis):
    return [own[0]] + [swap(own[j], axis, j) for j in range(1, len(own))]


def core_stage(parts, axis):
    moved = {j ^ 1: swap(parts[j], axis, 1) for j in sorted(parts) if j % 2}
    return {j: add_low(parts[j], moved[j]) if j else [parts[0], moved[0]] for j in moved}


def far_stage(parts, axis):
    parts = dict(parts)
    terms = list(parts[0])
    size = lax.axis_size(axis)
    bit = 2
    while bit < size:
        odd = list(range(bit, size, 2 * bit))
        moved = swap(jnp.stack([parts[j] for j in odd]) if len(odd) > 1 else parts[bit], axis, bit)
        for k, j in enumerate(odd):
            part = moved[k] if len(odd) > 1 else moved
            if j == bit:
                terms.append(part)
            else:
                parts[j ^ bit] = add_low(parts[j ^ bit], part)
        bit *= 2
    return terms


def scatter_terms(keep, send, axis):
    moved = swap(send, axis, 1)
    parts = {2 * k: add_low(keep[k], moved[k]) for k in range(1, keep.shape[0])}
    parts[0] = [keep[0], moved[0]]
    return far_stage(parts, axis)


def total_of(terms):
    return functools.reduce(add_low, terms)


def add_low(left, right):
    return (left.astype(jnp.float32) + right.astype(jnp.float32)).astype(left.dtype)


def part_device(me, place, size):
    half = size // 2
    return 2 * (place % half) + ((me % 2) ^ (place // half))


def pair_finish(sums, axis, *gates):
    half = sums.shape[0]
    groups = [[2 * k + bit for k in range(half)] for bit in range(2)]
    moved = after(lax.all_to_all(sums, axis, 0, 0, axis_index_groups=groups), *gates)
    return jnp.sum(moved.astype(jnp.float32), axis=0)


def after(value, *others):
    return lax.optimization_barrier((value,) + others)[0]


def stats_kernel(cols, steps, count, blocks, has_earlier, me_ref, embed_ref, *refs):
    z_refs, refs = refs[:blocks], refs[blocks:]
    earlier_ref, refs = (refs[0], refs[1:]) if has_earlier else (None, refs)
    out_ref, rows_ref, turned_ref, max_ref, sum_ref, mix_ref, turn_ref = refs
    step = pl.program_id(0)
    half = rows_ref.shape[0] // 2
    part = rows_ref.shape[1] // count
    size = half // blocks

    @pl.when(step == 0)
    def _():
        max_ref[...] = jnp.full_like(max_ref, -jnp.inf)
        sum_ref[...] = jnp.zeros_like(sum_ref)
        mix_ref[...] = jnp.zeros_like(mix_ref)
        for p in range(2):
            for k, ref in enumerate(z_refs):
                rows_ref[p * half + k * size : p * half + (k + 1) * size, :] = ref[p]
        turn_ref[...] = rows_ref[...].T
        for place in range(count):
            start = pl.multiple_of(part_device(me_ref[0], place, count) * part, part)
            turned_ref[place * part : (place + 1) * part, :] = turn_ref[pl.ds(start, part), :]

    embed = embed_ref[...]
    for col in range(half // cols):
        places = [slice(p * half + col * cols, p * half + (col + 1) * cols) for p in range(2)]
        logits = [dot(embed, rows_ref[place, :], NT).reshape(-1, 8, cols) for place in places]
        apart = logits[0] - logits[1]
        for place, logit in zip(places, logits):
            old = max_ref[:, place]
            new = jnp.maximum(old, jnp.max(logit, axis=0))
            max_ref[:, place] = new
            scale = jnp.exp2((old - new) * LOG2E)
            weights = jnp.exp2((logit - new[None]) * LOG2E)
            sum_ref[:, place] = sum_ref[:, place] * scale + jnp.sum(weights, axis=0)
            mix_ref[:, place] = mix_ref[:, place] * scale + jnp.sum(weights * apart, axis=0)

    @pl.when(step == steps - 1)
    def _():
        top = jnp.max(max_ref[...], axis=0, keepdims=True)
        scale = jnp.exp2((max_ref[...] - top) * LOG2E)
        first = 0
        if has_earlier:
            first = earlier_ref.shape[0]
            out_ref[:first, :] = earlier_ref[...]
        out_ref[first : first + 1, :] = top
        out_ref[first + 1 : first + 2, :] = jnp.sum(sum_ref[...] * scale, axis=0, keepdims=True)
        out_ref[first + 2 : first + 3, :] = jnp.sum(mix_ref[...] * scale, axis=0, keepdims=True)


def row_tile(rows, limit):
    return max(size for size in range(16, limit + 1, 16) if rows % size == 0)


def vocab_stats(me, embed, blocks, count, earlier):
    vocab, width = embed.shape
    rows = sum(block.shape[0] * block.shape[1] for block in blocks)
    tile = row_tile(vocab, 800)
    cols = min(256, rows // 2)
    steps = vocab // tile
    operands = [me, embed, *blocks] + ([] if earlier is None else [earlier])
    shapes = [wide(3 if earlier is None else 3 + earlier.shape[0], rows), low(rows, width), low(width, rows)]
    return pl.pallas_call(
        functools.partial(stats_kernel, cols, steps, count, len(blocks), earlier is not None),
        grid=(steps,),
        in_specs=[
            pl.BlockSpec(memory_space=pltpu.SMEM),
            pl.BlockSpec((tile, width), lambda i: (i, 0)),
        ] + [whole(leaf) for leaf in operands[2:]],
        out_specs=[whole(leaf) for leaf in shapes],
        out_shape=shapes,
        scratch_shapes=[pltpu.VMEM((8, rows), jnp.float32)] * 3
        + [pltpu.VMEM((width, rows), jnp.bfloat16)],
        compiler_params=pltpu.CompilerParams(vmem_limit_bytes=VMEM_LIMIT),
        cost_estimate=SMALL,
    )(*operands)


def rows_kernel(groups, vocab_total, me_ref, length_ref, target_ref, *refs):
    stat_refs, (value_ref, label_ref, loss_ref) = refs[:-3], refs[-3:]
    devices = len(stat_refs)
    per_group = devices // groups
    rows = stat_refs[0].shape[1] // (2 * per_group)

    def stat(device, block, p, kind):
        block = block ^ device
        row = 3 * (block // per_group) + kind
        lane = (p * per_group + block % per_group) * rows
        return stat_refs[device][row : row + 1, lane : lane + rows]

    for block in range(devices):
        group, lane = block // per_group, (block % per_group) * rows
        place = slice(lane, lane + rows)
        start = pl.multiple_of((me_ref[0] ^ block) * rows, rows)
        position = start + lax.broadcasted_iota(jnp.int32, (1, rows), 1)
        live = position < length_ref[0]
        label_ref[group, 0:1, place] = jnp.where(live, target_ref[0:1, pl.ds(start, rows)], -1)
        logs, expects = [], []
        for p in range(2):
            tops = [stat(device, block, p, 0) for device in range(devices)]
            top = functools.reduce(jnp.maximum, tops)
            scales = [jnp.exp2((one - top) * LOG2E) for one in tops]
            total = sum(stat(device, block, p, 1) * scales[device] for device in range(devices))
            mixed = sum(stat(device, block, p, 2) * scales[device] for device in range(devices))
            logs.append(top + jnp.log(total))
            expects.append(mixed / total)
        values = [
            jnp.where(live, logs[0] * LOG2E, 1e30),
            jnp.where(live, logs[1] * LOG2E, 1e30),
            2.0 - expects[0],
            2.0 + expects[1],
            jnp.where(live, 1.0 - SMOOTH + SMOOTH / vocab_total, 0.0),
            jnp.where(live, SMOOTH / vocab_total, 0.0),
        ]
        for k, value in enumerate(values):
            value_ref[group, k : k + 1, place] = value
        if block == 0:
            loss_ref[...] = jnp.where(live, logs[0] + logs[1] + expects[0] - expects[1], 0.0)


def padded_kernel(count, embed_ref, pad_ref, turned_ref):
    start = pl.program_id(0) * embed_ref.shape[0]
    rows = lax.broadcasted_iota(jnp.int32, embed_ref.shape, 0) + start
    values = jnp.where(rows < count, embed_ref[...], jnp.zeros_like(embed_ref[...]))
    pad_ref[...] = values
    turned_ref[...] = values.T


def padded_embed(embed, padded):
    count, width = embed.shape
    return pl.pallas_call(
        functools.partial(padded_kernel, count),
        grid=(padded // TILE,),
        in_specs=[pl.BlockSpec((TILE, width), lambda i: (i, 0))],
        out_specs=[
            pl.BlockSpec((TILE, width), lambda i: (i, 0)),
            pl.BlockSpec((width, TILE), lambda i: (0, i)),
        ],
        out_shape=[
            jax.ShapeDtypeStruct((padded, width), embed.dtype),
            jax.ShapeDtypeStruct((width, padded), embed.dtype),
        ],
        compiler_params=pltpu.CompilerParams(vmem_limit_bytes=VMEM_LIMIT),
        cost_estimate=SMALL,
    )(embed)


def loss_back_kernel(cols, steps, groups, has_total, has_carry, pieces, last, *refs):
    count = len(groups)
    base_ref, embed_ref, embed_t_ref = refs[:3]
    z_refs, z_t_refs, refs = refs[3 : 3 + count], refs[3 + count : 3 + 2 * count], refs[3 + 2 * count :]
    (row_ref, label_ref), refs = refs[:2], list(refs[2:])
    total_ref = refs.pop(0) if has_total else None
    carry_ref = refs.pop(0) if has_carry else None
    loss_ref, grad_ref, sum_ref = refs[-3:]
    embed_refs, out_refs = refs[:pieces], refs[pieces:-3]
    step = pl.program_id(0)
    rows = z_refs[0].shape[0]
    half = rows // 2
    tile = embed_ref.shape[0]

    @pl.when(step == 0)
    def _():
        sum_ref[...] = carry_ref[...] if has_carry else jnp.zeros_like(sum_ref)
        loss_ref[...] = jnp.zeros_like(loss_ref)

    embed = embed_ref[...]
    ids = lax.broadcasted_iota(jnp.int32, (tile // 8, 8, cols), 0) * 8
    ids = ids + lax.broadcasted_iota(jnp.int32, (tile // 8, 8, cols), 1)
    base = base_ref[0] + step * tile
    for k, group in enumerate(groups):
        for col in range(half // cols):
            one = slice(col * cols, (col + 1) * cols)
            two = slice(half + col * cols, half + (col + 1) * cols)
            logit_one = dot(embed, z_refs[k][one, :], NT).reshape(-1, 8, cols)
            logit_two = dot(embed, z_refs[k][two, :], NT).reshape(-1, 8, cols)
            row = [row_ref[group, v : v + 1, one].reshape(1, 1, cols) for v in range(6)]
            prob_one = jnp.exp2(logit_one * LOG2E - row[0])
            prob_two = jnp.exp2(logit_two * LOG2E - row[1])
            apart = logit_one - logit_two
            hits = ids == (label_ref[group, 0:1, one] - base).reshape(1, 1, cols)
            smooth = jnp.where(hits, row[4], row[5])
            grad_one = prob_one * (apart + row[2]) - (prob_two + smooth)
            grad_two = prob_two * (row[3] - apart) - (prob_one + smooth)
            loss_ref[k, :, one] += jnp.sum(smooth * (logit_one + logit_two), axis=0)
            lane = k * rows + col * cols
            grad_ref[:, lane : lane + cols] = grad_one.reshape(tile, cols).astype(jnp.bfloat16)
            grad_ref[:, lane + half : lane + half + cols] = grad_two.reshape(tile, cols).astype(jnp.bfloat16)
    grad_embed = total_ref[...].astype(jnp.float32) if has_total else 0.0
    for k in range(count):
        place = slice(k * rows, (k + 1) * rows)
        grad_embed = grad_embed + dot(z_t_refs[k][...], grad_ref[:, place], NT)
        sum_ref[:, place] += dot(embed_t_ref[...], grad_ref[:, place], NN)
    grad_embed = grad_embed.astype(jnp.bfloat16)
    part = grad_embed.shape[0] // len(embed_refs)
    for k, ref in enumerate(embed_refs):
        ref[...] = grad_embed[k * part : (k + 1) * part]

    @pl.when(step == steps - 1)
    def _():
        if not last:
            out_refs[0][...] = sum_ref[...]
        else:
            size = half * count // len(out_refs)
            per_group = len(out_refs) // count
            for k, ref in enumerate(out_refs):
                for p in range(2):
                    lane = k // per_group * rows + p * half + k % per_group * size
                    ref[p] = sum_ref[:, lane : lane + size].T.astype(ref.dtype)


def loss_back(base, embed, embed_t, z_rows, z_t, row_values, labels, groups, span, total, carry, pieces, last):
    width = embed.shape[1]
    count = len(groups)
    rows = z_rows[0].shape[0]
    tile = TILE
    start, end = span
    steps, first = (end - start) // tile, start // tile
    cols = min(256, rows // 2)
    operands = [base + start, embed, embed_t, *z_rows, *z_t, row_values, labels]
    vmem = pl.BlockSpec(memory_space=pltpu.VMEM)
    specs = [
        pl.BlockSpec(memory_space=pltpu.SMEM),
        pl.BlockSpec((tile, width), lambda i: (i + first, 0)),
        pl.BlockSpec((width, tile), lambda i: (0, i + first)),
    ] + [vmem] * (2 * count + 2)
    if total is not None:
        operands.append(total)
        specs.append(pl.BlockSpec((width, tile), lambda i: (0, i + first)))
    if carry is not None:
        operands.append(carry)
        specs.append(vmem)
    piece = width // pieces
    grad_z = [low(2, rows * count // 2 // last, width)] * last if last else [wide(width, rows * count)]
    return pl.pallas_call(
        functools.partial(
            loss_back_kernel, cols, steps, groups, total is not None, carry is not None, pieces, last
        ),
        grid=(steps,),
        in_specs=specs,
        out_specs=[pl.BlockSpec((piece, tile), lambda i: (0, i))] * pieces + [vmem] * (len(grad_z) + 1),
        out_shape=[low(piece, end - start)] * pieces + grad_z + [wide(count, 8, rows // 2)],
        scratch_shapes=[
            pltpu.VMEM((tile, rows * count), jnp.bfloat16),
            pltpu.VMEM((width, rows * count), jnp.float32),
        ],
        compiler_params=pltpu.CompilerParams(vmem_limit_bytes=VMEM_LIMIT),
        cost_estimate=SMALL,
    )(*operands)


TILE = 1024


SCALE = HD ** (-0.5)


def head_lanes(pair, head):
    lanes = lax.broadcasted_iota(jnp.int32, pair.shape, 1)
    return jnp.where((lanes >= HD) == (head % 2 == 1), pair, jnp.zeros_like(pair))


def block_bias(me, rows, blocks, causal):
    if not causal:
        return [None] * blocks
    keys = lax.broadcasted_iota(jnp.int32, (rows, rows), 0)
    queries = lax.broadcasted_iota(jnp.int32, (rows, rows), 1)
    biases = [jnp.where(keys <= queries, 0.0, -1e30)]
    for block in range(1, blocks):
        biases.append(jnp.where((me ^ block) < me, 0.0, -1e30))
    return biases


def head_weights(keys, query, biases, rows):
    scores = []
    for block, bias in enumerate(biases):
        part = dot(keys[block * rows : (block + 1) * rows], query, NT)
        scores.append(part if bias is None else part + bias)
    return scores


def normed(values, gain):
    center = values - jnp.mean(values, axis=-1, keepdims=True)
    spread = jnp.mean(center * center, axis=-1, keepdims=True)
    return center * lax.rsqrt(spread + EPS_NORM) * gain


def normed_back(values, gain, upstream):
    center = values - jnp.mean(values, axis=-1, keepdims=True)
    spread = jnp.mean(center * center, axis=-1, keepdims=True)
    scale = lax.rsqrt(spread + EPS_NORM)
    unit = center * scale
    grad_gain = jnp.sum(upstream * unit, axis=0, keepdims=True)
    up = upstream * gain
    mean_up = jnp.mean(up, axis=-1, keepdims=True)
    mean_mix = jnp.mean(up * unit, axis=-1, keepdims=True)
    return scale * (up - mean_up - unit * mean_mix), grad_gain


def slot_rows(place_ref, count, passes):
    rows = place_ref.shape[1]
    slots = lax.broadcasted_iota(jnp.int32, (count, rows), 0)
    hits = functools.reduce(jnp.logical_or, [slots == place_ref[p : p + 1, :] for p in passes])
    return jnp.where(hits, 1.0, 0.0).astype(jnp.bfloat16)


def token_rows(place_ref, count, passes):
    rows = place_ref.shape[0]
    slots = lax.broadcasted_iota(jnp.int32, (rows, count), 1)
    hits = functools.reduce(jnp.logical_or, [slots == place_ref[:, p : p + 1] for p in passes])
    return jnp.where(hits, 1.0, 0.0).astype(jnp.bfloat16)


def attend_kernel(blocks, causal, *refs):
    me_ref, refs = refs[0], refs[1:]
    block_refs, refs = refs[:blocks], refs[blocks:]
    if causal:
        (first_gain_ref, gain_ref, wq_ref, wk_ref, wv_ref, wo_ref), refs = refs[:6], refs[6:]
        slot_refs = ()
    else:
        (source_ref, residual_ref, place_ref, gain_ref, wq_ref, wk_ref, wv_ref, wo_ref), refs = (
            refs[:8],
            refs[8:],
        )
        slot_refs, refs = refs[:blocks], refs[blocks:]
    (query_ref, key_ref, value_ref, all_ref, out_ref, log_ref, sum_ref, next_ref,
     value_t_ref, out_t_ref) = refs
    rows = block_refs[0].shape[0]
    for block, ref in enumerate(block_refs):
        part = ref[...]
        if causal:
            part = normed(part.astype(jnp.float32), first_gain_ref[...]).astype(jnp.bfloat16)
        all_ref[block * rows : (block + 1) * rows, :] = part
    source = all_ref[:rows, :] if causal else source_ref[...]
    residual = block_refs[0][...].astype(jnp.float32) if causal else residual_ref[...]
    query_ref[...] = dot(source, wq_ref[...], NN).astype(jnp.bfloat16)
    key_ref[...] = dot(all_ref[...], wk_ref[...], NN).astype(jnp.bfloat16)
    values = dot(all_ref[...], wv_ref[...], NN).astype(jnp.bfloat16)
    value_ref[...] = values
    value_t_ref[...] = values.T
    biases = block_bias(me_ref[0], rows, blocks, causal)
    factor = SCALE * LOG2E
    for head in range(HEADS):
        lanes = slice(head // 2 * 128, head // 2 * 128 + 128)
        query = head_lanes(query_ref[:, lanes], head)
        scores = head_weights(key_ref[:, lanes], query, biases, rows)
        top = functools.reduce(
            jnp.maximum, [jnp.max(part.reshape(-1, 8, rows), axis=0) for part in scores]
        )
        top = jnp.max(top, axis=0, keepdims=True) * factor
        weights = [jnp.exp2(part * factor - top) for part in scores]
        total = sum(jnp.sum(part.reshape(-1, 8, rows), axis=0) for part in weights)
        total = jnp.sum(total, axis=0, keepdims=True)
        log_ref[head : head + 1, :] = top + jnp.log2(total)
        weights = jnp.concatenate([part.astype(jnp.bfloat16) for part in weights], axis=0)
        place = slice(head * HD, (head + 1) * HD)
        out_t_ref[place, :] = dot(value_t_ref[place, :], weights, NN) / total
    out = out_t_ref[...].T.astype(jnp.bfloat16)
    out_ref[...] = out
    states = residual + dot(out, wo_ref[...], NN)
    sum_ref[...] = states
    following = normed(states, gain_ref[...]).astype(jnp.bfloat16)
    next_ref[...] = following
    if slot_refs:
        count = slot_refs[0].shape[0]
        sends = dot(slot_rows(place_ref, blocks * count, (0, 1)), following, NN).astype(jnp.bfloat16)
        for block, ref in enumerate(slot_refs):
            ref[...] = sends[block * count : (block + 1) * count]


def low(*shape):
    return jax.ShapeDtypeStruct(shape, jnp.bfloat16)


def wide(*shape):
    return jax.ShapeDtypeStruct(shape, jnp.float32)


def attend(me, blocks, weights, gains, slots, source=None, residual=None, place=None):
    rows, width = blocks[0].shape
    count = rows * len(blocks)
    causal = source is None
    operands = [me, *blocks]
    if not causal:
        operands += [source, residual, place]
    operands += [gain[None] for gain in gains] + list(weights)
    shapes = [low(slots, width)] * (0 if causal else len(blocks)) + [
        low(rows, width), low(count, width), low(count, width), low(count, width),
        low(rows, width), wide(HEADS, rows), wide(rows, width), low(rows, width),
    ]
    return pl.pallas_call(
        functools.partial(attend_kernel, len(blocks), causal),
        grid=(1,),
        in_specs=[pl.BlockSpec(memory_space=pltpu.SMEM)] + [whole(leaf) for leaf in operands[1:]],
        out_specs=[whole(leaf) for leaf in shapes],
        out_shape=shapes,
        scratch_shapes=[pltpu.VMEM((width, count), jnp.bfloat16), pltpu.VMEM((width, rows), jnp.float32)],
        compiler_params=pltpu.CompilerParams(vmem_limit_bytes=VMEM_LIMIT),
        cost_estimate=SMALL,
    )(*operands)


def attend_back_core(causal, me_ref, branch, wo_ref, query_ref, key_ref, value_ref, log_ref,
                     grad_query_ref, grad_key_ref, grad_value_ref, key_t_ref, up_ref, query_t_ref):
    rows = query_ref.shape[0]
    blocks = key_ref.shape[0] // rows
    up_ref[...] = dot(branch, wo_ref[...], NT).astype(jnp.bfloat16)
    key_t_ref[...] = key_ref[...].T
    biases = block_bias(me_ref[0], rows, blocks, causal)
    factor = SCALE * LOG2E
    for pair in range(HEADS // 2):
        lanes = slice(pair * 128, pair * 128 + 128)
        grad_keys, grad_values = 0.0, 0.0
        for head in (2 * pair, 2 * pair + 1):
            query = head_lanes(query_ref[:, lanes], head)
            upstream = head_lanes(up_ref[:, lanes], head)
            log_total = log_ref[head : head + 1, :]
            scores = head_weights(key_ref[:, lanes], query, biases, rows)
            probs = jnp.concatenate([jnp.exp2(part * factor - log_total) for part in scores], axis=0)
            grad_probs = dot(value_ref[:, lanes], upstream, NT)
            inner = jnp.sum((probs * grad_probs).reshape(-1, 8, rows), axis=0)
            inner = jnp.sum(inner, axis=0, keepdims=True)
            grad_scores = (probs * (grad_probs - inner)).astype(jnp.bfloat16)
            grad_values = grad_values + dot(probs.astype(jnp.bfloat16), upstream, NN)
            grad_keys = grad_keys + dot(grad_scores, query, NN)
            place = slice(head * HD, (head + 1) * HD)
            query_t_ref[place, :] = dot(key_t_ref[place, :], grad_scores, NN) * SCALE
        grad_value_ref[:, lanes] = grad_values.astype(jnp.bfloat16)
        grad_key_ref[:, lanes] = (grad_keys * SCALE).astype(jnp.bfloat16)
    grad_query_ref[...] = query_t_ref[...].T.astype(jnp.bfloat16)


def cross_back_kernel(blocks, *refs):
    me_ref, back_refs, refs = refs[0], refs[1 : 1 + blocks], refs[1 + blocks :]
    (place_ref, after_ref, gain_ffn_ref, grad_sum_ref, middle_ref, gain_cross_ref, wo_ref, wq_ref,
     query_ref, key_ref, value_ref, log_ref), refs = refs[:12], refs[12:]
    (branch_ref, middle_grad_ref, gains_ref, grad_query_ref, grad_key_ref, grad_value_ref,
     key_t_ref, up_ref, query_t_ref) = refs
    back = jnp.concatenate([ref[...] for ref in back_refs], axis=0)
    grad_normed = dot(token_rows(place_ref, back.shape[0], (0, 1)), back, NN)
    grad_after, gains_ref[0:1, :] = normed_back(after_ref[...], gain_ffn_ref[...], grad_normed)
    grad_after = grad_after + grad_sum_ref[...]
    branch = grad_after.astype(jnp.bfloat16)
    branch_ref[...] = branch
    attend_back_core(False, me_ref, branch, wo_ref, query_ref, key_ref, value_ref, log_ref,
                     grad_query_ref, grad_key_ref, grad_value_ref, key_t_ref, up_ref, query_t_ref)
    grad_normed = dot(grad_query_ref[...], wq_ref[...], NT)
    grad_middle, gains_ref[1:2, :] = normed_back(middle_ref[...], gain_cross_ref[...], grad_normed)
    middle_grad_ref[...] = grad_middle + grad_after


def self_back_kernel(me_ref, middle_grad_ref, wo_ref, wq_ref, wk_ref, wv_ref,
                     query_ref, key_ref, value_ref, log_ref,
                     keep_ref, send_ref, own_ref, grad_query_ref, grad_key_ref, grad_value_ref,
                     key_t_ref, up_ref, query_t_ref):
    rows = query_ref.shape[0]
    branch = middle_grad_ref[...].astype(jnp.bfloat16)
    attend_back_core(True, me_ref, branch, wo_ref, query_ref, key_ref, value_ref, log_ref,
                     grad_query_ref, grad_key_ref, grad_value_ref, key_t_ref, up_ref, query_t_ref)
    for block in range(key_ref.shape[0] // rows):
        place = slice(block * rows, (block + 1) * rows)
        part = dot(grad_key_ref[place, :], wk_ref[...], NT) + dot(grad_value_ref[place, :], wv_ref[...], NT)
        target = send_ref if block % 2 else keep_ref
        target[block // 2] = part.astype(jnp.bfloat16)
    own_ref[...] = dot(grad_query_ref[...], wq_ref[...], NT)


def back_call(kernel, operands, shapes, rows, count, width):
    return pl.pallas_call(
        kernel,
        grid=(1,),
        in_specs=[pl.BlockSpec(memory_space=pltpu.SMEM)] + [whole(leaf) for leaf in operands[1:]],
        out_specs=[whole(leaf) for leaf in shapes],
        out_shape=shapes,
        scratch_shapes=[
            pltpu.VMEM((width, count), jnp.bfloat16),
            pltpu.VMEM((rows, width), jnp.bfloat16),
            pltpu.VMEM((width, rows), jnp.float32),
        ],
        compiler_params=pltpu.CompilerParams(vmem_limit_bytes=VMEM_LIMIT),
        cost_estimate=SMALL,
    )(*operands)


def whole(leaf):
    rank = len(leaf.shape)
    return pl.BlockSpec(leaf.shape, lambda *_: (0,) * rank)


def plain_call(kernel, operands, shapes, flops, scratch=(), scalars=1):
    size = sum(leaf.size * leaf.dtype.itemsize for leaf in list(operands) + list(shapes))
    return pl.pallas_call(
        kernel,
        grid=(1,),
        in_specs=[pl.BlockSpec(memory_space=pltpu.SMEM)] * scalars
        + [whole(leaf) for leaf in operands[scalars:]],
        out_specs=[whole(leaf) for leaf in shapes],
        out_shape=shapes,
        scratch_shapes=list(scratch),
        compiler_params=pltpu.CompilerParams(vmem_limit_bytes=48 << 20),
        cost_estimate=SMALL,
    )(*operands)


def weights_kernel(pairs, targets, *refs):
    group_me_ref, batch_me_ref, refs = refs[0], refs[1], refs[2:]
    operand_refs, (keep_ref, send_ref, product_ref) = refs[: 2 * pairs], refs[2 * pairs :]
    groups, batches = targets
    width = product_ref.shape[0]
    row_part, col_part = width // batches, width // groups
    for pair in range(pairs):
        left, right = operand_refs[2 * pair][...], operand_refs[2 * pair + 1][...]
        if left.dtype != jnp.bfloat16:
            left = left.astype(jnp.bfloat16)
        if right.dtype != jnp.bfloat16:
            right = right.astype(jnp.bfloat16)
        product_ref[...] = dot(left.T, right, NN)
        for block in range(groups):
            target = send_ref if block % 2 else keep_ref
            at = group_me_ref[0] ^ block
            for spot in range(batches):
                row = pl.multiple_of(part_device(batch_me_ref[0], spot, batches) * row_part, row_part)
                if col_part % 128 == 0:
                    col = pl.multiple_of(at * col_part, 128)
                    part = product_ref[pl.ds(row, row_part), pl.ds(col, col_part)]
                else:
                    strip = product_ref[pl.ds(row, row_part), :]
                    part = functools.reduce(
                        lambda total, c: jnp.where(
                            at == c, strip[:, c * col_part : (c + 1) * col_part], total
                        ),
                        range(1, groups),
                        strip[:, :col_part],
                    )
                target[block // 2, spot, pair] = part.astype(jnp.bfloat16)


def weight_parts(group_me, batch_me, pairs, groups, batches):
    width = pairs[0][0].shape[1]
    operands = [group_me, batch_me] + [leaf for pair in pairs for leaf in pair]
    shape = low(groups // 2, batches, len(pairs), width // batches, width // groups)
    flops = sum(2 * pair[0].shape[0] * width * width for pair in pairs)
    return plain_call(
        functools.partial(weights_kernel, len(pairs), (groups, batches)),
        operands, [shape, shape], flops, [pltpu.VMEM((width, width), jnp.float32)], 2,
    )


def expert_kernel(parts, steps, w_in_ref, w_out_ref, *refs):
    row_refs, out_refs, (rows_ref, total_ref) = refs[:parts], refs[parts : 2 * parts], refs[2 * parts :]
    step = pl.program_id(0)
    size = row_refs[0].shape[0]

    @pl.when(step == 0)
    def _():
        for k, ref in enumerate(row_refs):
            rows_ref[k * size : (k + 1) * size, :] = ref[...]
        total_ref[...] = jnp.zeros_like(total_ref)

    activity = jax.nn.gelu(dot(rows_ref[...], w_in_ref[...], NN)).astype(jnp.bfloat16)
    total_ref[...] += dot(activity, w_out_ref[...], NN)

    @pl.when(step == steps - 1)
    def _():
        for k, ref in enumerate(out_refs):
            ref[...] = total_ref[k * size : (k + 1) * size, :].astype(jnp.bfloat16)


def expert_rows(parts, w_in, w_out):
    size, width = parts[0].shape
    hidden = w_in.shape[1]
    tile = min(512, hidden)
    rows = size * len(parts)
    return pl.pallas_call(
        functools.partial(expert_kernel, len(parts), hidden // tile),
        grid=(hidden // tile,),
        in_specs=[
            pl.BlockSpec((width, tile), lambda i: (0, i)),
            pl.BlockSpec((tile, width), lambda i: (i, 0)),
        ] + [whole(leaf) for leaf in parts],
        out_specs=[whole(leaf) for leaf in parts],
        out_shape=[low(size, width)] * len(parts),
        scratch_shapes=[pltpu.VMEM((rows, width), jnp.bfloat16), pltpu.VMEM((rows, width), jnp.float32)],
        compiler_params=pltpu.CompilerParams(vmem_limit_bytes=40 << 20),
        cost_estimate=SMALL,
    )(w_in, w_out, *parts)


def expert_back_kernel(parts, steps, batch_me_ref, w_in_ref, w_in_t_ref, w_out_ref, *refs):
    row_refs, grad_refs, refs = refs[:parts], refs[parts : 2 * parts], refs[2 * parts :]
    out_refs, refs = refs[:parts], refs[parts:]
    in_keep_ref, in_send_ref, out_keep_ref, out_send_ref, rows_ref, turned_ref, grads_ref, total_ref = refs
    step = pl.program_id(0)
    size = row_refs[0].shape[0]
    half = steps // 2
    part = turned_ref.shape[0] // steps

    @pl.when(step == 0)
    def _():
        for k in range(parts):
            rows_ref[k * size : (k + 1) * size, :] = row_refs[k][...]
            grads_ref[k * size : (k + 1) * size, :] = grad_refs[k][...]
        total_ref[...] = rows_ref[...].T.astype(jnp.float32)
        for place in range(steps):
            start = pl.multiple_of(part_device(batch_me_ref[0], place, steps) * part, part)
            turned_ref[place * part : (place + 1) * part, :] = total_ref[pl.ds(start, part), :].astype(
                jnp.bfloat16
            )
        total_ref[...] = jnp.zeros_like(total_ref)

    up = dot(w_in_t_ref[...], rows_ref[...], NT)
    inner = 0.7978845608028654 * (up + 0.044715 * up * up * up)
    curve = jnp.tanh(inner)
    activity = (0.5 * up * (1.0 + curve)).astype(jnp.bfloat16)
    slope = 0.5 * (1.0 + curve) + 0.5 * up * (1.0 - curve * curve) * 0.7978845608028654 * (
        1.0 + 3.0 * 0.044715 * up * up
    )
    grad_up = (dot(w_out_ref[...], grads_ref[...], NT) * slope).astype(jnp.bfloat16)
    grad_out = dot(activity, grads_ref[...], NN).astype(jnp.bfloat16)

    @pl.when(step < half)
    def _():
        out_keep_ref[...] = grad_out

    @pl.when(step >= half)
    def _():
        out_send_ref[...] = grad_out

    grad_in = dot(turned_ref[...], grad_up, NT).astype(jnp.bfloat16)
    in_keep_ref[...] = grad_in[: half * part]
    in_send_ref[...] = grad_in[half * part :]
    total_ref[...] += dot(w_in_ref[...], grad_up, NN)

    @pl.when(step == steps - 1)
    def _():
        for k, ref in enumerate(out_refs):
            ref[...] = total_ref[:, k * size : (k + 1) * size].T.astype(jnp.bfloat16)


def expert_back(batch_me, rows, grads, w_in, w_in_t, w_out, batches):
    size, width = rows[0].shape
    count = len(rows)
    hidden = w_in.shape[1]
    tile = hidden // batches
    half = batches // 2
    total = size * count

    def unit(i, me_ref):
        return part_device(me_ref[0], i, batches)

    wide_in = lambda: pl.BlockSpec((half * (width // batches), tile), lambda i, me_ref: (0, unit(i, me_ref)))
    return pl.pallas_call(
        functools.partial(expert_back_kernel, count, batches),
        grid_spec=pltpu.PrefetchScalarGridSpec(
            num_scalar_prefetch=1,
            grid=(batches,),
            in_specs=[
                pl.BlockSpec((width, tile), lambda i, me_ref: (0, unit(i, me_ref))),
                pl.BlockSpec((tile, width), lambda i, me_ref: (unit(i, me_ref), 0)),
                pl.BlockSpec((tile, width), lambda i, me_ref: (unit(i, me_ref), 0)),
            ] + [whole(leaf) for leaf in list(rows) + list(grads)],
            out_specs=[whole(leaf) for leaf in rows] + [
                wide_in(),
                wide_in(),
                pl.BlockSpec((tile, width), lambda i, me_ref: (jnp.minimum(i, half - 1), 0)),
                pl.BlockSpec((tile, width), lambda i, me_ref: (jnp.maximum(i - half, 0), 0)),
            ],
            scratch_shapes=[
                pltpu.VMEM((total, width), jnp.bfloat16),
                pltpu.VMEM((width, total), jnp.bfloat16),
                pltpu.VMEM((total, width), jnp.bfloat16),
                pltpu.VMEM((width, total), jnp.float32),
            ],
        ),
        out_shape=[low(size, width)] * count
        + [low(width // 2, hidden)] * 2
        + [low(hidden // 2, width)] * 2,
        compiler_params=pltpu.CompilerParams(vmem_limit_bytes=VMEM_LIMIT),
        cost_estimate=SMALL,
    )(batch_me, w_in, w_in_t, w_out, *rows, *grads)


def combine_kernel(parts, *refs):
    back_refs, (place_ref, after_ref, gain_ref, out_ref, z_ref) = refs[:parts], refs[parts:]
    back = jnp.concatenate([ref[...] for ref in back_refs], axis=0)
    for p in range(2):
        states = after_ref[...] + dot(token_rows(place_ref, back.shape[0], (p,)), back, NN)
        out_ref[p] = states
        z_ref[p] = normed(states, gain_ref[...]).astype(jnp.bfloat16)


def out_back_kernel(sources, *refs):
    grad_refs, (out_ref, gain_ref, place_ref), refs = refs[:sources], refs[sources : sources + 3], refs[sources + 3 :]
    slot_refs, (sum_ref, gain_grad_ref) = refs[:-2], refs[-2:]
    count = len(slot_refs) * slot_refs[0].shape[0]
    grads, gain_grad, slots = 0.0, 0.0, 0.0
    for p in range(2):
        upstream = sum(ref[p].astype(jnp.float32) for ref in grad_refs)
        grad, more = normed_back(out_ref[p], gain_ref[...], upstream)
        grads, gain_grad = grads + grad, gain_grad + more
        slots = slots + dot(slot_rows(place_ref, count, (p,)), grad.astype(jnp.bfloat16), NN)
    sum_ref[...] = grads
    gain_grad_ref[...] = gain_grad
    size = slot_refs[0].shape[0]
    for k, ref in enumerate(slot_refs):
        ref[...] = slots[k * size : (k + 1) * size].astype(jnp.bfloat16)


def token_back_kernel(sources, *refs):
    grad_refs, (own_ref, states_ref, gain_ref, middle_ref, out_ref, gain_grad_ref) = (
        refs[:sources],
        refs[sources:],
    )
    upstream = own_ref[...] + sum(ref[...].astype(jnp.float32) for ref in grad_refs)
    grad, gain_grad_ref[...] = normed_back(states_ref[...].astype(jnp.float32), gain_ref[...], upstream)
    out_ref[...] = grad + middle_ref[...]


def per_device(
    tokens,
    memory,
    lengths,
    targets,
    expert_ids,
    gain_self,
    gain_cross,
    gain_ffn,
    gain_out,
    wq,
    wk,
    wv,
    wo,
    cq,
    ck,
    cv,
    co,
    w_in,
    w_out,
    embed,
):
    group_index = lax.axis_index("blk")
    group_size = lax.axis_size("blk")
    batch_size = lax.axis_size("batch")
    own_rows, model_width = tokens.shape[1:]
    me = group_index.astype(jnp.int32).reshape(1)
    batch_me = lax.axis_index("batch").astype(jnp.int32).reshape(1)
    capacity = 3 * own_rows // (2 * group_size)
    w_in, w_out = w_in[0], w_out[0]

    vocab_part = embed.shape[0]
    padded = -(-vocab_part // TILE) * TILE
    embed_pad, embed_t = padded_embed(embed, padded)
    token_blocks = gather_blocks(tokens[0], "blk", embed_t)
    memory_blocks = gather_blocks(memory[0], "blk")
    picks = expert_ids[:, 0, :, 0]
    onehot = (picks[:, :, None] == jnp.arange(group_size, dtype=jnp.int32)).astype(jnp.int32)
    slot = jnp.sum(onehot * (jnp.cumsum(onehot, axis=1) - onehot), axis=-1)
    place = ((picks ^ group_index) * 2 + jnp.arange(2, dtype=jnp.int32)[:, None]) * capacity + slot
    place_t = place.T

    queries, all_keys, all_values, h_all, attn_out, self_log, middle, h_two = attend(
        me, token_blocks, (wq, wk, wv, wo), (gain_self, gain_cross), 0
    )
    *sends, cross_q, mem_keys, mem_values, memory_all, cross_out, cross_log, after_cross, _ = attend(
        me, memory_blocks, (cq, ck, cv, co), (gain_ffn,), 2 * capacity, h_two, middle, place
    )
    arrived = exchange_blocks(sends, "blk")
    results = expert_rows(arrived[:2], w_in, w_out)
    if group_size > 2:
        results = list(results) + list(expert_rows(arrived[2:], w_in, w_out))
    returned = exchange_blocks(results, "blk")
    outputs, z_pair = plain_call(
        functools.partial(combine_kernel, group_size),
        [*returned, place_t, after_cross, gain_out[None]],
        [wide(2, own_rows, model_width), low(2, own_rows, model_width)],
        8 * group_size * capacity * own_rows * model_width, (), 0,
    )

    near_z = [z_pair, swap(z_pair, "blk", 1)]
    far_z = {bit: swap(z_pair, "blk", bit) for bit in (1 << k for k in range(1, group_size.bit_length() - 1))}
    count = max(2, group_size * own_rows // 1024)
    per_group = group_size // count
    groups = [list(range(k * per_group, (k + 1) * per_group)) for k in range(count)]
    stats, group_z, group_z_t = None, [], []
    z_blocks = dict(enumerate(near_z))
    if per_group > 2:
        z_blocks = dict(enumerate(gather_blocks(z_pair, "blk")))
    for number, group in enumerate(groups):
        if number and 2 not in z_blocks:
            z_blocks[2] = after(far_z[2], stats)
            z_blocks[3] = swap(z_blocks[2], "blk", 1)
        stats, rows, rows_t = vocab_stats(
            batch_me, embed, [z_blocks[j] for j in group], batch_size, stats
        )
        group_z.append(rows)
        group_z_t.append(rows_t)
    all_stats = [stats] + [swap(stats, "blk", j) for j in range(1, group_size)]
    row_values, labels, own_terms = plain_call(
        functools.partial(rows_kernel, count, vocab_part * group_size),
        [me, lengths, targets, *all_stats],
        [
            wide(count, 6, per_group * own_rows),
            jax.ShapeDtypeStruct((count, 1, per_group * own_rows), jnp.int32),
            wide(1, own_rows),
        ],
        0, (), 2,
    )
    vocab_base = me * vocab_part
    total = None
    sums, smooth_parts, chunks, chunk_sums, finished = {}, {}, [], [], []
    joined = max(1, min(count, 1024 // (per_group * own_rows)))
    for at in range(count - joined, -1, -joined):
        mine = range(at, at + joined)
        operands = (
            vocab_base, embed_pad, embed_t, group_z[at : at + joined], group_z_t[at : at + joined],
            row_values, labels, tuple(mine),
        )
        if at > 0:
            total, *grad_z, smooth = loss_back(
                *operands, (0, padded), total, None, 1, joined * per_group
            )
        else:
            carry, smooth = None, 0.0
            tiles = padded // TILE
            cuts = [0, tiles // 4, 5 * tiles // 8, tiles] if tiles >= 8 else [0, tiles]
            for number in range(len(cuts) - 1):
                start, end = cuts[number] * TILE, cuts[number + 1] * TILE
                done = end == padded
                if done and number > 1:
                    chunk_sums.append(add_low(*chunks[0]))
                    carry = after(carry, chunk_sums[0])
                keep, send, *grad_z, more = loss_back(
                    *operands, (start, end), total, carry, 2, joined * per_group if done else 0
                )
                carry = grad_z[0]
                smooth = smooth + more
                shape = (batch_size // 2, model_width // batch_size, end - start)
                chunks.append((keep.reshape(shape), swap(send.reshape(shape), "batch", 1)))
        held = [j for group in mine for j in groups[group]]
        if len(chunk_sums) == 1:
            finished.append(pair_finish(chunk_sums[0], "batch", grad_z[0]))
            grad_z[0] = after(grad_z[0], finished[0])
        sums.update(core_stage(dict(zip(held, grad_z)), "blk"))
        smooth = jnp.sum(smooth, axis=1).reshape(joined * per_group, own_rows)
        for k, j in enumerate(held):
            smooth_parts[j] = smooth[k]
    for keep, moved in chunks[len(chunk_sums) : 2]:
        chunk_sums.append(add_low(keep, after(moved, *chunk_sums[-1:])))
    grad_z_terms = far_stage(sums, "blk")
    grad_z_terms[0] = after(grad_z_terms[0], *chunk_sums[:2])
    *send_grads, grad_sum, grad_gain_out = plain_call(
        functools.partial(out_back_kernel, len(grad_z_terms)),
        [*grad_z_terms, outputs, gain_out[None], place],
        [low(2 * capacity, model_width)] * group_size + [wide(own_rows, model_width), wide(1, model_width)],
        8 * group_size * capacity * own_rows * model_width, (), 0,
    )
    arrived_grads = exchange_blocks(send_grads, "blk")
    for keep, moved in chunks[len(chunk_sums) :]:
        chunk_sums.append(add_low(keep, after(moved, send_grads[0])))
    finished += [pair_finish(part, "batch", send_grads[0]) for part in chunk_sums[len(finished) : 2]]
    arrived_grads[0] = after(arrived_grads[0], *chunk_sums[2:], *finished[1:2])
    *grad_rows, in_keep, in_send, out_keep, out_send = expert_back(
        batch_me, arrived, arrived_grads, w_in, w_in.T, w_out, batch_size
    )
    back_rows = exchange_blocks(grad_rows, "blk")
    finished += [pair_finish(part, "batch", grad_rows[0]) for part in chunk_sums[len(finished) :]]
    branch_two, grad_middle, two_gains, cross_q_grad, memkey_part, memval_part = back_call(
        functools.partial(cross_back_kernel, group_size),
        [
            me, *back_rows, place_t, after_cross, gain_ffn[None], grad_sum, middle, gain_cross[None],
            co, cq, cross_q, mem_keys, mem_values, cross_log,
        ],
        [low(own_rows, model_width), wide(own_rows, model_width), wide(2, model_width)]
        + [low(own_rows, model_width)] + [low(group_size * own_rows, model_width)] * 2,
        own_rows, group_size * own_rows, model_width,
    )
    batch_half = batch_size // 2
    in_shape = (batch_half, model_width // batch_size, -1)
    out_shape = (batch_half, -1, model_width)
    w_in_moved = after(swap(in_send.reshape(in_shape), "batch", 1), branch_two)
    w_in_sums = add_low(in_keep.reshape(in_shape), w_in_moved)
    w_out_moved = swap(out_send.reshape(out_shape), "batch", 1)
    grad_middle = after(grad_middle, w_in_sums, *finished[2:])
    half = (group_size // 2, own_rows, model_width)
    state_keep, state_send, own_part, query_grad, key_part, value_part = back_call(
        self_back_kernel,
        [me, grad_middle, wo, wq, wk, wv, queries, all_keys, all_values, self_log],
        [low(*half)] * 2 + [wide(own_rows, model_width), low(own_rows, model_width)]
        + [low(group_size * own_rows, model_width)] * 2,
        own_rows, group_size * own_rows, model_width,
    )
    w_out_sums = add_low(out_keep.reshape(out_shape), after(w_out_moved, own_part))
    w_in_sum = pair_finish(w_in_sums, "batch", own_part)
    state_terms = scatter_terms(state_keep, state_send, "blk")
    state_terms[0] = after(state_terms[0], w_in_sum, w_out_sums)
    grad_tokens, self_gain = plain_call(
        functools.partial(token_back_kernel, len(state_terms)),
        [*state_terms, own_part, tokens[0], gain_self[None], grad_middle],
        [wide(own_rows, model_width), wide(1, model_width)],
        0, (), 0,
    )

    memory_part = (dot(memkey_part, ck, NT) + dot(memval_part, cv, NT)).astype(jnp.bfloat16)
    memory_part = memory_part.reshape(half[0], 2, own_rows, model_width)
    grad_memory = sum(
        term.astype(jnp.float32)
        for term in scatter_terms(memory_part[:, 0], memory_part[:, 1], "blk")
    )

    def sum_weights(pairs, gate, earlier):
        pairs[0] = (after(pairs[0][0], gate), pairs[0][1])
        keep, send = weight_parts(me, batch_me, pairs, group_size, batch_size)
        summed = total_of(scatter_terms(keep, send, "blk"))
        middle_part = batch_size // 2
        moved = after(swap(summed[middle_part:], "batch", 1), earlier)
        return add_low(summed[:middle_part], moved)

    cross_sums = sum_weights(
        [(h_two, cross_q_grad), (memory_all, memkey_part), (memory_all, memval_part), (cross_out, branch_two)],
        own_part, w_out_sums,
    )
    self_sums = sum_weights(
        [(h_all[:own_rows], query_grad), (h_all, key_part), (h_all, value_part), (attn_out, grad_middle)],
        own_part, cross_sums,
    )
    cross_sums = pair_finish(cross_sums, "batch")
    self_sums = pair_finish(self_sums, "batch")
    summed_weights = [self_sums[k] for k in range(4)] + [cross_sums[k] for k in range(4)]
    summed_gains = jnp.concatenate([self_gain, two_gains[1:], two_gains[:1], grad_gain_out])
    for axis in ("blk", "batch"):
        bit = 1
        while bit < lax.axis_size(axis):
            summed_gains = summed_gains + swap(summed_gains, axis, bit)
            bit *= 2
    w_in_sum = w_in_sum[None]
    w_out_sum = pair_finish(w_out_sums, "batch")[None]
    smooth_sums = core_stage({j: smooth_parts[j] for j in range(group_size)}, "blk")
    own_loss = own_terms[0] - sum(far_stage(smooth_sums, "blk"))
    embed_sum = jnp.concatenate(finished, axis=-1)[:, :vocab_part].T
    return (
        own_loss[None],
        grad_tokens[None],
        grad_memory[None],
        summed_gains[0],
        summed_gains[1],
        summed_gains[2],
        summed_gains[3],
        summed_weights[0],
        summed_weights[1],
        summed_weights[2],
        summed_weights[3],
        summed_weights[4],
        summed_weights[5],
        summed_weights[6],
        summed_weights[7],
        w_in_sum,
        w_out_sum,
        embed_sum,
    )


def solution(mesh):
    return jax.shard_map(
        per_device,
        mesh=mesh,
        in_specs=(
            P("batch", "blk", None),
            P("batch", "blk", None),
            P("batch"),
            P("batch", None),
            P(None, "batch", "blk", None),
            P(),
            P(),
            P(),
            P(),
            P(),
            P(),
            P(),
            P(),
            P(),
            P(),
            P(),
            P(),
            P("blk", None, None),
            P("blk", None, None),
            P("blk", None),
        ),
        out_specs=(
            P("batch", "blk"),
            P("batch", "blk", None),
            P("batch", "blk", None),
            P(),
            P(),
            P(),
            P(),
            P("batch", "blk"),
            P("batch", "blk"),
            P("batch", "blk"),
            P("batch", "blk"),
            P("batch", "blk"),
            P("batch", "blk"),
            P("batch", "blk"),
            P("batch", "blk"),
            P("blk", "batch", None),
            P("blk", "batch", None),
            P("blk", "batch"),
        ),
        check_vma=False,
    )
```

```python
import functools

import jax
import jax.numpy as jnp
from jax import lax
from jax.experimental import pallas as pl
from jax.experimental.pallas import tpu as pltpu
from jax.sharding import PartitionSpec as P

HEADS = 8
HD = 64


EPS_NORM = 1e-05
SMOOTH = 0.1
LOG2E = 1.4426950408889634
GELU = 0.7978845608028654
VMEM_LIMIT = 60 << 20
NN = (((1,), (0,)), ((), ()))
NT = (((1,), (1,)), ((), ()))


def work(flops):
    return pl.CostEstimate(flops=flops, bytes_accessed=0, transcendentals=0)


def dot(left, right, dims):
    return lax.dot_general(left, right, dims, preferred_element_type=jnp.float32)


def swap(value, axis, mask):
    size = lax.axis_size(axis)
    return lax.ppermute(value, axis, [(i, i ^ mask) for i in range(size)])


def gather_blocks(own, axis, *gates):
    size = lax.axis_size(axis)
    blocks = {0: own}
    bit = 2
    while bit < size:
        for k in range(0, bit, 2):
            blocks[bit | k] = swap(blocks[k], axis, bit)
        bit *= 2
    for k in range(0, size, 2):
        if k:
            blocks[k] = after(blocks[k], *gates)
        blocks[k | 1] = swap(blocks[k], axis, 1)
    return [blocks[j] for j in range(size)]


def exchange_blocks(own, axis):
    return [own[0]] + [swap(own[j], axis, j) for j in range(1, len(own))]


def core_stage(parts, axis, *gates):
    moved = {j ^ 1: after(swap(parts[j], axis, 1), *gates) for j in sorted(parts) if j % 2}
    return {j: add_low(parts[j], moved[j]) if j else [parts[0], moved[0]] for j in moved}


def far_stage(parts, axis):
    parts = dict(parts)
    terms = list(parts[0])
    size = lax.axis_size(axis)
    bit = 2
    while bit < size:
        odd = list(range(bit, size, 2 * bit))
        moved = swap(jnp.stack([parts[j] for j in odd]) if len(odd) > 1 else parts[bit], axis, bit)
        for k, j in enumerate(odd):
            part = moved[k] if len(odd) > 1 else moved
            if j == bit:
                terms.append(part)
            else:
                parts[j ^ bit] = add_low(parts[j ^ bit], part)
        bit *= 2
    return terms


def stacked_stage(keep, send, axis, *gates):
    moved = after(swap(send, axis, 1), *gates)
    parts = {2 * k: add_low(keep[k], moved[k]) for k in range(1, keep.shape[0])}
    parts[0] = [keep[0], moved[0]]
    return parts


def total_of(terms):
    return functools.reduce(add_low, terms)


def add_low(left, right):
    return (left.astype(jnp.float32) + right.astype(jnp.float32)).astype(left.dtype)


def part_device(me, place, size):
    half = size // 2
    return 2 * (place % half) + ((me % 2) ^ (place // half))


def pair_moved(sums, axis, *gates):
    half = sums.shape[0]
    groups = [[2 * k + bit for k in range(half)] for bit in range(2)]
    return after(lax.all_to_all(sums, axis, 0, 0, axis_index_groups=groups), *gates)


def pair_finish(sums, axis, *gates):
    return jnp.sum(pair_moved(sums, axis, *gates).astype(jnp.float32), axis=0)


def ring_start(sums, axis):
    half = sums.shape[0]
    gray = lambda k: k ^ (k >> 1)
    mine = lax.axis_index(axis) // 2
    shift = 1
    while (1 << shift) < 2 * half:
        mine = mine ^ (lax.axis_index(axis) // 2 >> shift)
        shift += 1
    links = [(2 * gray(k) + bit, 2 * gray((k + 1) % half) + bit) for k in range(half) for bit in range(2)]
    part = lambda step: lax.dynamic_index_in_dim(sums, gray((mine - 1 - step) % half), 0, keepdims=False)
    return part(0), lambda total: lax.ppermute(total, axis, links), [part(k) for k in range(1, half)]


def after(value, *others):
    return lax.optimization_barrier((value,) + others)[0]


def stats_kernel(cols, steps, count, blocks, has_earlier, me_ref, embed_ref, *refs):
    z_refs, refs = refs[:blocks], refs[blocks:]
    earlier_ref, refs = (refs[0], refs[1:]) if has_earlier else (None, refs)
    out_ref, rows_ref, turned_ref, max_ref, sum_ref, mix_ref, turn_ref = refs
    step = pl.program_id(0)
    half = rows_ref.shape[0] // 2
    part = rows_ref.shape[1] // count
    size = half // blocks

    @pl.when(step == 0)
    def _():
        max_ref[...] = jnp.full_like(max_ref, -jnp.inf)
        sum_ref[...] = jnp.zeros_like(sum_ref)
        mix_ref[...] = jnp.zeros_like(mix_ref)
        for p in range(2):
            for k, ref in enumerate(z_refs):
                rows_ref[p * half + k * size : p * half + (k + 1) * size, :] = ref[p]
        turn_ref[...] = rows_ref[...].T
        for place in range(count):
            start = pl.multiple_of(part_device(me_ref[0], place, count) * part, part)
            turned_ref[place * part : (place + 1) * part, :] = turn_ref[pl.ds(start, part), :]

    embed = embed_ref[...]
    for col in range(half // cols):
        places = [slice(p * half + col * cols, p * half + (col + 1) * cols) for p in range(2)]
        logits = [dot(embed, rows_ref[place, :], NT).reshape(-1, 8, cols) for place in places]
        apart = logits[0] - logits[1]
        for place, logit in zip(places, logits):
            old = max_ref[:, place]
            new = jnp.maximum(old, jnp.max(logit, axis=0))
            max_ref[:, place] = new
            scale = jnp.exp2((old - new) * LOG2E)
            weights = jnp.exp2((logit - new[None]) * LOG2E)
            sum_ref[:, place] = sum_ref[:, place] * scale + jnp.sum(weights, axis=0)
            mix_ref[:, place] = mix_ref[:, place] * scale + jnp.sum(weights * apart, axis=0)

    @pl.when(step == steps - 1)
    def _():
        top = jnp.max(max_ref[...], axis=0, keepdims=True)
        scale = jnp.exp2((max_ref[...] - top) * LOG2E)
        first = 0
        if has_earlier:
            first = earlier_ref.shape[0]
            out_ref[:first, :] = earlier_ref[...]
        out_ref[first : first + 1, :] = top
        out_ref[first + 1 : first + 2, :] = jnp.sum(sum_ref[...] * scale, axis=0, keepdims=True)
        out_ref[first + 2 : first + 3, :] = jnp.sum(mix_ref[...] * scale, axis=0, keepdims=True)


def row_tile(rows, limit):
    return max(size for size in range(16, limit + 1, 16) if rows % size == 0)


def vocab_stats(me, embed, blocks, count, earlier):
    vocab, width = embed.shape
    rows = sum(block.shape[0] * block.shape[1] for block in blocks)
    tile = row_tile(vocab, 800)
    cols = min(256, rows // 2)
    steps = vocab // tile
    operands = [me, embed, *blocks] + ([] if earlier is None else [earlier])
    shapes = [wide(3 if earlier is None else 3 + earlier.shape[0], rows), low(rows, width), low(width, rows)]
    return pl.pallas_call(
        functools.partial(stats_kernel, cols, steps, count, len(blocks), earlier is not None),
        grid=(steps,),
        in_specs=[
            pl.BlockSpec(memory_space=pltpu.SMEM),
            pl.BlockSpec((tile, width), lambda i: (i, 0)),
        ] + [whole(leaf) for leaf in operands[2:]],
        out_specs=[whole(leaf) for leaf in shapes],
        out_shape=shapes,
        scratch_shapes=[pltpu.VMEM((8, rows), jnp.float32)] * 3
        + [pltpu.VMEM((width, rows), jnp.bfloat16)],
        compiler_params=pltpu.CompilerParams(vmem_limit_bytes=VMEM_LIMIT),
        cost_estimate=work(5 * vocab * rows * width // 2),
    )(*operands)


def rows_kernel(groups, vocab_total, me_ref, length_ref, target_ref, *refs):
    stat_refs, (value_ref, label_ref, loss_ref) = refs[:-3], refs[-3:]
    devices = len(stat_refs)
    per_group = devices // groups
    rows = stat_refs[0].shape[1] // (2 * per_group)

    def stat(device, block, p, kind):
        block = block ^ device
        row = 3 * (block // per_group) + kind
        lane = (p * per_group + block % per_group) * rows
        return stat_refs[device][row : row + 1, lane : lane + rows]

    for block in range(devices):
        group, lane = block // per_group, (block % per_group) * rows
        place = slice(lane, lane + rows)
        start = pl.multiple_of((me_ref[0] ^ block) * rows, rows)
        position = start + lax.broadcasted_iota(jnp.int32, (1, rows), 1)
        live = position < length_ref[0]
        label_ref[group, 0:1, place] = jnp.where(live, target_ref[0:1, pl.ds(start, rows)], -1)
        logs, expects = [], []
        for p in range(2):
            tops = [stat(device, block, p, 0) for device in range(devices)]
            top = functools.reduce(jnp.maximum, tops)
            scales = [jnp.exp2((one - top) * LOG2E) for one in tops]
            total = sum(stat(device, block, p, 1) * scales[device] for device in range(devices))
            mixed = sum(stat(device, block, p, 2) * scales[device] for device in range(devices))
            logs.append(top + jnp.log(total))
            expects.append(mixed / total)
        values = [
            jnp.where(live, logs[0] * LOG2E, 1e30),
            jnp.where(live, logs[1] * LOG2E, 1e30),
            2.0 - expects[0],
            2.0 + expects[1],
            jnp.where(live, 1.0 - SMOOTH + SMOOTH / vocab_total, 0.0),
            jnp.where(live, SMOOTH / vocab_total, 0.0),
        ]
        for k, value in enumerate(values):
            value_ref[group, k : k + 1, place] = value
        if block == 0:
            loss_ref[...] = jnp.where(live, logs[0] + logs[1] + expects[0] - expects[1], 0.0)


def loss_back_kernel(cols, left, groups, has_total, has_carry, pieces, last, *refs):
    count = len(groups)
    base_ref, embed_ref = refs[:2]
    z_refs, z_t_refs, refs = refs[2 : 2 + count], refs[2 + count : 2 + 2 * count], refs[2 + 2 * count :]
    (row_ref, label_ref), refs = refs[:2], list(refs[2:])
    total_ref = refs.pop(0) if has_total else None
    carry_ref, loss_carry_ref = (refs.pop(0), refs.pop(0)) if has_carry else (None, None)
    loss_out_ref, grad_ref, sum_ref, loss_ref = refs[-4:]
    embed_refs, out_refs = refs[:pieces], refs[pieces:-4]
    step = pl.program_id(0)
    rows = z_refs[0].shape[0]
    half = rows // 2
    tile = embed_ref.shape[0]

    @pl.when(step == 0)
    def _():
        sum_ref[...] = carry_ref[...].astype(jnp.float32) if has_carry else jnp.zeros_like(sum_ref)
        loss_ref[...] = loss_carry_ref[...] if has_carry else jnp.zeros_like(loss_ref)

    rows_left = left - step * tile
    inside = lax.broadcasted_iota(jnp.int32, embed_ref.shape, 0) < rows_left
    embed = jnp.where(inside, embed_ref[...], jnp.zeros_like(embed_ref[...]))
    embed_t = embed.T
    ids = lax.broadcasted_iota(jnp.int32, (tile // 8, 8, cols), 0) * 8
    ids = ids + lax.broadcasted_iota(jnp.int32, (tile // 8, 8, cols), 1)
    base = base_ref[0] + step * tile
    for k, group in enumerate(groups):
        for col in range(half // cols):
            one = slice(col * cols, (col + 1) * cols)
            two = slice(half + col * cols, half + (col + 1) * cols)
            logit_one = dot(embed, z_refs[k][one, :], NT).reshape(-1, 8, cols)
            logit_two = dot(embed, z_refs[k][two, :], NT).reshape(-1, 8, cols)
            row = [row_ref[group, v : v + 1, one].reshape(1, 1, cols) for v in range(6)]
            prob_one = jnp.exp2(logit_one * LOG2E - row[0])
            prob_two = jnp.exp2(logit_two * LOG2E - row[1])
            apart = logit_one - logit_two
            hits = ids == (label_ref[group, 0:1, one] - base).reshape(1, 1, cols)
            smooth = jnp.where(hits, row[4], row[5])
            grad_one = prob_one * (apart + row[2]) - (prob_two + smooth)
            grad_two = prob_two * (row[3] - apart) - (prob_one + smooth)
            loss_ref[k, :, one] += jnp.sum(smooth * (logit_one + logit_two), axis=0)
            lane = k * rows + col * cols
            grad_ref[:, lane : lane + cols] = grad_one.reshape(tile, cols).astype(jnp.bfloat16)
            grad_ref[:, lane + half : lane + half + cols] = grad_two.reshape(tile, cols).astype(jnp.bfloat16)
    grad_embed = total_ref[...].astype(jnp.float32) if has_total else 0.0
    for k in range(count):
        place = slice(k * rows, (k + 1) * rows)
        grad_embed = grad_embed + dot(z_t_refs[k][...], grad_ref[:, place], NT)
        sum_ref[:, place] += dot(embed_t, grad_ref[:, place], NN)
    grad_embed = grad_embed.astype(jnp.bfloat16)
    part = grad_embed.shape[0] // len(embed_refs)
    for k, ref in enumerate(embed_refs):
        ref[...] = grad_embed[k * part : (k + 1) * part]

    @pl.when(step == pl.num_programs(0) - 1)
    def _():
        if not last:
            out_refs[0][...] = sum_ref[...].astype(jnp.bfloat16)
            loss_out_ref[...] = loss_ref[...]
        else:
            for k in range(last):
                size = half * count // last
                lane = k % (last // count) * size
                terms = loss_ref[k // (last // count), :, lane : lane + size]
                loss_out_ref[k : k + 1, :] = jnp.sum(terms, axis=0, keepdims=True)
            size = half * count // len(out_refs)
            per_group = len(out_refs) // count
            for k, ref in enumerate(out_refs):
                for p in range(2):
                    lane = k // per_group * rows + p * half + k % per_group * size
                    ref[p] = sum_ref[:, lane : lane + size].T.astype(ref.dtype)


def loss_back(base, embed, z_rows, z_t, row_values, labels, groups, span, total, carry, pieces, last):
    width = embed.shape[1]
    count = len(groups)
    rows = z_rows[0].shape[0]
    tile = TILE
    start, end = span
    steps, first = (end - start) // tile, start // tile
    cols = min(256, rows // 2)
    operands = [base + start, embed, *z_rows, *z_t, row_values, labels]
    vmem = pl.BlockSpec(memory_space=pltpu.VMEM)
    specs = [
        pl.BlockSpec(memory_space=pltpu.SMEM),
        pl.BlockSpec((tile, width), lambda i: (i + first, 0)),
    ] + [vmem] * (2 * count + 2)
    if total is not None:
        operands.append(total)
        specs.append(pl.BlockSpec((width, tile), lambda i: (0, i + first)))
    if carry is not None:
        operands += list(carry)
        specs += [vmem, vmem]
    piece = width // pieces
    grad_z = [low(2, rows * count // 2 // last, width)] * last if last else [low(width, rows * count)]
    loss = wide(last, rows * count // 2 // last) if last else wide(count, 8, rows // 2)
    return pl.pallas_call(
        functools.partial(
            loss_back_kernel, cols, embed.shape[0] - start, groups, total is not None, carry is not None, pieces, last
        ),
        grid=(steps,),
        in_specs=specs,
        out_specs=[pl.BlockSpec((piece, tile), lambda i: (0, i))] * pieces + [vmem] * (len(grad_z) + 1),
        out_shape=[low(piece, end - start)] * pieces + grad_z + [loss],
        scratch_shapes=[
            pltpu.VMEM((tile, rows * count), jnp.bfloat16),
            pltpu.VMEM((width, rows * count), jnp.float32),
            pltpu.VMEM((count, 8, rows // 2), jnp.float32),
        ],
        compiler_params=pltpu.CompilerParams(vmem_limit_bytes=VMEM_LIMIT),
        cost_estimate=work(9 * (end - start) * rows * count * width),
    )(*operands)


TILE = 1024


SCALE = HD ** (-0.5)


def head_lanes(pair, head):
    lanes = lax.broadcasted_iota(jnp.int32, pair.shape, 1)
    return jnp.where((lanes >= HD) == (head % 2 == 1), pair, jnp.zeros_like(pair))


def block_bias(me, rows, blocks, causal):
    if not causal:
        return [None] * blocks
    keys = lax.broadcasted_iota(jnp.int32, (rows, rows), 0)
    queries = lax.broadcasted_iota(jnp.int32, (rows, rows), 1)
    biases = [jnp.where(keys <= queries, 0.0, -1e30)]
    for block in range(1, blocks):
        biases.append(jnp.where((me ^ block) < me, 0.0, -1e30))
    return biases


def head_weights(keys, query, biases, rows):
    scores = []
    for block, bias in enumerate(biases):
        part = dot(keys[block * rows : (block + 1) * rows], query, NT)
        scores.append(part if bias is None else part + bias)
    return scores


def normed(values, gain):
    center = values - jnp.mean(values, axis=-1, keepdims=True)
    spread = jnp.mean(center * center, axis=-1, keepdims=True)
    return center * lax.rsqrt(spread + EPS_NORM) * gain


def normed_back(values, gain, upstream):
    center = values - jnp.mean(values, axis=-1, keepdims=True)
    spread = jnp.mean(center * center, axis=-1, keepdims=True)
    scale = lax.rsqrt(spread + EPS_NORM)
    unit = center * scale
    grad_gain = jnp.sum(upstream * unit, axis=0, keepdims=True)
    up = upstream * gain
    mean_up = jnp.mean(up, axis=-1, keepdims=True)
    mean_mix = jnp.mean(up * unit, axis=-1, keepdims=True)
    return scale * (up - mean_up - unit * mean_mix), grad_gain


def slot_rows(place_ref, count, passes):
    rows = place_ref.shape[1]
    slots = lax.broadcasted_iota(jnp.int32, (count, rows), 0)
    hits = functools.reduce(jnp.logical_or, [slots == place_ref[p : p + 1, :] for p in passes])
    return jnp.where(hits, 1.0, 0.0).astype(jnp.bfloat16)


def token_rows(place_ref, count, passes):
    rows = place_ref.shape[0]
    slots = lax.broadcasted_iota(jnp.int32, (rows, count), 1)
    hits = functools.reduce(jnp.logical_or, [slots == place_ref[:, p : p + 1] for p in passes])
    return jnp.where(hits, 1.0, 0.0).astype(jnp.bfloat16)


def attend_kernel(blocks, causal, *refs):
    me_ref, refs = refs[0], refs[1:]
    block_refs, refs = refs[:blocks], refs[blocks:]
    if causal:
        (first_gain_ref, gain_ref, wq_ref, wk_ref, wv_ref, wo_ref), refs = refs[:6], refs[6:]
        slot_refs = ()
    else:
        (source_ref, residual_ref, place_ref, gain_ref, wq_ref, wk_ref, wv_ref, wo_ref), refs = (
            refs[:8],
            refs[8:],
        )
        slot_refs, refs = refs[:blocks], refs[blocks:]
    (query_ref, key_ref, value_ref, all_ref, out_ref, log_ref, sum_ref, next_ref,
     value_t_ref, out_t_ref) = refs
    rows = block_refs[0].shape[0]
    for block, ref in enumerate(block_refs):
        part = ref[...]
        if causal:
            part = normed(part.astype(jnp.float32), first_gain_ref[...]).astype(jnp.bfloat16)
        all_ref[block * rows : (block + 1) * rows, :] = part
    source = all_ref[:rows, :] if causal else source_ref[...]
    residual = block_refs[0][...].astype(jnp.float32) if causal else residual_ref[...]
    query_ref[...] = dot(source, wq_ref[...], NN).astype(jnp.bfloat16)
    key_ref[...] = dot(all_ref[...], wk_ref[...], NN).astype(jnp.bfloat16)
    values = dot(all_ref[...], wv_ref[...], NN).astype(jnp.bfloat16)
    value_ref[...] = values
    value_t_ref[...] = values.T
    biases = block_bias(me_ref[0], rows, blocks, causal)
    factor = SCALE * LOG2E
    for head in range(HEADS):
        lanes = slice(head // 2 * 128, head // 2 * 128 + 128)
        query = head_lanes(query_ref[:, lanes], head)
        scores = head_weights(key_ref[:, lanes], query, biases, rows)
        top = functools.reduce(
            jnp.maximum, [jnp.max(part.reshape(-1, 8, rows), axis=0) for part in scores]
        )
        top = jnp.max(top, axis=0, keepdims=True) * factor
        weights = [jnp.exp2(part * factor - top) for part in scores]
        total = sum(jnp.sum(part.reshape(-1, 8, rows), axis=0) for part in weights)
        total = jnp.sum(total, axis=0, keepdims=True)
        log_ref[head : head + 1, :] = top + jnp.log2(total)
        weights = jnp.concatenate([part.astype(jnp.bfloat16) for part in weights], axis=0)
        place = slice(head * HD, (head + 1) * HD)
        out_t_ref[place, :] = dot(value_t_ref[place, :], weights, NN) / total
    out = out_t_ref[...].T.astype(jnp.bfloat16)
    out_ref[...] = out
    states = residual + dot(out, wo_ref[...], NN)
    sum_ref[...] = states
    following = normed(states, gain_ref[...]).astype(jnp.bfloat16)
    next_ref[...] = following
    if slot_refs:
        count = slot_refs[0].shape[0]
        sends = dot(slot_rows(place_ref, blocks * count, (0, 1)), following, NN).astype(jnp.bfloat16)
        for block, ref in enumerate(slot_refs):
            ref[...] = sends[block * count : (block + 1) * count]


def low(*shape):
    return jax.ShapeDtypeStruct(shape, jnp.bfloat16)


def wide(*shape):
    return jax.ShapeDtypeStruct(shape, jnp.float32)


def attend(me, blocks, weights, gains, slots, source=None, residual=None, place=None):
    rows, width = blocks[0].shape
    count = rows * len(blocks)
    causal = source is None
    operands = [me, *blocks]
    if not causal:
        operands += [source, residual, place]
    operands += [gain[None] for gain in gains] + list(weights)
    shapes = [low(slots, width)] * (0 if causal else len(blocks)) + [
        low(rows, width), low(count, width), low(count, width), low(count, width),
        low(rows, width), wide(HEADS, rows), wide(rows, width), low(rows, width),
    ]
    return pl.pallas_call(
        functools.partial(attend_kernel, len(blocks), causal),
        grid=(1,),
        in_specs=[pl.BlockSpec(memory_space=pltpu.SMEM)] + [whole(leaf) for leaf in operands[1:]],
        out_specs=[whole(leaf) for leaf in shapes],
        out_shape=shapes,
        scratch_shapes=[pltpu.VMEM((width, count), jnp.bfloat16), pltpu.VMEM((width, rows), jnp.float32)],
        compiler_params=pltpu.CompilerParams(vmem_limit_bytes=VMEM_LIMIT),
        cost_estimate=work(9 * 10**9),
    )(*operands)


def attend_back_core(causal, me_ref, branch, wo_ref, query_ref, key_ref, value_ref, log_ref,
                     grad_query_ref, grad_key_ref, grad_value_ref, key_t_ref, up_ref, query_t_ref):
    rows = query_ref.shape[0]
    blocks = key_ref.shape[0] // rows
    up_ref[...] = dot(branch, wo_ref[...], NT).astype(jnp.bfloat16)
    key_t_ref[...] = key_ref[...].T
    biases = block_bias(me_ref[0], rows, blocks, causal)
    factor = SCALE * LOG2E
    for pair in range(HEADS // 2):
        lanes = slice(pair * 128, pair * 128 + 128)
        grad_keys, grad_values = 0.0, 0.0
        for head in (2 * pair, 2 * pair + 1):
            query = head_lanes(query_ref[:, lanes], head)
            upstream = head_lanes(up_ref[:, lanes], head)
            log_total = log_ref[head : head + 1, :]
            scores = head_weights(key_ref[:, lanes], query, biases, rows)
            probs = jnp.concatenate([jnp.exp2(part * factor - log_total) for part in scores], axis=0)
            grad_probs = dot(value_ref[:, lanes], upstream, NT)
            inner = jnp.sum((probs * grad_probs).reshape(-1, 8, rows), axis=0)
            inner = jnp.sum(inner, axis=0, keepdims=True)
            grad_scores = (probs * (grad_probs - inner)).astype(jnp.bfloat16)
            grad_values = grad_values + dot(probs.astype(jnp.bfloat16), upstream, NN)
            grad_keys = grad_keys + dot(grad_scores, query, NN)
            place = slice(head * HD, (head + 1) * HD)
            query_t_ref[place, :] = dot(key_t_ref[place, :], grad_scores, NN) * SCALE
        grad_value_ref[:, lanes] = grad_values.astype(jnp.bfloat16)
        grad_key_ref[:, lanes] = (grad_keys * SCALE).astype(jnp.bfloat16)
    grad_query_ref[...] = query_t_ref[...].T.astype(jnp.bfloat16)


def cross_back_kernel(blocks, *refs):
    me_ref, back_refs, refs = refs[0], refs[1 : 1 + blocks], refs[1 + blocks :]
    (place_ref, after_ref, gain_ffn_ref, grad_sum_ref, middle_ref, gain_cross_ref, wo_ref, wq_ref,
     query_ref, key_ref, value_ref, log_ref), refs = refs[:12], refs[12:]
    (branch_ref, middle_grad_ref, gains_ref, grad_query_ref, grad_key_ref, grad_value_ref,
     key_t_ref, up_ref, query_t_ref) = refs
    back = jnp.concatenate([ref[...] for ref in back_refs], axis=0)
    grad_normed = dot(token_rows(place_ref, back.shape[0], (0, 1)), back, NN)
    grad_after, gains_ref[0:1, :] = normed_back(after_ref[...], gain_ffn_ref[...], grad_normed)
    grad_after = grad_after + grad_sum_ref[...]
    branch = grad_after.astype(jnp.bfloat16)
    branch_ref[...] = branch
    attend_back_core(False, me_ref, branch, wo_ref, query_ref, key_ref, value_ref, log_ref,
                     grad_query_ref, grad_key_ref, grad_value_ref, key_t_ref, up_ref, query_t_ref)
    grad_normed = dot(grad_query_ref[...], wq_ref[...], NT)
    grad_middle, gains_ref[1:2, :] = normed_back(middle_ref[...], gain_cross_ref[...], grad_normed)
    middle_grad_ref[...] = grad_middle + grad_after


def self_back_kernel(me_ref, middle_grad_ref, wo_ref, wq_ref, wk_ref, wv_ref,
                     query_ref, key_ref, value_ref, log_ref, memkey_ref, memval_ref, ck_ref, cv_ref,
                     keep_ref, send_ref, own_ref, grad_query_ref, grad_key_ref, grad_value_ref,
                     key_t_ref, up_ref, query_t_ref):
    rows = query_ref.shape[0]
    branch = middle_grad_ref[...].astype(jnp.bfloat16)
    attend_back_core(True, me_ref, branch, wo_ref, query_ref, key_ref, value_ref, log_ref,
                     grad_query_ref, grad_key_ref, grad_value_ref, key_t_ref, up_ref, query_t_ref)
    for block in range(key_ref.shape[0] // rows):
        place = slice(block * rows, (block + 1) * rows)
        part = dot(grad_key_ref[place, :], wk_ref[...], NT) + dot(grad_value_ref[place, :], wv_ref[...], NT)
        target = send_ref if block % 2 else keep_ref
        target[block // 2, 0] = part.astype(jnp.bfloat16)
        part = dot(memkey_ref[place, :], ck_ref[...], NT) + dot(memval_ref[place, :], cv_ref[...], NT)
        target[block // 2, 1] = part.astype(jnp.bfloat16)
    own_ref[...] = dot(grad_query_ref[...], wq_ref[...], NT)


def back_call(kernel, operands, shapes, rows, count, width):
    return pl.pallas_call(
        kernel,
        grid=(1,),
        in_specs=[pl.BlockSpec(memory_space=pltpu.SMEM)] + [whole(leaf) for leaf in operands[1:]],
        out_specs=[whole(leaf) for leaf in shapes],
        out_shape=shapes,
        scratch_shapes=[
            pltpu.VMEM((width, count), jnp.bfloat16),
            pltpu.VMEM((rows, width), jnp.bfloat16),
            pltpu.VMEM((width, rows), jnp.float32),
        ],
        compiler_params=pltpu.CompilerParams(vmem_limit_bytes=VMEM_LIMIT),
        cost_estimate=work(100 * rows * count * width),
    )(*operands)


def whole(leaf):
    rank = len(leaf.shape)
    return pl.BlockSpec(leaf.shape, lambda *_: (0,) * rank)


def plain_call(kernel, operands, shapes, flops, scratch=(), scalars=1):
    size = sum(leaf.size * leaf.dtype.itemsize for leaf in list(operands) + list(shapes))
    return pl.pallas_call(
        kernel,
        grid=(1,),
        in_specs=[pl.BlockSpec(memory_space=pltpu.SMEM)] * scalars
        + [whole(leaf) for leaf in operands[scalars:]],
        out_specs=[whole(leaf) for leaf in shapes],
        out_shape=shapes,
        scratch_shapes=list(scratch),
        compiler_params=pltpu.CompilerParams(vmem_limit_bytes=48 << 20),
        cost_estimate=work(flops),
    )(*operands)


def weights_kernel(plan, targets, lefts, *refs):
    group_me_ref, batch_me_ref, refs = refs[0], refs[1], refs[2:]
    operand_refs, target_refs, product_ref = refs[:-5], refs[-5:-1], refs[-1]
    groups, batches = targets
    width = product_ref.shape[0]
    row_part, col_part = width // batches, width // groups
    turned = {left: operand_refs[left][...].T for left in lefts}
    for number, pairs in enumerate(plan):
        for pair, (left, right) in enumerate(pairs):
            value = operand_refs[right][...].astype(jnp.bfloat16)
            product_ref[...] = dot(turned[left][:, : value.shape[0]], value, NN)
            for block in range(groups):
                target = target_refs[2 * number + block % 2]
                at = group_me_ref[0] ^ block
                for spot in range(batches):
                    row = pl.multiple_of(part_device(batch_me_ref[0], spot, batches) * row_part, row_part)
                    col = pl.multiple_of(at * col_part, 128)
                    part = product_ref[pl.ds(row, row_part), pl.ds(col, col_part)]
                    target[block // 2, spot, pair] = part.astype(jnp.bfloat16)


def plain_parts(group_me, batch_me, operands, plan, groups, batches):
    width = operands[0].shape[1]
    columns = group_me ^ jnp.arange(groups, dtype=jnp.int32)
    spots = jnp.stack([part_device(batch_me, spot, batches) for spot in range(batches)])
    outputs = []
    for pairs in plan:
        stacked = []
        for left, right in pairs:
            value = operands[right].astype(jnp.bfloat16)
            stacked.append(dot(operands[left][: value.shape[0]].T, value, NN).astype(jnp.bfloat16))
        parts = jnp.stack(stacked).reshape(len(pairs), batches, width // batches, groups, width // groups)
        parts = parts.transpose(3, 1, 0, 2, 4)[columns][:, spots]
        outputs += [parts[0::2], parts[1::2]]
    return outputs


def weight_parts(group_me, batch_me, operands, plan, groups, batches):
    width = operands[0].shape[1]
    if width // groups % 128:
        return plain_parts(group_me[0], batch_me[0], operands, plan, groups, batches)
    lefts = sorted({left for pairs in plan for left, _ in pairs})
    shapes = [
        low(groups // 2, batches, len(pairs), width // batches, width // groups)
        for pairs in plan for _ in range(2)
    ]
    return plain_call(
        functools.partial(weights_kernel, plan, (groups, batches), lefts),
        [group_me, batch_me, *operands], shapes, 8 * 10**9, [pltpu.VMEM((width, width), jnp.float32)], 2,
    )


def expert_kernel(parts, steps, w_in_ref, w_out_ref, *refs):
    row_refs, out_refs, (rows_ref, total_ref) = refs[:parts], refs[parts : 2 * parts], refs[2 * parts :]
    step = pl.program_id(0)
    size = row_refs[0].shape[0]

    @pl.when(step == 0)
    def _():
        for k, ref in enumerate(row_refs):
            rows_ref[k * size : (k + 1) * size, :] = ref[...]
        total_ref[...] = jnp.zeros_like(total_ref)

    up = dot(rows_ref[...], w_in_ref[...], NN)
    curve = jnp.tanh(up * (GELU + GELU * 0.044715 * (up * up)))
    activity = (up * (0.5 + 0.5 * curve)).astype(jnp.bfloat16)
    total_ref[...] += dot(activity, w_out_ref[...], NN)

    @pl.when(step == steps - 1)
    def _():
        for k, ref in enumerate(out_refs):
            ref[...] = total_ref[k * size : (k + 1) * size, :].astype(jnp.bfloat16)


def expert_rows(parts, w_in, w_out):
    size, width = parts[0].shape
    hidden = w_in.shape[1]
    tile = min(512, hidden)
    rows = size * len(parts)
    return pl.pallas_call(
        functools.partial(expert_kernel, len(parts), hidden // tile),
        grid=(hidden // tile,),
        in_specs=[
            pl.BlockSpec((width, tile), lambda i: (0, i)),
            pl.BlockSpec((tile, width), lambda i: (i, 0)),
        ] + [whole(leaf) for leaf in parts],
        out_specs=[whole(leaf) for leaf in parts],
        out_shape=[low(size, width)] * len(parts),
        scratch_shapes=[pltpu.VMEM((rows, width), jnp.bfloat16), pltpu.VMEM((rows, width), jnp.float32)],
        compiler_params=pltpu.CompilerParams(vmem_limit_bytes=40 << 20),
        cost_estimate=work(4 * rows * width * hidden),
    )(w_in, w_out, *parts)


def expert_back_kernel(parts, steps, batch_me_ref, w_in_ref, w_in_t_ref, w_out_ref, *refs):
    row_refs, grad_refs, refs = refs[:parts], refs[parts : 2 * parts], refs[2 * parts :]
    out_refs, refs = refs[:parts], refs[parts:]
    keep_ref, send_ref, rows_ref, turned_ref, grads_ref, total_ref = refs
    step = pl.program_id(0)
    size = row_refs[0].shape[0]
    half = steps // 2
    width = turned_ref.shape[0]
    part = width // steps
    tile = w_out_ref.shape[0]

    @pl.when(step == 0)
    def _():
        for k in range(parts):
            rows_ref[k * size : (k + 1) * size, :] = row_refs[k][...]
            grads_ref[k * size : (k + 1) * size, :] = grad_refs[k][...]
        total_ref[...] = rows_ref[...].T.astype(jnp.float32)
        for place in range(steps):
            start = pl.multiple_of(part_device(batch_me_ref[0], place, steps) * part, part)
            turned_ref[place * part : (place + 1) * part, :] = total_ref[pl.ds(start, part), :].astype(
                jnp.bfloat16
            )
        total_ref[...] = jnp.zeros_like(total_ref)

    up = dot(w_in_t_ref[...], rows_ref[...], NT)
    square = up * up
    curve = jnp.tanh(up * (GELU + GELU * 0.044715 * square))
    share = 0.5 + 0.5 * curve
    active = up * share
    activity = active.astype(jnp.bfloat16)
    slope = share + active * (1.0 - curve) * (GELU + GELU * 3.0 * 0.044715 * square)
    grad_up = (dot(w_out_ref[...], grads_ref[...], NT) * slope).astype(jnp.bfloat16)
    grad_out = dot(activity, grads_ref[...], NN).astype(jnp.bfloat16)

    @pl.when(step < half)
    def _():
        keep_ref[step, :tile, :] = grad_out

    @pl.when(step >= half)
    def _():
        send_ref[step - half, :tile, :] = grad_out

    grad_in = dot(turned_ref[...], grad_up, NT).astype(jnp.bfloat16)
    column = part_device(batch_me_ref[0], step, steps) * tile
    row = pl.multiple_of(tile + column // width * part, part)
    lane = pl.multiple_of(column % width, tile)
    for place in range(steps):
        target = keep_ref if place < half else send_ref
        target[place % half, pl.ds(row, part), pl.ds(lane, tile)] = grad_in[place * part : (place + 1) * part]
    total_ref[...] += dot(w_in_ref[...], grad_up, NN)

    @pl.when(step == steps - 1)
    def _():
        for k, ref in enumerate(out_refs):
            ref[...] = total_ref[:, k * size : (k + 1) * size].T.astype(jnp.bfloat16)


def expert_back(batch_me, rows, grads, w_in, w_in_t, w_out, batches):
    size, width = rows[0].shape
    count = len(rows)
    hidden = w_in.shape[1]
    tile = hidden // batches
    half = batches // 2
    total = size * count

    def unit(i, me_ref):
        return part_device(me_ref[0], i, batches)

    both = low(half, 2 * tile, width)
    return pl.pallas_call(
        functools.partial(expert_back_kernel, count, batches),
        grid_spec=pltpu.PrefetchScalarGridSpec(
            num_scalar_prefetch=1,
            grid=(batches,),
            in_specs=[
                pl.BlockSpec((width, tile), lambda i, me_ref: (0, unit(i, me_ref))),
                pl.BlockSpec((tile, width), lambda i, me_ref: (unit(i, me_ref), 0)),
                pl.BlockSpec((tile, width), lambda i, me_ref: (unit(i, me_ref), 0)),
            ] + [whole(leaf) for leaf in list(rows) + list(grads)],
            out_specs=[whole(leaf) for leaf in [*rows, both, both]],
            scratch_shapes=[
                pltpu.VMEM((total, width), jnp.bfloat16),
                pltpu.VMEM((width, total), jnp.bfloat16),
                pltpu.VMEM((total, width), jnp.bfloat16),
                pltpu.VMEM((width, total), jnp.float32),
            ],
        ),
        out_shape=[low(size, width)] * count + [both, both],
        compiler_params=pltpu.CompilerParams(vmem_limit_bytes=VMEM_LIMIT),
        cost_estimate=work(24 * total * width * hidden),
    )(batch_me, w_in, w_in_t, w_out, *rows, *grads)


def combine_kernel(parts, *refs):
    back_refs, (place_ref, after_ref, gain_ref, out_ref, z_ref) = refs[:parts], refs[parts:]
    back = jnp.concatenate([ref[...] for ref in back_refs], axis=0)
    for p in range(2):
        states = after_ref[...] + dot(token_rows(place_ref, back.shape[0], (p,)), back, NN)
        out_ref[p] = states
        z_ref[p] = normed(states, gain_ref[...]).astype(jnp.bfloat16)


def out_back_kernel(sources, *refs):
    grad_refs, (out_ref, gain_ref, place_ref), refs = refs[:sources], refs[sources : sources + 3], refs[sources + 3 :]
    slot_refs, (sum_ref, gain_grad_ref) = refs[:-2], refs[-2:]
    count = len(slot_refs) * slot_refs[0].shape[0]
    grads, gain_grad, slots = 0.0, 0.0, 0.0
    for p in range(2):
        upstream = sum(ref[p].astype(jnp.float32) for ref in grad_refs)
        grad, more = normed_back(out_ref[p], gain_ref[...], upstream)
        grads, gain_grad = grads + grad, gain_grad + more
        slots = slots + dot(slot_rows(place_ref, count, (p,)), grad.astype(jnp.bfloat16), NN)
    sum_ref[...] = grads
    gain_grad_ref[...] = gain_grad
    size = slot_refs[0].shape[0]
    for k, ref in enumerate(slot_refs):
        ref[...] = slots[k * size : (k + 1) * size].astype(jnp.bfloat16)


def token_back_kernel(sources, *refs):
    grad_refs, (own_ref, states_ref, gain_ref, middle_ref, out_ref, memory_ref, gain_grad_ref) = (
        refs[:sources],
        refs[sources:],
    )
    upstream = own_ref[...] + sum(ref[0].astype(jnp.float32) for ref in grad_refs)
    memory_ref[...] = sum(ref[1].astype(jnp.float32) for ref in grad_refs)
    grad, gain_grad_ref[...] = normed_back(states_ref[...].astype(jnp.float32), gain_ref[...], upstream)
    out_ref[...] = grad + middle_ref[...]


def per_device(
    tokens,
    memory,
    lengths,
    targets,
    expert_ids,
    gain_self,
    gain_cross,
    gain_ffn,
    gain_out,
    wq,
    wk,
    wv,
    wo,
    cq,
    ck,
    cv,
    co,
    w_in,
    w_out,
    embed,
):
    group_index = lax.axis_index("blk")
    group_size = lax.axis_size("blk")
    batch_size = lax.axis_size("batch")
    own_rows, model_width = tokens.shape[1:]
    me = group_index.astype(jnp.int32).reshape(1)
    batch_me = lax.axis_index("batch").astype(jnp.int32).reshape(1)
    capacity = 3 * own_rows // (2 * group_size)
    w_in, w_out = w_in[0], w_out[0]

    vocab_part = embed.shape[0]
    padded = -(-vocab_part // TILE) * TILE
    token_blocks = gather_blocks(tokens[0], "blk")
    memory_own = memory[0]
    picks = expert_ids[:, 0, :, 0]
    onehot = (picks[:, :, None] == jnp.arange(group_size, dtype=jnp.int32)).astype(jnp.int32)
    slot = jnp.sum(onehot * (jnp.cumsum(onehot, axis=1) - onehot), axis=-1)
    place = ((picks ^ group_index) * 2 + jnp.arange(2, dtype=jnp.int32)[:, None]) * capacity + slot
    place_t = place.T

    queries, all_keys, all_values, h_all, attn_out, self_log, middle, h_two = attend(
        me, token_blocks, (wq, wk, wv, wo), (gain_self, gain_cross), 0
    )
    memory_blocks = gather_blocks(memory_own, "blk", h_two)
    *sends, cross_q, mem_keys, mem_values, memory_all, cross_out, cross_log, after_cross, _ = attend(
        me, memory_blocks, (cq, ck, cv, co), (gain_ffn,), 2 * capacity, h_two, middle, place
    )
    arrived = exchange_blocks(sends, "blk")
    results = expert_rows(arrived[:2], w_in, w_out)
    if group_size > 2:
        results = list(results) + list(expert_rows(arrived[2:], w_in, w_out))
    returned = exchange_blocks(results, "blk")
    outputs, z_pair = plain_call(
        functools.partial(combine_kernel, group_size),
        [*returned, place_t, after_cross, gain_out[None]],
        [wide(2, own_rows, model_width), low(2, own_rows, model_width)],
        8 * group_size * capacity * own_rows * model_width, (), 0,
    )

    near_z = [z_pair, swap(z_pair, "blk", 1)]
    far_z = {bit: swap(z_pair, "blk", bit) for bit in (1 << k for k in range(1, group_size.bit_length() - 1))}
    count = max(2, group_size * own_rows // 1024)
    per_group = group_size // count
    groups = [list(range(k * per_group, (k + 1) * per_group)) for k in range(count)]
    stats, group_z, group_z_t = None, [], []
    z_blocks = dict(enumerate(near_z))
    if per_group > 2:
        z_blocks = dict(enumerate(gather_blocks(z_pair, "blk")))
    for number, group in enumerate(groups):
        if number and 2 not in z_blocks:
            z_blocks[2] = after(far_z[2], stats)
            z_blocks[3] = swap(z_blocks[2], "blk", 1)
        stats, rows, rows_t = vocab_stats(
            batch_me, embed, [z_blocks[j] for j in group], batch_size, stats
        )
        group_z.append(rows)
        group_z_t.append(rows_t)
    all_stats = [stats] + [swap(stats, "blk", j) for j in range(1, group_size)]
    row_values, labels, own_terms = plain_call(
        functools.partial(rows_kernel, count, vocab_part * group_size),
        [me, lengths, targets, *all_stats],
        [
            wide(count, 6, per_group * own_rows),
            jax.ShapeDtypeStruct((count, 1, per_group * own_rows), jnp.int32),
            wide(1, own_rows),
        ],
        0, (), 2,
    )
    vocab_base = me * vocab_part
    total = None
    sums, smooth_parts, chunks, chunk_sums, finished = {}, {}, [], [], []
    joined = max(1, min(count, 1024 // (per_group * own_rows)))
    for at in range(count - joined, -1, -joined):
        mine = range(at, at + joined)
        operands = (
            vocab_base, embed, group_z[at : at + joined], group_z_t[at : at + joined],
            row_values, labels, tuple(mine),
        )
        if at > 0:
            total, *grad_z, smooth = loss_back(
                *operands, (0, padded), total, None, 1, joined * per_group
            )
        else:
            carry = None
            tiles = padded // TILE
            cuts = [0, tiles // 4, 5 * tiles // 8, tiles] if tiles >= 8 else [0, tiles]
            for number in range(len(cuts) - 1):
                start, end = cuts[number] * TILE, cuts[number + 1] * TILE
                done = end == padded
                if done and number > 1:
                    chunk_sums.append(add_low(*chunks[0]))
                    carry = (after(carry[0], chunk_sums[0]), carry[1])
                keep, send, *grad_z, smooth = loss_back(
                    *operands, (start, end), total, carry, 2, joined * per_group if done else 0
                )
                carry = (grad_z[0], smooth)
                shape = (batch_size // 2, model_width // batch_size, end - start)
                send = send.reshape(shape)
                chunks.append((keep.reshape(shape), send if number > 1 else swap(send, "batch", 1)))
        held = [j for group in mine for j in groups[group]]
        if len(chunk_sums) == 1:
            first_moved = pair_moved(chunk_sums[0], "batch", grad_z[0])
            finished.append(jnp.sum(first_moved.astype(jnp.float32), axis=0))
            sums.update(core_stage(dict(zip(held, grad_z)), "blk", first_moved))
            near = [sums[j] for j in sums if j]
            chunk_sums.append(add_low(chunks[1][0], after(chunks[1][1], *near)))
            for number in range(2, len(chunks)):
                keep, send = chunks[number]
                chunks[number] = (keep, swap(after(send, *near), "batch", 1))
        else:
            sums.update(core_stage(dict(zip(held, grad_z)), "blk"))
        smooth_parts[at] = smooth
    for keep, moved in chunks[len(chunk_sums) : 2]:
        chunk_sums.append(add_low(keep, moved))
    grad_z_terms = far_stage(sums, "blk")
    *send_grads, grad_sum, grad_gain_out = plain_call(
        functools.partial(out_back_kernel, len(grad_z_terms)),
        [*grad_z_terms, outputs, gain_out[None], place],
        [low(2 * capacity, model_width)] * group_size + [wide(own_rows, model_width), wide(1, model_width)],
        8 * group_size * capacity * own_rows * model_width, (), 0,
    )
    arrived_grads = exchange_blocks(send_grads, "blk")
    *grad_rows, io_keep, io_send = expert_back(
        batch_me, arrived, arrived_grads, w_in, w_in.T, w_out, batch_size
    )
    back_rows = exchange_blocks(grad_rows, "blk")
    for keep, moved in chunks[len(chunk_sums) :]:
        chunk_sums.append(add_low(keep, after(moved, back_rows[1])))
    finished += [pair_finish(part, "batch", back_rows[1]) for part in chunk_sums[len(finished) : 2]]
    back_rows[0] = after(back_rows[0], *chunk_sums[2:], *finished[1:2])
    branch_two, grad_middle, two_gains, cross_q_grad, memkey_part, memval_part = back_call(
        functools.partial(cross_back_kernel, group_size),
        [
            me, *back_rows, place_t, after_cross, gain_ffn[None], grad_sum, middle, gain_cross[None],
            co, cq, cross_q, mem_keys, mem_values, cross_log,
        ],
        [low(own_rows, model_width), wide(own_rows, model_width), wide(2, model_width)]
        + [low(own_rows, model_width)] + [low(group_size * own_rows, model_width)] * 2,
        own_rows, group_size * own_rows, model_width,
    )
    io_moved = swap(io_send, "batch", 1)
    half = (group_size // 2, 2, own_rows, model_width)
    state_keep, state_send, own_part, query_grad, key_part, value_part = back_call(
        self_back_kernel,
        [
            me, grad_middle, wo, wq, wk, wv, queries, all_keys, all_values, self_log,
            memkey_part, memval_part, ck, cv,
        ],
        [low(*half)] * 2 + [wide(own_rows, model_width), low(own_rows, model_width)]
        + [low(group_size * own_rows, model_width)] * 2,
        own_rows, group_size * own_rows, model_width,
    )
    later = lambda parts: [parts[j] for j in parts if j]
    state_sums = stacked_stage(state_keep, state_send, "blk")
    state_terms = far_stage(state_sums, "blk")
    io_sums = add_low(io_keep, after(io_moved, own_part))
    io_total, io_pass, io_parts = ring_start(io_sums, "batch")
    io_hop = io_pass(io_total)
    last_moved = [pair_moved(part, "batch", *later(state_sums)) for part in chunk_sums[len(finished) :]]
    operands = [
        after(h_two, io_total, *later(state_sums), *last_moved), memory_all, cross_out, h_all, attn_out,
        cross_q_grad, memkey_part, memval_part, branch_two, query_grad, key_part, value_part, grad_middle,
    ]
    plan = (((0, 5), (1, 6), (1, 7), (2, 8)), ((3, 9), (3, 10), (3, 11), (4, 12)))
    cross_keep, cross_send, self_keep, self_send = weight_parts(
        me, batch_me, operands, plan, group_size, batch_size
    )
    middle_part = batch_size // 2
    state_terms[-1] = after(state_terms[-1], cross_keep)
    grad_tokens, grad_memory, self_gain = plain_call(
        functools.partial(token_back_kernel, len(state_terms)),
        [*state_terms, own_part, tokens[0], gain_self[None], grad_middle],
        [wide(own_rows, model_width), wide(own_rows, model_width), wide(1, model_width)],
        0, (), 0,
    )
    cross_parts = stacked_stage(cross_keep, cross_send, "blk", self_gain)
    cross_terms = far_stage(cross_parts, "blk")
    self_sums = add_low(self_keep, after(swap(self_send, "blk", 1), *later(cross_parts)))
    self_moved = swap(self_sums[:, middle_part:], "batch", 1)
    io_total = add_low(after(io_hop, self_gain), io_parts[0])
    io_hop = io_pass(io_total)
    self_pair = add_low(self_sums[:, :middle_part], after(self_moved, io_total))
    self_terms = far_stage(
        {2 * k: self_pair[k] if k else [self_pair[0]] for k in range(group_size // 2)}, "blk"
    )
    cross_terms[-1] = after(cross_terms[-1], self_pair)
    cross_summed = total_of(cross_terms)
    cross_moved = swap(cross_summed[middle_part:], "batch", 1)
    gate = cross_summed
    for number in range(1, len(io_parts) - 1):
        io_total = add_low(after(io_hop, gate), io_parts[number])
        io_hop = io_pass(io_total)
        gate = io_total
    cross_pair = add_low(cross_summed[:middle_part], after(cross_moved, io_total))
    self_terms[-1] = after(self_terms[-1], cross_pair)
    both = jnp.concatenate([cross_pair, total_of(self_terms)], axis=1)
    both = pair_finish(both, "batch")
    cross_sums, self_sums = both[:4], both[4:]
    finished += [jnp.sum(part.astype(jnp.float32), axis=0) for part in last_moved]
    io_sum = io_hop.astype(jnp.float32) + io_parts[-1].astype(jnp.float32)
    tile = w_out.shape[0] // batch_size
    w_out_sum = io_sum[:tile]
    w_in_sum = io_sum[tile:].reshape(-1, model_width // batch_size, model_width)
    w_in_sum = w_in_sum.transpose(1, 0, 2).reshape(model_width // batch_size, -1)
    summed_weights = [self_sums[k] for k in range(4)] + [cross_sums[k] for k in range(4)]
    summed_gains = jnp.concatenate([self_gain, two_gains[1:], two_gains[:1], grad_gain_out])
    summed_gains = summed_gains + sum(swap(summed_gains, "blk", j) for j in range(1, group_size))
    summed_gains = after(summed_gains, self_pair)
    summed_gains = summed_gains + swap(summed_gains, "batch", 1)
    summed_gains = summed_gains + sum(swap(summed_gains, "batch", j) for j in range(2, batch_size, 2))
    smooth_all = jnp.concatenate([smooth_parts[at] for at in sorted(smooth_parts)])
    smooth_moved = [swap(after(smooth_all, self_gain), "blk", j)[j] for j in range(1, group_size)]
    own_loss = own_terms[0] - smooth_all[0] - sum(smooth_moved)
    w_in_sum = w_in_sum[None]
    w_out_sum = w_out_sum[None]
    embed_sum = jnp.concatenate(finished, axis=-1)[:, :vocab_part].T
    return (
        own_loss[None],
        grad_tokens[None],
        grad_memory[None],
        summed_gains[0],
        summed_gains[1],
        summed_gains[2],
        summed_gains[3],
        summed_weights[0],
        summed_weights[1],
        summed_weights[2],
        summed_weights[3],
        summed_weights[4],
        summed_weights[5],
        summed_weights[6],
        summed_weights[7],
        w_in_sum,
        w_out_sum,
        embed_sum,
    )


def solution(mesh):
    return jax.shard_map(
        per_device,
        mesh=mesh,
        in_specs=(
            P("batch", "blk", None),
            P("batch", "blk", None),
            P("batch"),
            P("batch", None),
            P(None, "batch", "blk", None),
            P(),
            P(),
            P(),
            P(),
            P(),
            P(),
            P(),
            P(),
            P(),
            P(),
            P(),
            P(),
            P("blk", None, None),
            P("blk", None, None),
            P("blk", None),
        ),
        out_specs=(
            P("batch", "blk"),
            P("batch", "blk", None),
            P("batch", "blk", None),
            P(),
            P(),
            P(),
            P(),
            P("batch", "blk"),
            P("batch", "blk"),
            P("batch", "blk"),
            P("batch", "blk"),
            P("batch", "blk"),
            P("batch", "blk"),
            P("batch", "blk"),
            P("batch", "blk"),
            P("blk", "batch", None),
            P("blk", "batch", None),
            P("blk", "batch"),
        ),
        check_vma=False,
    )
```

```python
import functools

import jax
import jax.numpy as jnp
from jax import lax
from jax.experimental import pallas as pl
from jax.experimental.pallas import tpu as pltpu
from jax.sharding import PartitionSpec as P

HEADS = 8
HD = 64


EPS_NORM = 1e-05
SMOOTH = 0.1
LOG2E = 1.4426950408889634
GELU = 0.7978845608028654
VMEM_LIMIT = 60 << 20
NN = (((1,), (0,)), ((), ()))
NT = (((1,), (1,)), ((), ()))


def work(flops):
    return pl.CostEstimate(flops=flops, bytes_accessed=0, transcendentals=0)


def dot(left, right, dims):
    return lax.dot_general(left, right, dims, preferred_element_type=jnp.float32)


def swap(value, axis, mask):
    size = lax.axis_size(axis)
    return lax.ppermute(value, axis, [(i, i ^ mask) for i in range(size)])


def gather_blocks(own, axis, *gates):
    size = lax.axis_size(axis)
    blocks = {0: own}
    bit = 2
    while bit < size:
        for k in range(0, bit, 2):
            blocks[bit | k] = swap(blocks[k], axis, bit)
        bit *= 2
    for k in range(0, size, 2):
        if k:
            blocks[k] = after(blocks[k], *gates)
        blocks[k | 1] = swap(blocks[k], axis, 1)
    return [blocks[j] for j in range(size)]


def exchange_blocks(own, axis):
    return [own[0]] + [swap(own[j], axis, j) for j in range(1, len(own))]


def core_stage(parts, axis, *gates):
    moved = {j ^ 1: after(swap(parts[j], axis, 1), *gates) for j in sorted(parts) if j % 2}
    return {j: add_low(parts[j], moved[j]) if j else [parts[0], moved[0]] for j in moved}


def far_stage(parts, axis):
    parts = dict(parts)
    terms = list(parts[0])
    size = lax.axis_size(axis)
    bit = 2
    while bit < size:
        odd = list(range(bit, size, 2 * bit))
        moved = swap(jnp.stack([parts[j] for j in odd]) if len(odd) > 1 else parts[bit], axis, bit)
        for k, j in enumerate(odd):
            part = moved[k] if len(odd) > 1 else moved
            if j == bit:
                terms.append(part)
            else:
                parts[j ^ bit] = add_low(parts[j ^ bit], part)
        bit *= 2
    return terms


def stacked_stage(keep, send, axis, *gates):
    moved = after(swap(send, axis, 1), *gates)
    parts = {2 * k: add_low(keep[k], moved[k]) for k in range(1, keep.shape[0])}
    parts[0] = [keep[0], moved[0]]
    return parts


def total_of(terms):
    return functools.reduce(add_low, terms)


def add_low(left, right):
    return (left.astype(jnp.float32) + right.astype(jnp.float32)).astype(left.dtype)


def part_device(me, place, size):
    half = size // 2
    return 2 * (place % half) + ((me % 2) ^ (place // half))


def pair_moved(sums, axis, *gates):
    half = sums.shape[0]
    groups = [[2 * k + bit for k in range(half)] for bit in range(2)]
    return after(lax.all_to_all(sums, axis, 0, 0, axis_index_groups=groups), *gates)


def pair_finish(sums, axis, *gates):
    return jnp.sum(pair_moved(sums, axis, *gates).astype(jnp.float32), axis=0)


def ring_start(sums, axis):
    half = sums.shape[0]
    gray = lambda k: k ^ (k >> 1)
    mine = lax.axis_index(axis) // 2
    shift = 1
    while (1 << shift) < 2 * half:
        mine = mine ^ (lax.axis_index(axis) // 2 >> shift)
        shift += 1
    links = [(2 * gray(k) + bit, 2 * gray((k + 1) % half) + bit) for k in range(half) for bit in range(2)]
    part = lambda step: lax.dynamic_index_in_dim(sums, gray((mine - 1 - step) % half), 0, keepdims=False)
    return part(0), lambda total: lax.ppermute(total, axis, links), [part(k) for k in range(1, half)]


def after(value, *others):
    return lax.optimization_barrier((value,) + others)[0]


def stats_kernel(cols, steps, count, blocks, has_earlier, me_ref, embed_ref, *refs):
    z_refs, refs = refs[:blocks], refs[blocks:]
    earlier_ref, refs = (refs[0], refs[1:]) if has_earlier else (None, refs)
    out_ref, rows_ref, turned_ref, max_ref, sum_ref, mix_ref, turn_ref = refs
    step = pl.program_id(0)
    half = rows_ref.shape[0] // 2
    part = rows_ref.shape[1] // count
    size = half // blocks

    @pl.when(step == 0)
    def _():
        max_ref[...] = jnp.full_like(max_ref, -jnp.inf)
        sum_ref[...] = jnp.zeros_like(sum_ref)
        mix_ref[...] = jnp.zeros_like(mix_ref)
        for p in range(2):
            for k, ref in enumerate(z_refs):
                rows_ref[p * half + k * size : p * half + (k + 1) * size, :] = ref[p]
        turn_ref[...] = rows_ref[...].T
        for place in range(count):
            start = pl.multiple_of(part_device(me_ref[0], place, count) * part, part)
            turned_ref[place * part : (place + 1) * part, :] = turn_ref[pl.ds(start, part), :]

    embed = embed_ref[...]
    for col in range(half // cols):
        places = [slice(p * half + col * cols, p * half + (col + 1) * cols) for p in range(2)]
        logits = [dot(embed, rows_ref[place, :], NT).reshape(-1, 8, cols) for place in places]
        apart = logits[0] - logits[1]
        for place, logit in zip(places, logits):
            old = max_ref[:, place]
            new = jnp.maximum(old, jnp.max(logit, axis=0))
            max_ref[:, place] = new
            scale = jnp.exp2((old - new) * LOG2E)
            weights = jnp.exp2((logit - new[None]) * LOG2E)
            sum_ref[:, place] = sum_ref[:, place] * scale + jnp.sum(weights, axis=0)
            mix_ref[:, place] = mix_ref[:, place] * scale + jnp.sum(weights * apart, axis=0)

    @pl.when(step == steps - 1)
    def _():
        top = jnp.max(max_ref[...], axis=0, keepdims=True)
        scale = jnp.exp2((max_ref[...] - top) * LOG2E)
        first = 0
        if has_earlier:
            first = earlier_ref.shape[0]
            out_ref[:first, :] = earlier_ref[...]
        out_ref[first : first + 1, :] = top
        out_ref[first + 1 : first + 2, :] = jnp.sum(sum_ref[...] * scale, axis=0, keepdims=True)
        out_ref[first + 2 : first + 3, :] = jnp.sum(mix_ref[...] * scale, axis=0, keepdims=True)


def row_tile(rows, limit):
    return max(size for size in range(16, limit + 1, 16) if rows % size == 0)


def vocab_stats(me, embed, blocks, count, earlier):
    vocab, width = embed.shape
    rows = sum(block.shape[0] * block.shape[1] for block in blocks)
    tile = row_tile(vocab, 800)
    cols = min(256, rows // 2)
    steps = vocab // tile
    operands = [me, embed, *blocks] + ([] if earlier is None else [earlier])
    shapes = [wide(3 if earlier is None else 3 + earlier.shape[0], rows), low(rows, width), low(width, rows)]
    return pl.pallas_call(
        functools.partial(stats_kernel, cols, steps, count, len(blocks), earlier is not None),
        grid=(steps,),
        in_specs=[
            pl.BlockSpec(memory_space=pltpu.SMEM),
            pl.BlockSpec((tile, width), lambda i: (i, 0)),
        ] + [whole(leaf) for leaf in operands[2:]],
        out_specs=[whole(leaf) for leaf in shapes],
        out_shape=shapes,
        scratch_shapes=[pltpu.VMEM((8, rows), jnp.float32)] * 3
        + [pltpu.VMEM((width, rows), jnp.bfloat16)],
        compiler_params=pltpu.CompilerParams(vmem_limit_bytes=VMEM_LIMIT),
        cost_estimate=work(5 * vocab * rows * width // 2),
    )(*operands)


def rows_kernel(groups, vocab_total, me_ref, length_ref, target_ref, *refs):
    stat_refs, (value_ref, label_ref, loss_ref) = refs[:-3], refs[-3:]
    devices = len(stat_refs)
    per_group = devices // groups
    rows = stat_refs[0].shape[1] // (2 * per_group)

    def stat(device, block, p, kind):
        block = block ^ device
        row = 3 * (block // per_group) + kind
        lane = (p * per_group + block % per_group) * rows
        return stat_refs[device][row : row + 1, lane : lane + rows]

    for block in range(devices):
        group, lane = block // per_group, (block % per_group) * rows
        place = slice(lane, lane + rows)
        start = pl.multiple_of((me_ref[0] ^ block) * rows, rows)
        position = start + lax.broadcasted_iota(jnp.int32, (1, rows), 1)
        live = position < length_ref[0]
        label_ref[group, 0:1, place] = jnp.where(live, target_ref[0:1, pl.ds(start, rows)], -1)
        logs, expects = [], []
        for p in range(2):
            tops = [stat(device, block, p, 0) for device in range(devices)]
            top = functools.reduce(jnp.maximum, tops)
            scales = [jnp.exp2((one - top) * LOG2E) for one in tops]
            total = sum(stat(device, block, p, 1) * scales[device] for device in range(devices))
            mixed = sum(stat(device, block, p, 2) * scales[device] for device in range(devices))
            logs.append(top + jnp.log(total))
            expects.append(mixed / total)
        values = [
            jnp.where(live, logs[0] * LOG2E, 1e30),
            jnp.where(live, logs[1] * LOG2E, 1e30),
            2.0 - expects[0],
            2.0 + expects[1],
            jnp.where(live, 1.0 - SMOOTH + SMOOTH / vocab_total, 0.0),
            jnp.where(live, SMOOTH / vocab_total, 0.0),
        ]
        for k, value in enumerate(values):
            value_ref[group, k : k + 1, place] = value
        if block == 0:
            loss_ref[...] = jnp.where(live, logs[0] + logs[1] + expects[0] - expects[1], 0.0)


def loss_back_kernel(cols, left, groups, has_total, has_carry, pieces, last, *refs):
    count = len(groups)
    base_ref, embed_ref = refs[:2]
    z_refs, z_t_refs, refs = refs[2 : 2 + count], refs[2 + count : 2 + 2 * count], refs[2 + 2 * count :]
    (row_ref, label_ref), refs = refs[:2], list(refs[2:])
    total_ref = refs.pop(0) if has_total else None
    carry_ref, loss_carry_ref = (refs.pop(0), refs.pop(0)) if has_carry else (None, None)
    loss_out_ref, grad_ref, sum_ref, loss_ref = refs[-4:]
    embed_refs, out_refs = refs[:pieces], refs[pieces:-4]
    step = pl.program_id(0)
    rows = z_refs[0].shape[0]
    half = rows // 2
    tile = embed_ref.shape[0]

    @pl.when(step == 0)
    def _():
        sum_ref[...] = carry_ref[...].astype(jnp.float32) if has_carry else jnp.zeros_like(sum_ref)
        loss_ref[...] = loss_carry_ref[...] if has_carry else jnp.zeros_like(loss_ref)

    rows_left = left - step * tile
    inside = lax.broadcasted_iota(jnp.int32, embed_ref.shape, 0) < rows_left
    embed = jnp.where(inside, embed_ref[...], jnp.zeros_like(embed_ref[...]))
    embed_t = embed.T
    ids = lax.broadcasted_iota(jnp.int32, (tile // 8, 8, cols), 0) * 8
    ids = ids + lax.broadcasted_iota(jnp.int32, (tile // 8, 8, cols), 1)
    base = base_ref[0] + step * tile
    for k, group in enumerate(groups):
        for col in range(half // cols):
            one = slice(col * cols, (col + 1) * cols)
            two = slice(half + col * cols, half + (col + 1) * cols)
            logit_one = dot(embed, z_refs[k][one, :], NT).reshape(-1, 8, cols)
            logit_two = dot(embed, z_refs[k][two, :], NT).reshape(-1, 8, cols)
            row = [row_ref[group, v : v + 1, one].reshape(1, 1, cols) for v in range(6)]
            prob_one = jnp.exp2(logit_one * LOG2E - row[0])
            prob_two = jnp.exp2(logit_two * LOG2E - row[1])
            apart = logit_one - logit_two
            hits = ids == (label_ref[group, 0:1, one] - base).reshape(1, 1, cols)
            smooth = jnp.where(hits, row[4], row[5])
            grad_one = prob_one * (apart + row[2]) - (prob_two + smooth)
            grad_two = prob_two * (row[3] - apart) - (prob_one + smooth)
            loss_ref[k, :, one] += jnp.sum(smooth * (logit_one + logit_two), axis=0)
            lane = k * rows + col * cols
            grad_ref[:, lane : lane + cols] = grad_one.reshape(tile, cols).astype(jnp.bfloat16)
            grad_ref[:, lane + half : lane + half + cols] = grad_two.reshape(tile, cols).astype(jnp.bfloat16)
    grad_embed = total_ref[...].astype(jnp.float32) if has_total else 0.0
    for k in range(count):
        place = slice(k * rows, (k + 1) * rows)
        grad_embed = grad_embed + dot(z_t_refs[k][...], grad_ref[:, place], NT)
        sum_ref[:, place] += dot(embed_t, grad_ref[:, place], NN)
    grad_embed = grad_embed.astype(jnp.bfloat16)
    part = grad_embed.shape[0] // len(embed_refs)
    for k, ref in enumerate(embed_refs):
        ref[...] = grad_embed[k * part : (k + 1) * part]

    @pl.when(step == pl.num_programs(0) - 1)
    def _():
        if not last:
            out_refs[0][...] = sum_ref[...].astype(jnp.bfloat16)
            loss_out_ref[...] = loss_ref[...]
        else:
            for k in range(last):
                size = half * count // last
                lane = k % (last // count) * size
                terms = loss_ref[k // (last // count), :, lane : lane + size]
                loss_out_ref[k : k + 1, :] = jnp.sum(terms, axis=0, keepdims=True)
            size = half * count // len(out_refs)
            per_group = len(out_refs) // count
            for k, ref in enumerate(out_refs):
                for p in range(2):
                    lane = k // per_group * rows + p * half + k % per_group * size
                    ref[p] = sum_ref[:, lane : lane + size].astype(ref.dtype).T


def loss_back(base, embed, z_rows, z_t, row_values, labels, groups, span, total, carry, pieces, last):
    width = embed.shape[1]
    count = len(groups)
    rows = z_rows[0].shape[0]
    tile = TILE
    start, end = span
    steps, first = (end - start) // tile, start // tile
    cols = min(256, rows // 2)
    operands = [base + start, embed, *z_rows, *z_t, row_values, labels]
    vmem = pl.BlockSpec(memory_space=pltpu.VMEM)
    specs = [
        pl.BlockSpec(memory_space=pltpu.SMEM),
        pl.BlockSpec((tile, width), lambda i: (i + first, 0)),
    ] + [vmem] * (2 * count + 2)
    if total is not None:
        operands.append(total)
        specs.append(pl.BlockSpec((width, tile), lambda i: (0, i + first)))
    if carry is not None:
        operands += list(carry)
        specs += [vmem, vmem]
    piece = width // pieces
    grad_z = [low(2, rows * count // 2 // last, width)] * last if last else [low(width, rows * count)]
    loss = wide(last, rows * count // 2 // last) if last else wide(count, 8, rows // 2)
    return pl.pallas_call(
        functools.partial(
            loss_back_kernel, cols, embed.shape[0] - start, groups, total is not None, carry is not None, pieces, last
        ),
        grid=(steps,),
        in_specs=specs,
        out_specs=[pl.BlockSpec((piece, tile), lambda i: (0, i))] * pieces + [vmem] * (len(grad_z) + 1),
        out_shape=[low(piece, end - start)] * pieces + grad_z + [loss],
        scratch_shapes=[
            pltpu.VMEM((tile, rows * count), jnp.bfloat16),
            pltpu.VMEM((width, rows * count), jnp.float32),
            pltpu.VMEM((count, 8, rows // 2), jnp.float32),
        ],
        compiler_params=pltpu.CompilerParams(vmem_limit_bytes=VMEM_LIMIT),
        cost_estimate=work(9 * (end - start) * rows * count * width),
    )(*operands)


TILE = 1024


SCALE = HD ** (-0.5)


def head_lanes(pair, head):
    lanes = lax.broadcasted_iota(jnp.int32, pair.shape, 1)
    return jnp.where((lanes >= HD) == (head % 2 == 1), pair, jnp.zeros_like(pair))


def block_bias(me, rows, blocks, causal):
    if not causal:
        return [None] * blocks
    keys = lax.broadcasted_iota(jnp.int32, (rows, rows), 0)
    queries = lax.broadcasted_iota(jnp.int32, (rows, rows), 1)
    biases = [jnp.where(keys <= queries, 0.0, -1e30)]
    for block in range(1, blocks):
        biases.append(jnp.where((me ^ block) < me, 0.0, -1e30))
    return biases


def head_weights(keys, query, biases, rows):
    scores = []
    for block, bias in enumerate(biases):
        part = dot(keys[block * rows : (block + 1) * rows], query, NT)
        scores.append(part if bias is None else part + bias)
    return scores


def normed(values, gain):
    center = values - jnp.mean(values, axis=-1, keepdims=True)
    spread = jnp.mean(center * center, axis=-1, keepdims=True)
    return center * lax.rsqrt(spread + EPS_NORM) * gain


def normed_back(values, gain, upstream):
    center = values - jnp.mean(values, axis=-1, keepdims=True)
    spread = jnp.mean(center * center, axis=-1, keepdims=True)
    scale = lax.rsqrt(spread + EPS_NORM)
    unit = center * scale
    grad_gain = jnp.sum(upstream * unit, axis=0, keepdims=True)
    up = upstream * gain
    mean_up = jnp.mean(up, axis=-1, keepdims=True)
    mean_mix = jnp.mean(up * unit, axis=-1, keepdims=True)
    return scale * (up - mean_up - unit * mean_mix), grad_gain


def slot_rows(place_ref, count, passes):
    rows = place_ref.shape[1]
    slots = lax.broadcasted_iota(jnp.int32, (count, rows), 0)
    hits = functools.reduce(jnp.logical_or, [slots == place_ref[p : p + 1, :] for p in passes])
    return jnp.where(hits, 1.0, 0.0).astype(jnp.bfloat16)


def token_rows(place_ref, count, passes):
    rows = place_ref.shape[0]
    slots = lax.broadcasted_iota(jnp.int32, (rows, count), 1)
    hits = functools.reduce(jnp.logical_or, [slots == place_ref[:, p : p + 1] for p in passes])
    return jnp.where(hits, 1.0, 0.0).astype(jnp.bfloat16)


def attend_kernel(blocks, causal, *refs):
    me_ref, refs = refs[0], refs[1:]
    block_refs, refs = refs[:blocks], refs[blocks:]
    if causal:
        (first_gain_ref, gain_ref, wq_ref, wk_ref, wv_ref, wo_ref), refs = refs[:6], refs[6:]
        slot_refs = ()
    else:
        (source_ref, residual_ref, place_ref, gain_ref, wq_ref, wk_ref, wv_ref, wo_ref), refs = (
            refs[:8],
            refs[8:],
        )
        slot_refs, refs = refs[:blocks], refs[blocks:]
    (query_ref, key_ref, value_ref, all_ref, out_ref, log_ref, sum_ref, next_ref,
     value_t_ref, out_t_ref) = refs
    rows = block_refs[0].shape[0]
    for block, ref in enumerate(block_refs):
        part = ref[...]
        if causal:
            part = normed(part.astype(jnp.float32), first_gain_ref[...]).astype(jnp.bfloat16)
        all_ref[block * rows : (block + 1) * rows, :] = part
    source = all_ref[:rows, :] if causal else source_ref[...]
    residual = block_refs[0][...].astype(jnp.float32) if causal else residual_ref[...]
    query_ref[...] = dot(source, wq_ref[...], NN).astype(jnp.bfloat16)
    key_ref[...] = dot(all_ref[...], wk_ref[...], NN).astype(jnp.bfloat16)
    values = dot(all_ref[...], wv_ref[...], NN).astype(jnp.bfloat16)
    value_ref[...] = values
    value_t_ref[...] = values.T
    biases = block_bias(me_ref[0], rows, blocks, causal)
    factor = SCALE * LOG2E
    for head in range(HEADS):
        lanes = slice(head // 2 * 128, head // 2 * 128 + 128)
        query = head_lanes(query_ref[:, lanes], head)
        scores = head_weights(key_ref[:, lanes], query, biases, rows)
        top = functools.reduce(
            jnp.maximum, [jnp.max(part.reshape(-1, 8, rows), axis=0) for part in scores]
        )
        top = jnp.max(top, axis=0, keepdims=True) * factor
        weights = [jnp.exp2(part * factor - top) for part in scores]
        total = sum(jnp.sum(part.reshape(-1, 8, rows), axis=0) for part in weights)
        total = jnp.sum(total, axis=0, keepdims=True)
        log_ref[head : head + 1, :] = top + jnp.log2(total)
        weights = jnp.concatenate([part.astype(jnp.bfloat16) for part in weights], axis=0)
        place = slice(head * HD, (head + 1) * HD)
        out_t_ref[place, :] = dot(value_t_ref[place, :], weights, NN) / total
    out = out_t_ref[...].astype(jnp.bfloat16).T
    out_ref[...] = out
    states = residual + dot(out, wo_ref[...], NN)
    sum_ref[...] = states
    following = normed(states, gain_ref[...]).astype(jnp.bfloat16)
    next_ref[...] = following
    if slot_refs:
        count = slot_refs[0].shape[0]
        sends = dot(slot_rows(place_ref, blocks * count, (0, 1)), following, NN).astype(jnp.bfloat16)
        for block, ref in enumerate(slot_refs):
            ref[...] = sends[block * count : (block + 1) * count]


def low(*shape):
    return jax.ShapeDtypeStruct(shape, jnp.bfloat16)


def wide(*shape):
    return jax.ShapeDtypeStruct(shape, jnp.float32)


def attend(me, blocks, weights, gains, slots, source=None, residual=None, place=None):
    rows, width = blocks[0].shape
    count = rows * len(blocks)
    causal = source is None
    operands = [me, *blocks]
    if not causal:
        operands += [source, residual, place]
    operands += [gain[None] for gain in gains] + list(weights)
    shapes = [low(slots, width)] * (0 if causal else len(blocks)) + [
        low(rows, width), low(count, width), low(count, width), low(count, width),
        low(rows, width), wide(HEADS, rows), wide(rows, width), low(rows, width),
    ]
    return pl.pallas_call(
        functools.partial(attend_kernel, len(blocks), causal),
        grid=(1,),
        in_specs=[pl.BlockSpec(memory_space=pltpu.SMEM)] + [whole(leaf) for leaf in operands[1:]],
        out_specs=[whole(leaf) for leaf in shapes],
        out_shape=shapes,
        scratch_shapes=[pltpu.VMEM((width, count), jnp.bfloat16), pltpu.VMEM((width, rows), jnp.float32)],
        compiler_params=pltpu.CompilerParams(vmem_limit_bytes=VMEM_LIMIT),
        cost_estimate=work(9 * 10**9),
    )(*operands)


def attend_back_core(causal, me_ref, branch, wo_ref, query_ref, key_ref, value_ref, log_ref,
                     grad_query_ref, grad_key_ref, grad_value_ref, key_t_ref, up_ref, query_t_ref):
    rows = query_ref.shape[0]
    blocks = key_ref.shape[0] // rows
    up_ref[...] = dot(branch, wo_ref[...], NT).astype(jnp.bfloat16)
    key_t_ref[...] = key_ref[...].T
    biases = block_bias(me_ref[0], rows, blocks, causal)
    factor = SCALE * LOG2E
    for pair in range(HEADS // 2):
        lanes = slice(pair * 128, pair * 128 + 128)
        grad_keys, grad_values = 0.0, 0.0
        for head in (2 * pair, 2 * pair + 1):
            query = head_lanes(query_ref[:, lanes], head)
            upstream = head_lanes(up_ref[:, lanes], head)
            log_total = log_ref[head : head + 1, :]
            scores = head_weights(key_ref[:, lanes], query, biases, rows)
            probs = jnp.concatenate([jnp.exp2(part * factor - log_total) for part in scores], axis=0)
            grad_probs = dot(value_ref[:, lanes], upstream, NT)
            inner = jnp.sum((probs * grad_probs).reshape(-1, 8, rows), axis=0)
            inner = jnp.sum(inner, axis=0, keepdims=True)
            grad_scores = (probs * (grad_probs - inner)).astype(jnp.bfloat16)
            grad_values = grad_values + dot(probs.astype(jnp.bfloat16), upstream, NN)
            grad_keys = grad_keys + dot(grad_scores, query, NN)
            place = slice(head * HD, (head + 1) * HD)
            query_t_ref[place, :] = dot(key_t_ref[place, :], grad_scores, NN) * SCALE
        grad_value_ref[:, lanes] = grad_values.astype(jnp.bfloat16)
        grad_key_ref[:, lanes] = (grad_keys * SCALE).astype(jnp.bfloat16)
    grad_query_ref[...] = query_t_ref[...].astype(jnp.bfloat16).T


def cross_back_kernel(blocks, *refs):
    me_ref, back_refs, refs = refs[0], refs[1 : 1 + blocks], refs[1 + blocks :]
    (place_ref, after_ref, gain_ffn_ref, grad_sum_ref, middle_ref, gain_cross_ref, wo_ref, wq_ref,
     query_ref, key_ref, value_ref, log_ref), refs = refs[:12], refs[12:]
    (branch_ref, middle_grad_ref, gains_ref, grad_query_ref, grad_key_ref, grad_value_ref,
     key_t_ref, up_ref, query_t_ref) = refs
    back = jnp.concatenate([ref[...] for ref in back_refs], axis=0)
    grad_normed = dot(token_rows(place_ref, back.shape[0], (0, 1)), back, NN)
    grad_after, gains_ref[0:1, :] = normed_back(after_ref[...], gain_ffn_ref[...], grad_normed)
    grad_after = grad_after + grad_sum_ref[...]
    branch = grad_after.astype(jnp.bfloat16)
    branch_ref[...] = branch
    attend_back_core(False, me_ref, branch, wo_ref, query_ref, key_ref, value_ref, log_ref,
                     grad_query_ref, grad_key_ref, grad_value_ref, key_t_ref, up_ref, query_t_ref)
    grad_normed = dot(grad_query_ref[...], wq_ref[...], NT)
    grad_middle, gains_ref[1:2, :] = normed_back(middle_ref[...], gain_cross_ref[...], grad_normed)
    middle_grad_ref[...] = grad_middle + grad_after


def self_back_kernel(me_ref, middle_grad_ref, wo_ref, wq_ref, wk_ref, wv_ref,
                     query_ref, key_ref, value_ref, log_ref, memkey_ref, memval_ref, ck_ref, cv_ref,
                     keep_ref, send_ref, own_ref, grad_query_ref, grad_key_ref, grad_value_ref,
                     key_t_ref, up_ref, query_t_ref):
    rows = query_ref.shape[0]
    branch = middle_grad_ref[...].astype(jnp.bfloat16)
    attend_back_core(True, me_ref, branch, wo_ref, query_ref, key_ref, value_ref, log_ref,
                     grad_query_ref, grad_key_ref, grad_value_ref, key_t_ref, up_ref, query_t_ref)
    for block in range(key_ref.shape[0] // rows):
        place = slice(block * rows, (block + 1) * rows)
        part = dot(grad_key_ref[place, :], wk_ref[...], NT) + dot(grad_value_ref[place, :], wv_ref[...], NT)
        target = send_ref if block % 2 else keep_ref
        target[block // 2, 0] = part.astype(jnp.bfloat16)
        part = dot(memkey_ref[place, :], ck_ref[...], NT) + dot(memval_ref[place, :], cv_ref[...], NT)
        target[block // 2, 1] = part.astype(jnp.bfloat16)
    own_ref[...] = dot(grad_query_ref[...], wq_ref[...], NT)


def back_call(kernel, operands, shapes, rows, count, width):
    return pl.pallas_call(
        kernel,
        grid=(1,),
        in_specs=[pl.BlockSpec(memory_space=pltpu.SMEM)] + [whole(leaf) for leaf in operands[1:]],
        out_specs=[whole(leaf) for leaf in shapes],
        out_shape=shapes,
        scratch_shapes=[
            pltpu.VMEM((width, count), jnp.bfloat16),
            pltpu.VMEM((rows, width), jnp.bfloat16),
            pltpu.VMEM((width, rows), jnp.float32),
        ],
        compiler_params=pltpu.CompilerParams(vmem_limit_bytes=VMEM_LIMIT),
        cost_estimate=work(100 * rows * count * width),
    )(*operands)


def whole(leaf):
    rank = len(leaf.shape)
    return pl.BlockSpec(leaf.shape, lambda *_: (0,) * rank)


def plain_call(kernel, operands, shapes, flops, scratch=(), scalars=1):
    size = sum(leaf.size * leaf.dtype.itemsize for leaf in list(operands) + list(shapes))
    return pl.pallas_call(
        kernel,
        grid=(1,),
        in_specs=[pl.BlockSpec(memory_space=pltpu.SMEM)] * scalars
        + [whole(leaf) for leaf in operands[scalars:]],
        out_specs=[whole(leaf) for leaf in shapes],
        out_shape=shapes,
        scratch_shapes=list(scratch),
        compiler_params=pltpu.CompilerParams(vmem_limit_bytes=48 << 20),
        cost_estimate=work(flops),
    )(*operands)


def weights_kernel(plan, targets, lefts, *refs):
    group_me_ref, batch_me_ref, refs = refs[0], refs[1], refs[2:]
    operand_refs, target_refs, product_ref = refs[:-5], refs[-5:-1], refs[-1]
    groups, batches = targets
    width = product_ref.shape[0]
    row_part, col_part = width // batches, width // groups
    turned = {left: operand_refs[left][...].T for left in lefts}
    for number, pairs in enumerate(plan):
        for pair, (left, right) in enumerate(pairs):
            value = operand_refs[right][...].astype(jnp.bfloat16)
            product_ref[...] = dot(turned[left][:, : value.shape[0]], value, NN)
            for block in range(groups):
                target = target_refs[2 * number + block % 2]
                at = group_me_ref[0] ^ block
                for spot in range(batches):
                    row = pl.multiple_of(part_device(batch_me_ref[0], spot, batches) * row_part, row_part)
                    col = pl.multiple_of(at * col_part, 128)
                    part = product_ref[pl.ds(row, row_part), pl.ds(col, col_part)]
                    target[block // 2, spot, pair] = part.astype(jnp.bfloat16)


def plain_parts(group_me, batch_me, operands, plan, groups, batches):
    width = operands[0].shape[1]
    columns = group_me ^ jnp.arange(groups, dtype=jnp.int32)
    spots = jnp.stack([part_device(batch_me, spot, batches) for spot in range(batches)])
    outputs = []
    for pairs in plan:
        stacked = []
        for left, right in pairs:
            value = operands[right].astype(jnp.bfloat16)
            stacked.append(dot(operands[left][: value.shape[0]].T, value, NN).astype(jnp.bfloat16))
        parts = jnp.stack(stacked).reshape(len(pairs), batches, width // batches, groups, width // groups)
        parts = parts.transpose(3, 1, 0, 2, 4)[columns][:, spots]
        outputs += [parts[0::2], parts[1::2]]
    return outputs


def weight_parts(group_me, batch_me, operands, plan, groups, batches):
    width = operands[0].shape[1]
    if width // groups % 128:
        return plain_parts(group_me[0], batch_me[0], operands, plan, groups, batches)
    lefts = sorted({left for pairs in plan for left, _ in pairs})
    shapes = [
        low(groups // 2, batches, len(pairs), width // batches, width // groups)
        for pairs in plan for _ in range(2)
    ]
    return plain_call(
        functools.partial(weights_kernel, plan, (groups, batches), lefts),
        [group_me, batch_me, *operands], shapes, 8 * 10**9, [pltpu.VMEM((width, width), jnp.float32)], 2,
    )


def expert_kernel(parts, steps, w_in_ref, w_out_ref, *refs):
    row_refs, out_refs, (rows_ref, total_ref) = refs[:parts], refs[parts : 2 * parts], refs[2 * parts :]
    step = pl.program_id(0)
    size = row_refs[0].shape[0]

    @pl.when(step == 0)
    def _():
        for k, ref in enumerate(row_refs):
            rows_ref[k * size : (k + 1) * size, :] = ref[...]
        total_ref[...] = jnp.zeros_like(total_ref)

    up = dot(rows_ref[...], w_in_ref[...], NN)
    curve = jnp.tanh(up * (GELU + GELU * 0.044715 * (up * up)))
    activity = (up * (0.5 + 0.5 * curve)).astype(jnp.bfloat16)
    total_ref[...] += dot(activity, w_out_ref[...], NN)

    @pl.when(step == steps - 1)
    def _():
        for k, ref in enumerate(out_refs):
            ref[...] = total_ref[k * size : (k + 1) * size, :].astype(jnp.bfloat16)


def expert_rows(parts, w_in, w_out):
    size, width = parts[0].shape
    hidden = w_in.shape[1]
    tile = min(512, hidden)
    rows = size * len(parts)
    return pl.pallas_call(
        functools.partial(expert_kernel, len(parts), hidden // tile),
        grid=(hidden // tile,),
        in_specs=[
            pl.BlockSpec((width, tile), lambda i: (0, i)),
            pl.BlockSpec((tile, width), lambda i: (i, 0)),
        ] + [whole(leaf) for leaf in parts],
        out_specs=[whole(leaf) for leaf in parts],
        out_shape=[low(size, width)] * len(parts),
        scratch_shapes=[pltpu.VMEM((rows, width), jnp.bfloat16), pltpu.VMEM((rows, width), jnp.float32)],
        compiler_params=pltpu.CompilerParams(vmem_limit_bytes=40 << 20),
        cost_estimate=work(4 * rows * width * hidden),
    )(w_in, w_out, *parts)


def expert_back_kernel(parts, steps, batch_me_ref, w_in_ref, w_in_t_ref, w_out_ref, *refs):
    row_refs, grad_refs, refs = refs[:parts], refs[parts : 2 * parts], refs[2 * parts :]
    out_refs, refs = refs[:parts], refs[parts:]
    keep_ref, send_ref, rows_ref, turned_ref, whole_ref, grads_ref, total_ref = refs
    step = pl.program_id(0)
    size = row_refs[0].shape[0]
    half = steps // 2
    width = turned_ref.shape[0]
    part = width // steps
    tile = w_out_ref.shape[0]

    @pl.when(step == 0)
    def _():
        for k in range(parts):
            rows_ref[k * size : (k + 1) * size, :] = row_refs[k][...]
            grads_ref[k * size : (k + 1) * size, :] = grad_refs[k][...]
        whole_ref[...] = rows_ref[...].T
        for place in range(steps):
            start = pl.multiple_of(part_device(batch_me_ref[0], place, steps) * part, part)
            turned_ref[place * part : (place + 1) * part, :] = whole_ref[pl.ds(start, part), :]
        total_ref[...] = jnp.zeros_like(total_ref)

    up = dot(w_in_t_ref[...], rows_ref[...], NT)
    square = up * up
    curve = jnp.tanh(up * (GELU + GELU * 0.044715 * square))
    share = 0.5 + 0.5 * curve
    active = up * share
    activity = active.astype(jnp.bfloat16)
    slope = share + active * (1.0 - curve) * (GELU + GELU * 3.0 * 0.044715 * square)
    grad_up = (dot(w_out_ref[...], grads_ref[...], NT) * slope).astype(jnp.bfloat16)
    grad_out = dot(activity, grads_ref[...], NN).astype(jnp.bfloat16)

    @pl.when(step < half)
    def _():
        keep_ref[step, :tile, :] = grad_out

    @pl.when(step >= half)
    def _():
        send_ref[step - half, :tile, :] = grad_out

    grad_in = dot(turned_ref[...], grad_up, NT).astype(jnp.bfloat16)
    column = part_device(batch_me_ref[0], step, steps) * tile
    row = pl.multiple_of(tile + column // width * part, part)
    lane = pl.multiple_of(column % width, tile)
    for place in range(steps):
        target = keep_ref if place < half else send_ref
        target[place % half, pl.ds(row, part), pl.ds(lane, tile)] = grad_in[place * part : (place + 1) * part]
    total_ref[...] += dot(w_in_ref[...], grad_up, NN)

    @pl.when(step == steps - 1)
    def _():
        for k, ref in enumerate(out_refs):
            ref[...] = total_ref[:, k * size : (k + 1) * size].astype(jnp.bfloat16).T


def expert_back(batch_me, rows, grads, w_in, w_in_t, w_out, batches):
    size, width = rows[0].shape
    count = len(rows)
    hidden = w_in.shape[1]
    tile = hidden // batches
    half = batches // 2
    total = size * count

    def unit(i, me_ref):
        return part_device(me_ref[0], i, batches)

    both = low(half, 2 * tile, width)
    return pl.pallas_call(
        functools.partial(expert_back_kernel, count, batches),
        grid_spec=pltpu.PrefetchScalarGridSpec(
            num_scalar_prefetch=1,
            grid=(batches,),
            in_specs=[
                pl.BlockSpec((width, tile), lambda i, me_ref: (0, unit(i, me_ref))),
                pl.BlockSpec((tile, width), lambda i, me_ref: (unit(i, me_ref), 0)),
                pl.BlockSpec((tile, width), lambda i, me_ref: (unit(i, me_ref), 0)),
            ] + [whole(leaf) for leaf in list(rows) + list(grads)],
            out_specs=[whole(leaf) for leaf in [*rows, both, both]],
            scratch_shapes=[
                pltpu.VMEM((total, width), jnp.bfloat16),
                pltpu.VMEM((width, total), jnp.bfloat16),
                pltpu.VMEM((width, total), jnp.bfloat16),
                pltpu.VMEM((total, width), jnp.bfloat16),
                pltpu.VMEM((width, total), jnp.float32),
            ],
        ),
        out_shape=[low(size, width)] * count + [both, both],
        compiler_params=pltpu.CompilerParams(vmem_limit_bytes=VMEM_LIMIT),
        cost_estimate=work(24 * total * width * hidden),
    )(batch_me, w_in, w_in_t, w_out, *rows, *grads)


def combine_kernel(parts, *refs):
    back_refs, (place_ref, after_ref, gain_ref, out_ref, z_ref) = refs[:parts], refs[parts:]
    back = jnp.concatenate([ref[...] for ref in back_refs], axis=0)
    for p in range(2):
        states = after_ref[...] + dot(token_rows(place_ref, back.shape[0], (p,)), back, NN)
        out_ref[p] = states
        z_ref[p] = normed(states, gain_ref[...]).astype(jnp.bfloat16)


def out_back_kernel(sources, *refs):
    grad_refs, (out_ref, gain_ref, place_ref), refs = refs[:sources], refs[sources : sources + 3], refs[sources + 3 :]
    slot_refs, (sum_ref, gain_grad_ref) = refs[:-2], refs[-2:]
    count = len(slot_refs) * slot_refs[0].shape[0]
    grads, gain_grad, slots = 0.0, 0.0, 0.0
    for p in range(2):
        upstream = sum(ref[p].astype(jnp.float32) for ref in grad_refs)
        grad, more = normed_back(out_ref[p], gain_ref[...], upstream)
        grads, gain_grad = grads + grad, gain_grad + more
        slots = slots + dot(slot_rows(place_ref, count, (p,)), grad.astype(jnp.bfloat16), NN)
    sum_ref[...] = grads
    gain_grad_ref[...] = gain_grad
    size = slot_refs[0].shape[0]
    for k, ref in enumerate(slot_refs):
        ref[...] = slots[k * size : (k + 1) * size].astype(jnp.bfloat16)


def token_back_kernel(sources, *refs):
    grad_refs, (own_ref, states_ref, gain_ref, middle_ref, out_ref, memory_ref, gain_grad_ref) = (
        refs[:sources],
        refs[sources:],
    )
    upstream = own_ref[...] + sum(ref[0].astype(jnp.float32) for ref in grad_refs)
    memory_ref[...] = sum(ref[1].astype(jnp.float32) for ref in grad_refs)
    grad, gain_grad_ref[...] = normed_back(states_ref[...].astype(jnp.float32), gain_ref[...], upstream)
    out_ref[...] = grad + middle_ref[...]


def per_device(
    tokens,
    memory,
    lengths,
    targets,
    expert_ids,
    gain_self,
    gain_cross,
    gain_ffn,
    gain_out,
    wq,
    wk,
    wv,
    wo,
    cq,
    ck,
    cv,
    co,
    w_in,
    w_out,
    embed,
):
    group_index = lax.axis_index("blk")
    group_size = lax.axis_size("blk")
    batch_size = lax.axis_size("batch")
    own_rows, model_width = tokens.shape[1:]
    me = group_index.astype(jnp.int32).reshape(1)
    batch_me = lax.axis_index("batch").astype(jnp.int32).reshape(1)
    capacity = 3 * own_rows // (2 * group_size)
    w_in, w_out = w_in[0], w_out[0]

    vocab_part = embed.shape[0]
    padded = -(-vocab_part // TILE) * TILE
    token_blocks = gather_blocks(tokens[0], "blk")
    memory_own = memory[0]
    picks = expert_ids[:, 0, :, 0]
    onehot = (picks[:, :, None] == jnp.arange(group_size, dtype=jnp.int32)).astype(jnp.int32)
    slot = jnp.sum(onehot * (jnp.cumsum(onehot, axis=1) - onehot), axis=-1)
    place = ((picks ^ group_index) * 2 + jnp.arange(2, dtype=jnp.int32)[:, None]) * capacity + slot
    place_t = place.T

    queries, all_keys, all_values, h_all, attn_out, self_log, middle, h_two = attend(
        me, token_blocks, (wq, wk, wv, wo), (gain_self, gain_cross), 0
    )
    memory_blocks = gather_blocks(memory_own, "blk", h_two)
    *sends, cross_q, mem_keys, mem_values, memory_all, cross_out, cross_log, after_cross, _ = attend(
        me, memory_blocks, (cq, ck, cv, co), (gain_ffn,), 2 * capacity, h_two, middle, place
    )
    arrived = exchange_blocks(sends, "blk")
    results = expert_rows(arrived[:2], w_in, w_out)
    if group_size > 2:
        results = list(results) + list(expert_rows(arrived[2:], w_in, w_out))
    returned = exchange_blocks(results, "blk")
    outputs, z_pair = plain_call(
        functools.partial(combine_kernel, group_size),
        [*returned, place_t, after_cross, gain_out[None]],
        [wide(2, own_rows, model_width), low(2, own_rows, model_width)],
        8 * group_size * capacity * own_rows * model_width, (), 0,
    )

    near_z = [z_pair, swap(z_pair, "blk", 1)]
    far_z = {bit: swap(z_pair, "blk", bit) for bit in (1 << k for k in range(1, group_size.bit_length() - 1))}
    count = max(2, group_size * own_rows // 1024)
    per_group = group_size // count
    groups = [list(range(k * per_group, (k + 1) * per_group)) for k in range(count)]
    stats, group_z, group_z_t = None, [], []
    z_blocks = dict(enumerate(near_z))
    if per_group > 2:
        z_blocks = dict(enumerate(gather_blocks(z_pair, "blk")))
    for number, group in enumerate(groups):
        if number and 2 not in z_blocks:
            z_blocks[2] = after(far_z[2], stats)
            z_blocks[3] = swap(z_blocks[2], "blk", 1)
        stats, rows, rows_t = vocab_stats(
            batch_me, embed, [z_blocks[j] for j in group], batch_size, stats
        )
        group_z.append(rows)
        group_z_t.append(rows_t)
    all_stats = [stats] + [swap(stats, "blk", j) for j in range(1, group_size)]
    row_values, labels, own_terms = plain_call(
        functools.partial(rows_kernel, count, vocab_part * group_size),
        [me, lengths, targets, *all_stats],
        [
            wide(count, 6, per_group * own_rows),
            jax.ShapeDtypeStruct((count, 1, per_group * own_rows), jnp.int32),
            wide(1, own_rows),
        ],
        0, (), 2,
    )
    vocab_base = me * vocab_part
    total = None
    sums, smooth_parts, chunks, chunk_sums, finished = {}, {}, [], [], []
    joined = max(1, min(count, 1024 // (per_group * own_rows)))
    for at in range(count - joined, -1, -joined):
        mine = range(at, at + joined)
        operands = (
            vocab_base, embed, group_z[at : at + joined], group_z_t[at : at + joined],
            row_values, labels, tuple(mine),
        )
        if at > 0:
            total, *grad_z, smooth = loss_back(
                *operands, (0, padded), total, None, 1, joined * per_group
            )
        else:
            carry = None
            tiles = padded // TILE
            cuts = [0, tiles // 4, 5 * tiles // 8, tiles] if tiles >= 8 else [0, tiles]
            for number in range(len(cuts) - 1):
                start, end = cuts[number] * TILE, cuts[number + 1] * TILE
                done = end == padded
                if done and number > 1:
                    chunk_sums.append(add_low(*chunks[0]))
                    carry = (after(carry[0], chunk_sums[0]), carry[1])
                keep, send, *grad_z, smooth = loss_back(
                    *operands, (start, end), total, carry, 2, joined * per_group if done else 0
                )
                carry = (grad_z[0], smooth)
                shape = (batch_size // 2, model_width // batch_size, end - start)
                send = send.reshape(shape)
                chunks.append((keep.reshape(shape), send if number > 1 else swap(send, "batch", 1)))
        held = [j for group in mine for j in groups[group]]
        if len(chunk_sums) == 1:
            first_moved = pair_moved(chunk_sums[0], "batch", grad_z[0])
            finished.append(jnp.sum(first_moved.astype(jnp.float32), axis=0))
            sums.update(core_stage(dict(zip(held, grad_z)), "blk", first_moved))
            near = [sums[j] for j in sums if j]
            chunk_sums.append(add_low(chunks[1][0], after(chunks[1][1], *near)))
            for number in range(2, len(chunks)):
                keep, send = chunks[number]
                chunks[number] = (keep, swap(after(send, *near), "batch", 1))
        else:
            sums.update(core_stage(dict(zip(held, grad_z)), "blk"))
        smooth_parts[at] = smooth
    for keep, moved in chunks[len(chunk_sums) : 2]:
        chunk_sums.append(add_low(keep, moved))
    grad_z_terms = far_stage(sums, "blk")
    *send_grads, grad_sum, grad_gain_out = plain_call(
        functools.partial(out_back_kernel, len(grad_z_terms)),
        [*grad_z_terms, outputs, gain_out[None], place],
        [low(2 * capacity, model_width)] * group_size + [wide(own_rows, model_width), wide(1, model_width)],
        8 * group_size * capacity * own_rows * model_width, (), 0,
    )
    arrived_grads = exchange_blocks(send_grads, "blk")
    *grad_rows, io_keep, io_send = expert_back(
        batch_me, arrived, arrived_grads, w_in, w_in.T, w_out, batch_size
    )
    back_rows = exchange_blocks(grad_rows, "blk")
    for keep, moved in chunks[len(chunk_sums) :]:
        chunk_sums.append(add_low(keep, after(moved, back_rows[1])))
    finished += [pair_finish(part, "batch", back_rows[1]) for part in chunk_sums[len(finished) : 2]]
    back_rows[0] = after(back_rows[0], *chunk_sums[2:], *finished[1:2])
    branch_two, grad_middle, two_gains, cross_q_grad, memkey_part, memval_part = back_call(
        functools.partial(cross_back_kernel, group_size),
        [
            me, *back_rows, place_t, after_cross, gain_ffn[None], grad_sum, middle, gain_cross[None],
            co, cq, cross_q, mem_keys, mem_values, cross_log,
        ],
        [low(own_rows, model_width), wide(own_rows, model_width), wide(2, model_width)]
        + [low(own_rows, model_width)] + [low(group_size * own_rows, model_width)] * 2,
        own_rows, group_size * own_rows, model_width,
    )
    io_moved = swap(io_send, "batch", 1)
    half = (group_size // 2, 2, own_rows, model_width)
    state_keep, state_send, own_part, query_grad, key_part, value_part = back_call(
        self_back_kernel,
        [
            me, grad_middle, wo, wq, wk, wv, queries, all_keys, all_values, self_log,
            memkey_part, memval_part, ck, cv,
        ],
        [low(*half)] * 2 + [wide(own_rows, model_width), low(own_rows, model_width)]
        + [low(group_size * own_rows, model_width)] * 2,
        own_rows, group_size * own_rows, model_width,
    )
    later = lambda parts: [parts[j] for j in parts if j]
    state_sums = stacked_stage(state_keep, state_send, "blk")
    state_terms = far_stage(state_sums, "blk")
    last_moved = [pair_moved(part, "batch", own_part) for part in chunk_sums[len(finished) :]]
    operands = [
        after(h_two, own_part), memory_all, cross_out, h_all, attn_out,
        cross_q_grad, memkey_part, memval_part, branch_two, query_grad, key_part, value_part, grad_middle,
    ]
    plan = (((0, 5), (1, 6), (1, 7), (2, 8)), ((3, 9), (3, 10), (3, 11), (4, 12)))
    cross_keep, cross_send, self_keep, self_send = weight_parts(
        me, batch_me, operands, plan, group_size, batch_size
    )
    middle_part = batch_size // 2
    io_sums = add_low(io_keep, after(io_moved, cross_keep, *last_moved))
    io_total, io_pass, io_parts = ring_start(io_sums, "batch")
    io_hop = io_pass(io_total)
    cross_parts = stacked_stage(cross_keep, cross_send, "blk", io_total)
    cross_terms = far_stage(cross_parts, "blk")
    self_sums = add_low(self_keep, after(swap(self_send, "blk", 1), *later(cross_parts)))
    self_moved = swap(self_sums[:, middle_part:], "batch", 1)
    io_total = add_low(after(io_hop, self_sums), io_parts[0])
    io_hop = io_pass(io_total)
    self_pair = add_low(self_sums[:, :middle_part], after(self_moved, io_total))
    self_terms = far_stage(
        {2 * k: self_pair[k] if k else [self_pair[0]] for k in range(group_size // 2)}, "blk"
    )
    cross_terms[-1] = after(cross_terms[-1], self_pair)
    cross_summed = total_of(cross_terms)
    cross_moved = swap(cross_summed[middle_part:], "batch", 1)
    for number in range(1, len(io_parts) - 1):
        io_total = add_low(after(io_hop, cross_summed), io_parts[number])
        io_hop = io_pass(io_total)
    state_terms[-1] = after(state_terms[-1], cross_summed, io_total)
    grad_tokens, grad_memory, self_gain = plain_call(
        functools.partial(token_back_kernel, len(state_terms)),
        [*state_terms, own_part, tokens[0], gain_self[None], grad_middle],
        [wide(own_rows, model_width), wide(own_rows, model_width), wide(1, model_width)],
        0, (), 0,
    )
    cross_pair = add_low(cross_summed[:middle_part], after(cross_moved, io_total))
    self_terms[-1] = after(self_terms[-1], cross_pair)
    both = jnp.concatenate([cross_pair, total_of(self_terms)], axis=1)
    both = pair_finish(both, "batch")
    cross_sums, self_sums = both[:4], both[4:]
    finished += [jnp.sum(after(part, cross_pair).astype(jnp.float32), axis=0) for part in last_moved]
    io_sum = io_hop.astype(jnp.float32) + io_parts[-1].astype(jnp.float32)
    tile = w_out.shape[0] // batch_size
    w_out_sum = io_sum[:tile]
    w_in_sum = io_sum[tile:].reshape(-1, model_width // batch_size, model_width)
    w_in_sum = w_in_sum.transpose(1, 0, 2).reshape(model_width // batch_size, -1)
    summed_weights = [self_sums[k] for k in range(4)] + [cross_sums[k] for k in range(4)]
    summed_gains = jnp.concatenate([self_gain, two_gains[1:], two_gains[:1], grad_gain_out])
    summed_gains = summed_gains + sum(swap(summed_gains, "blk", j) for j in range(1, group_size))
    summed_gains = after(summed_gains, cross_pair)
    summed_gains = summed_gains + swap(summed_gains, "batch", 1)
    summed_gains = summed_gains + sum(swap(summed_gains, "batch", j) for j in range(2, batch_size, 2))
    smooth_all = jnp.concatenate([smooth_parts[at] for at in sorted(smooth_parts)])
    smooth_moved = [swap(after(smooth_all, cross_pair), "blk", j)[j] for j in range(1, group_size)]
    own_loss = own_terms[0] - smooth_all[0] - sum(smooth_moved)
    w_in_sum = w_in_sum[None]
    w_out_sum = w_out_sum[None]
    embed_sum = jnp.concatenate(finished, axis=-1)[:, :vocab_part].T
    return (
        own_loss[None],
        grad_tokens[None],
        grad_memory[None],
        summed_gains[0],
        summed_gains[1],
        summed_gains[2],
        summed_gains[3],
        summed_weights[0],
        summed_weights[1],
        summed_weights[2],
        summed_weights[3],
        summed_weights[4],
        summed_weights[5],
        summed_weights[6],
        summed_weights[7],
        w_in_sum,
        w_out_sum,
        embed_sum,
    )


def solution(mesh):
    return jax.shard_map(
        per_device,
        mesh=mesh,
        in_specs=(
            P("batch", "blk", None),
            P("batch", "blk", None),
            P("batch"),
            P("batch", None),
            P(None, "batch", "blk", None),
            P(),
            P(),
            P(),
            P(),
            P(),
            P(),
            P(),
            P(),
            P(),
            P(),
            P(),
            P(),
            P("blk", None, None),
            P("blk", None, None),
            P("blk", None),
        ),
        out_specs=(
            P("batch", "blk"),
            P("batch", "blk", None),
            P("batch", "blk", None),
            P(),
            P(),
            P(),
            P(),
            P("batch", "blk"),
            P("batch", "blk"),
            P("batch", "blk"),
            P("batch", "blk"),
            P("batch", "blk"),
            P("batch", "blk"),
            P("batch", "blk"),
            P("batch", "blk"),
            P("blk", "batch", None),
            P("blk", "batch", None),
            P("blk", "batch"),
        ),
        check_vma=False,
    )
```
